32 devices in a mesh: dp: 4 (over y, core), seq: 8 (over z, x).
Axes of the slice: x: 2, y: 2, z: 4, core: 2. Of those that a mesh axis runs over, the one named last changes fastest.
Arguments:
- inputs: bfloat16 [16, 1024, 768], P('dp', 'seq'), may hold values from -6 to 6
- cotangent: bfloat16 [16, 1024, 768], P('dp', 'seq'), may hold values from -6 to 6
- lengths: int32 [16, 4], P('dp'), may hold values from 0 to 1024, as said below
- clusters: int32 [16, 1024, 12], P('dp', 'seq'), may hold values from 0 to 99, as said below
- gain_attn: float32 [768], replicated, may hold values from 0.1 to 1.9
- bias_attn: float32 [768], replicated, may hold values from -0.6 to 0.6
- w_query: bfloat16 [768, 768], replicated, may hold values from -1 to 1
- w_key: bfloat16 [768, 768], replicated, may hold values from -0.3125 to 0.3125
- w_value: bfloat16 [768, 768], replicated, may hold values from -0.21875 to 0.21875
- w_out: bfloat16 [768, 768], replicated, may hold values from -0.875 to 0.875
- gain_ffn: float32 [768], replicated, may hold values from 0.1 to 1.9
- bias_ffn: float32 [768], replicated, may hold values from -1.8 to 1.8
- w_up: bfloat16 [768, 3072], replicated, may hold values from -0.21875 to 0.21875
- w_down: bfloat16 [3072, 768], replicated, may hold values from -0.109375 to 0.109375
Outputs:
- output: float32 [16, 1024, 768], P('dp', 'seq')
- grad_inputs: float32 [16, 1024, 768], P('dp', 'seq')
- grad_gain_attn: float32 [768], P('seq')
- grad_bias_attn: float32 [768], P('seq')
- grad_w_query: float32 [768, 768], P('seq')
- grad_w_key: float32 [768, 768], P('seq')
- grad_w_value: float32 [768, 768], P('seq')
- grad_w_out: float32 [768, 768], P('seq')
- grad_gain_ffn: float32 [768], P('seq')
- grad_bias_ffn: float32 [768], P('seq')
- grad_w_up: float32 [768, 3072], P('seq')
- grad_w_down: float32 [3072, 768], P('seq')
The draws below stay inside these ranges and needn't reach their ends.
Inputs may be any that keep to these rules, and one draw needn't show every extreme that they name: Each row's lengths add up to 1024; a length may be 0. In every aligned block of 4 rows one row is a single document of 1024 tokens. `clusters`: in every row and head each of the 100 cluster numbers is given to at least one token.
All inputs are finite; a program needn't handle non-finite values.
Results may differ from the reference program's by a relative error of at most 0.018.
Values may be sent and summed in bfloat16 or wider, within the bound.
A program may use at most 192 MiB of HBM per device.

```python
import jax
import jax.numpy as jnp
from jax import lax

D = 768
HEADS = 12
HEAD_DIM = 64
FF = 3072
CLUSTERS = 100
DOCS = 4
ROWS = 4
ROW = 1024
NROWS = 16


def draw_lengths(key, part):
    key = jax.random.fold_in(key, 11)
    count_key, cut_key, single_key = jax.random.split(key, 3)
    doc_counts = jax.random.randint(count_key, (NROWS, 1), 1, DOCS + 1)
    single = jax.random.randint(single_key, (NROWS // ROWS, 1), 0, ROWS)
    row_pos = jnp.arange(ROWS, dtype=jnp.int32)[None, :]
    is_single = (row_pos == single).reshape(NROWS, 1)
    doc_counts = jnp.where(is_single, 1, doc_counts)
    cut_points = jnp.sort(jax.random.randint(cut_key, (NROWS, DOCS - 1), 1, ROW), axis=1)
    slot_index = jnp.arange(DOCS - 1, dtype=jnp.int32)[None, :]
    cut_points = jnp.where(slot_index < doc_counts - 1, cut_points, ROW)
    bounds = jnp.concatenate([jnp.zeros((NROWS, 1), jnp.int32), cut_points.astype(jnp.int32), jnp.full((NROWS, 1), ROW, jnp.int32)], axis=1)
    return (bounds[:, 1:] - bounds[:, :-1]).astype(jnp.int32)


def draw_clusters(key, part):
    key = jax.random.fold_in(key, 23)
    fill_key, order_key = jax.random.split(key)
    fill_ids = jax.random.randint(fill_key, (NROWS, HEADS, ROW), 0, CLUSTERS)
    spread = jax.random.randint(order_key, (NROWS, HEADS, ROW), 0, 2 ** 31 // ROW - 1)
    scores = spread * ROW + jnp.arange(ROW, dtype=jnp.int32)
    ordering = jnp.argsort(scores, axis=2)
    ranking = jnp.argsort(ordering, axis=2).astype(jnp.int32)
    cluster_ids = jnp.where(ranking < CLUSTERS, ranking, fill_ids)
    return jnp.transpose(cluster_ids, (0, 2, 1)).astype(jnp.int32)


def levels(rng, shape, shards, least, high):
    factor_of, own = 1.0, jax.random.fold_in(rng, 6)
    for dim, parts in shards:
        draws = jnp.exp(jax.random.uniform(jax.random.fold_in(own, dim), (parts,), jnp.float32, least / len(shards), high / len(shards)))
        factor_of = factor_of * jnp.repeat(draws, shape[dim] // parts).reshape([-1 if axis == dim else 1 for axis in range(len(shape))])
    return factor_of


def noise(stream_key, extent, width, most, cuts=(), kind=jnp.bfloat16):
    values = jax.random.normal(stream_key, extent, jnp.float32) * width
    if len(cuts) > 0:
        values = levels(stream_key, extent, cuts, -0.22, 0.18) * values
    return jnp.clip(values, min=-most, max=most).astype(kind)


def setup_inputs(seed: int = 0) -> dict:
    key_list = jax.random.split(jax.random.key(seed), 15)
    return {
        "inputs": noise(key_list[0], (NROWS, ROW, D), 1.0, 6.0, ((0, 4), (1, 8))),
        "cotangent": noise(key_list[1], (NROWS, ROW, D), 1.0, 6.0, ((0, 4), (1, 8))),
        "lengths": draw_lengths(jax.random.fold_in(key_list[14], 71), 0),
        "clusters": draw_clusters(jax.random.fold_in(key_list[14], 71), 0),
        "gain_attn": jnp.clip(1.0 + 0.18 * jax.random.normal(key_list[4], (D,), jnp.float32), 0.1, 1.9),
        "bias_attn": noise(key_list[5], (D,), 0.1, 0.6, (), jnp.float32),
        "w_query": noise(key_list[6], (D, D), (D * CLUSTERS // (2 * ROW)) ** -0.5, 1.0),
        "w_key": noise(key_list[7], (D, D), (D // 2) ** -0.5, 0.3125),
        "w_value": noise(key_list[8], (D, D), D ** -0.5, 0.21875),
        "w_out": noise(key_list[9], (D, D), (D // 16) ** -0.5, 0.875),
        "gain_ffn": jnp.clip(1.0 + 0.18 * jax.random.normal(key_list[10], (D,), jnp.float32), 0.1, 1.9),
        "bias_ffn": noise(key_list[11], (D,), 0.3, 1.8, (), jnp.float32),
        "w_up": noise(key_list[12], (D, FF), D ** -0.5, 0.21875),
        "w_down": noise(key_list[13], (FF, D), FF ** -0.5, 0.109375),
    }


@jax.custom_vjp
def low(v):
    return lax.optimization_barrier(v.astype(jnp.bfloat16)).astype(jnp.float32)

@jax.custom_vjp
def low_back(v):
    return v

def low_keep(v):
    return (low(v), None)

def low_pass(kept, grad):
    return (grad,)

def back_keep(v):
    return (v, None)

def back_low(kept, grad):
    return (low(grad),)
low.defvjp(low_keep, low_pass)
low_back.defvjp(back_keep, back_low)
EPSILON = 1e-05
PRECISE = lax.Precision.HIGHEST

def layer_norm(values, gain, bias):
    average = lax.optimization_barrier(jnp.mean(values, axis=-1, keepdims=True))
    centered = values - average
    variance = lax.optimization_barrier(jnp.mean(centered * centered, axis=-1, keepdims=True))
    return centered * lax.rsqrt(variance + EPSILON) * gain + bias

def matmul(left, right):
    return jnp.dot(left, right, precision=PRECISE, preferred_element_type=jnp.float32)

def row_forward(row_len, row_clu, values, params):
    gain_attn, bias_attn, w_query, w_key, w_value, w_out, gain_ffn, bias_ffn, w_up, w_down = params
    position = jnp.arange(ROW, dtype=jnp.int32)
    doc_ends = jnp.cumsum(row_len)
    segment = lax.optimization_barrier(jnp.sum((position[:, None] >= doc_ends[None, :]).astype(jnp.int32), axis=1))
    doc_hot = (segment[:, None] == jnp.arange(DOCS, dtype=jnp.int32)[None, :]).astype(jnp.float32)
    absent = (row_len == 0).astype(jnp.float32)
    member = (row_clu[:, :, None] == jnp.arange(CLUSTERS, dtype=jnp.int32)[None, None, :]).astype(jnp.float32)
    normed = low(layer_norm(values, gain_attn, bias_attn))
    query_rows = low_back(low(matmul(normed, w_query))).reshape(ROW, HEADS, HEAD_DIM)
    key_rows = low_back(low(matmul(normed, w_key))).reshape(ROW, HEADS, HEAD_DIM)
    value_rows = low_back(low(matmul(normed, w_value))).reshape(ROW, HEADS, HEAD_DIM)
    counts = lax.optimization_barrier(jnp.sum(member, axis=0))
    sums = jnp.einsum('thc,thd->hcd', member, query_rows, precision=PRECISE)
    centroid = low(sums / counts[:, :, None])
    scores = low_back(jnp.einsum('hcd,thd->hct', centroid, key_rows, precision=PRECISE)) * 0.125
    row_max = lax.optimization_barrier(jnp.max(scores, axis=2, keepdims=True))
    exp_scores = jnp.exp(scores - row_max)
    denom = jnp.einsum('hct,ts->hcs', exp_scores, doc_hot, precision=PRECISE) + absent[None, None, :]
    weights = low(exp_scores)
    unnorm = low_back(jnp.einsum('hct,ts,thd->hcsd', weights, doc_hot, value_rows, precision=PRECISE))
    result = unnorm / denom[:, :, :, None]
    picked = jnp.einsum('thc,ts,hcsd->thd', member, doc_hot, result, precision=PRECISE)
    attended = low(picked).reshape(ROW, D)
    middle = values + low_back(matmul(attended, w_out))
    normed2 = low(layer_norm(middle, gain_ffn, bias_ffn))
    hidden_pre = low_back(matmul(normed2, w_up))
    active = low(jax.nn.gelu(hidden_pre, approximate=True))
    return middle + matmul(active, w_down)

def reference(inputs, cotangent, lengths, clusters, gain_attn, bias_attn, w_query, w_key, w_value, w_out, gain_ffn, bias_ffn, w_up, w_down):
    params = (gain_attn, bias_attn, w_query.astype(jnp.float32), w_key.astype(jnp.float32), w_value.astype(jnp.float32), w_out.astype(jnp.float32), gain_ffn, bias_ffn, w_up.astype(jnp.float32), w_down.astype(jnp.float32))

    def row_step(running, row_data):
        row_in, row_cot, row_len, row_clu = row_data

        def forward(values, weights_all):
            return row_forward(row_len, row_clu, values, weights_all)
        row_out, pullback = jax.vjp(forward, row_in.astype(jnp.float32), params)
        grad_row, grad_params = pullback(row_cot.astype(jnp.float32))
        running = tuple((total + piece for total, piece in zip(running, grad_params)))
        return (running, (row_out, grad_row))
    zero_grads = tuple((jnp.zeros_like(weight) for weight in params))
    totals, (outputs, grad_inputs) = lax.scan(row_step, zero_grads, (inputs, cotangent, lengths, clusters))
    return (outputs, grad_inputs, totals[0], totals[1], totals[2], totals[3], totals[4], totals[5], totals[6], totals[7], totals[8], totals[9])
```

```python
import functools

import jax
import jax.numpy as jnp
from jax import lax
from jax.experimental import pallas as pl
from jax.experimental.pallas import tpu as pltpu
from jax.sharding import PartitionSpec as P

CLUSTERS = 100
PAD = 128
EPSILON = 1e-05
GELU_A = 0.7978845608028654
GELU_B = 0.044715
MESH = pl.DeviceIdType.MESH
F32 = jnp.float32
BF16 = jnp.bfloat16
VMEM_LIMIT = 60 * 2**20


class Plan:
    def __init__(self, mesh_shape, inputs, clusters, lengths, w_up):
        self.seq, self.dp = mesh_shape["seq"], mesh_shape["dp"]
        self.rows, self.part, self.width = inputs.shape
        self.heads, self.docs, self.hidden = clusters.shape[2], lengths.shape[1], w_up.shape[1]
        self.head = self.width // self.heads
        self.tokens = self.rows * self.part
        self.mates = self.seq // self.rows
        self.sent_docs = 1 if self.mates == 2 else self.docs
        self.block = self.width // self.seq
        self.fast = (
            self.dp == 4 and self.seq == 8 and self.block % 16 == 0 and self.hidden == 4 * self.width
        )

    def place(self, j):
        r, h = j // self.mates, j % self.mates
        if self.mates == 2:
            h = lax.rem(h + r, 2)
        return r, h

    def owner(self, r, h):
        if self.mates == 2:
            h = lax.rem(h + r, 2)
        return r * self.mates + h


def nn(a, b):
    return lax.dot_general(a, b, (((1,), (0,)), ((), ())), preferred_element_type=F32)


def nt(a, b):
    return lax.dot_general(a, b, (((1,), (1,)), ((), ())), preferred_element_type=F32)


def tn(a, b):
    return lax.dot_general(a, b, (((0,), (0,)), ((), ())), preferred_element_type=F32)


def remote(src, dst, send, recv, to):
    return pltpu.make_async_remote_copy(
        src_ref=src, dst_ref=dst, send_sem=send, recv_sem=recv, device_id=to, device_id_type=MESH
    )


def one_hot(row):
    ids = lax.broadcasted_iota(jnp.int32, (PAD, row.shape[1]), 0)
    return jnp.where(ids == row, 1.0, 0.0).astype(BF16)


def doc_masks(z, r, h, len_ref):
    pos = h * z.tokens + lax.broadcasted_iota(jnp.int32, (1, z.tokens), 1)
    seg = jnp.zeros((1, z.tokens), jnp.int32)
    end, ends = jnp.int32(0), []
    for s in range(z.docs):
        end = end + len_ref[r, s]
        ends.append(end)
        seg = seg + (pos >= end).astype(jnp.int32)
    last = sum((z.tokens - 1 >= e).astype(jnp.int32) for e in ends)
    first = sum((z.tokens >= e).astype(jnp.int32) for e in ends)
    spans = last == first
    mine = jnp.where(h == 0, last, first)
    return seg, spans, mine


def stacked_masks(z, seg):
    ids = lax.broadcasted_iota(jnp.int32, (z.docs * z.head, z.tokens), 0)
    body = jnp.where(ids // z.head == seg, 1.0, 0.0).astype(BF16)
    low = lax.broadcasted_iota(jnp.int32, (16, z.tokens), 0)
    tail = jnp.where((low % z.docs == seg) & (low < 2 * z.docs), 1.0, 0.0).astype(BF16)
    return body, tail


def pick_doc(z, blocks, mine):
    out = blocks[0]
    for s in range(1, z.docs):
        out = jnp.where(mine == s, blocks[s], out)
    return out


def mate_id(z, r, h, step):
    return {"seq": z.owner(r, lax.rem(h + step, z.mates))}


def greet_row(z, j):
    barrier = pltpu.get_barrier_semaphore()
    for d in range(1, z.seq):
        pl.semaphore_signal(
            barrier, 1, device_id={"seq": lax.rem(j + d, z.seq)}, device_id_type=MESH
        )
    return barrier


def scatter_rows(z, j, r, h, src, dst, send, recv, wait=False):
    slot = lax.rem(j, z.rows)
    for row in range(z.rows):
        to = z.owner(row, j // z.rows)

        @pl.when(to != j)
        def _():
            copy = remote(src.at[row], dst.at[slot], send.at[row], recv.at[slot], {"seq": to})
            if wait:
                copy.wait_send()
            else:
                copy.start()

        if not wait:

            @pl.when(to == j)
            def _():
                pltpu.make_async_copy(src.at[row], dst.at[slot], recv.at[slot]).start()


def landed(z, j, h, src, dst, send, recv, slot):
    source = h * z.rows + slot

    @pl.when(source == j)
    def _():
        pltpu.make_async_copy(src.at[0], dst.at[slot], recv.at[slot]).wait()

    @pl.when(source != j)
    def _():
        remote(
            src.at[0], dst.at[slot], send.at[0], recv.at[slot], {"seq": lax.rem(j + 1, z.seq)}
        ).wait_recv()


def norm_parts(values):
    average = jnp.mean(values, axis=-1, keepdims=True)
    centered = values - average
    inverse = lax.rsqrt(jnp.mean(centered * centered, axis=-1, keepdims=True) + EPSILON)
    return centered * inverse, inverse


def forward_kernel(
    z,
    x_ref, c_ref, clu_ref, len_ref, gain_ref, bias_ref, wq_ref, wk_ref, wv_ref,
    xrow, crow, n_t, k_t, v_t, att_t, wts, cent_t, cnts, res_t, rfac, clus,
    clu_in, q_t, body, sums, sums_in, u_s, big, big_in, small, small_in,
    x_send, x_recv, c_send, c_recv, i_send, i_recv, a_send, a_recv, b_send, b_recv, s_send, s_recv,
):
    j = lax.axis_index("seq")
    r, h = z.place(j)
    barrier = greet_row(z, j)
    seg, spans, mine = doc_masks(z, r, h, len_ref)
    body_value, tail = stacked_masks(z, seg)
    body[...] = body_value
    pl.semaphore_wait(barrier, z.seq - 1)
    scatter_rows(z, j, r, h, clu_ref, clu_in, i_send, i_recv)
    scatter_rows(z, j, r, h, x_ref, xrow, x_send, x_recv)

    def project(slot, carry):
        landed(z, j, h, x_ref, xrow, x_send, x_recv, slot)
        unit, _ = norm_parts(xrow[slot].astype(F32))
        normed = (unit * gain_ref[...] + bias_ref[...]).astype(BF16)
        where = pl.ds(pl.multiple_of(slot * z.part, z.part), z.part)
        n_t[:, where] = normed.T
        for w_ref, out in ((wq_ref, q_t), (wk_ref, k_t), (wv_ref, v_t)):
            out[:, where] = nn(normed, w_ref[...]).astype(BF16).T
        return carry

    lax.fori_loop(0, z.rows, project, 0)
    for slot in range(z.rows):
        landed(z, j, h, clu_ref, clu_in, i_send, i_recv, slot)
        clus[:, slot * z.part : (slot + 1) * z.part] = clu_in[slot]
    scatter_rows(z, j, r, h, x_ref, xrow, x_send, x_recv, wait=True)
    scatter_rows(z, j, r, h, clu_ref, clu_in, i_send, i_recv, wait=True)
    scatter_rows(z, j, r, h, c_ref, crow, c_send, c_recv)

    ones = jnp.ones((16, z.tokens), BF16)

    def sum_copy(i, step):
        return remote(
            sums.at[i], sums_in.at[step - 1, i], a_send.at[step - 1, i], a_recv.at[step - 1, i],
            mate_id(z, r, h, step),
        )

    def result_copies(i, step):
        to = mate_id(z, r, h, step)
        return (
            remote(big.at[i], big_in.at[step - 1, i], b_send.at[step - 1, i], b_recv.at[step - 1, i], to),
            remote(small.at[i], small_in.at[step - 1, i], s_send.at[step - 1, i], s_recv.at[step - 1, i], to),
        )

    def head_rows(i):
        return pl.ds(pl.multiple_of(i * z.head, z.head), z.head)

    def cluster_sums(i, carry):
        member = one_hot(clus[pl.ds(i, 1), :])
        both = nt(jnp.concatenate([q_t[head_rows(i), :], ones], axis=0), member)
        sums[i] = both[: z.head + 8]
        for step in range(1, z.mates):
            sum_copy(i, step).start()
        return carry

    lax.fori_loop(0, z.heads, cluster_sums, 0)

    def attend(i, carry):
        total = sums[i]
        for step in range(1, z.mates):
            sum_copy(i, step).wait()
            total = total + sums_in[step - 1, i]
        count = jnp.maximum(total[z.head :], 1.0)
        cent = (total[: z.head] / count[0:1]).astype(BF16)
        cent_t[i] = cent
        cnts[i] = count
        scores = tn(cent, k_t[head_rows(i), :]) * 0.125
        top = jnp.max(scores, axis=1, keepdims=True)
        weights = jnp.exp(scores - top).astype(BF16)
        wts[i] = weights
        value = v_t[head_rows(i), :]
        masked = jnp.concatenate([value] * z.docs, axis=0) * body[...]
        both = nt(jnp.concatenate([masked, tail], axis=0), weights)
        u_s[i] = both[: z.docs * z.head]
        top_row = jnp.broadcast_to(top, (PAD, PAD)).T
        small[i] = jnp.concatenate([both[z.docs * z.head : z.docs * z.head + 4], top_row[:4]], axis=0)
        if z.mates == 2:
            parts = [both[s * z.head : (s + 1) * z.head] for s in range(z.docs)]
            big[i] = pick_doc(z, parts, mine).astype(BF16)
        else:
            big[i] = both[: z.docs * z.head].astype(BF16)
        for step in range(1, z.mates):
            for copy in result_copies(i, step):
                copy.start()
        return carry

    lax.fori_loop(0, z.heads, attend, 0)
    empty = [jnp.where(jnp.sum((seg == s).astype(F32)) > 0.5, 0.0, 1.0) for s in range(z.docs)]

    def finish(i, carry):
        own = small[i]
        top, denoms = own[4:5], own[:4]
        highest = top
        for step in range(1, z.mates):
            for copy in result_copies(i, step):
                copy.wait()
            highest = jnp.maximum(highest, small_in[step - 1, i][4:5])
        scale = jnp.exp(top - highest)
        member = one_hot(clus[pl.ds(i, 1), :])
        scaled, factors = [], []
        for s in range(z.docs):
            part = u_s[i, s * z.head : (s + 1) * z.head]
            denom = denoms[s : s + 1]
            joined, joined_denom = part * scale, denom * scale
            for step in range(1, z.mates):
                other = small_in[step - 1, i]
                other_scale = jnp.exp(other[4:5] - highest)
                lo = 0 if z.mates == 2 else s * z.head
                joined = joined + big_in[step - 1, i][lo : lo + z.head].astype(F32) * other_scale
                joined_denom = joined_denom + other[s : s + 1] * other_scale
            if z.mates == 2:
                here = jnp.logical_and(spans, mine == s)
            else:
                here = True
            joined = jnp.where(here, joined, part)
            joined_denom = jnp.where(here, joined_denom, denom)
            factor = jnp.where(here, scale, jnp.ones_like(scale))
            joined_denom = joined_denom + jnp.where(joined_denom > 0.0, 0.0, empty[s])
            inverse = 1.0 / joined_denom
            scaled.append((joined * inverse).astype(BF16))
            factors.append(inverse * factor)
        result = jnp.concatenate(scaled, axis=0)
        res_t[i] = result
        rfac[i] = jnp.concatenate(factors + [jnp.zeros((8 - z.docs, PAD), F32)], axis=0)
        picked = nn(result, member)
        out = picked[: z.head]
        for s in range(1, z.docs):
            out = jnp.where(seg == s, picked[s * z.head : (s + 1) * z.head], out)
        att_t[head_rows(i), :] = out.astype(BF16)
        return carry

    lax.fori_loop(0, z.heads, finish, 0)
    for slot in range(z.rows):
        landed(z, j, h, c_ref, crow, c_send, c_recv, slot)
    scatter_rows(z, j, r, h, c_ref, crow, c_send, c_recv, wait=True)


def middle_kernel(
    z,
    xrow, crow, att_t, wo_ref, gain_ref, bias_ref, up_ref, down_ref,
    out_ref, gm_ref, ga_t, d_out, d_up, d_down, vec_ref,
    low, low_t, g_low, act, gp, acc, acc_n,
):
    width, part = z.width, z.part
    total = z.tokens

    def first(t, carry):
        rows = pl.ds(pl.multiple_of(t * part, part), part)
        middle = xrow[t].astype(F32) + tn(att_t[:, rows], wo_ref[...])
        acc[rows, :] = middle
        gm_ref[rows, :] = middle
        unit, _ = norm_parts(middle)
        normed = (unit * gain_ref[...] + bias_ref[...]).astype(BF16)
        low[rows, :] = normed
        low_t[:, rows] = normed.T
        g_low[rows, :] = crow[t]
        return carry

    lax.fori_loop(0, z.rows, first, 0)
    acc_n[...] = jnp.zeros_like(acc_n)

    def chunk(f, carry):
        cols = pl.ds(pl.multiple_of(f * width, width), width)
        half = total // 2
        for t in range(2):
            rows = slice(t * half, (t + 1) * half)
            u = nn(low[rows, :], up_ref[:, cols])
            tanh = jnp.tanh(GELU_A * (u + GELU_B * (u * u * u)))
            cdf = 0.5 * (1.0 + tanh)
            act[rows, :] = (u * cdf).astype(BF16)
            slope = cdf + (0.5 * GELU_A) * u * (1.0 - tanh * tanh) * (1.0 + (3.0 * GELU_B) * (u * u))
            grad = nt(g_low[rows, :], down_ref[cols, :])
            gp[rows, :] = (grad * slope).astype(BF16)
            acc[rows, :] += nn(act[rows, :], down_ref[cols, :])
            acc_n[rows, :] += nt(gp[rows, :], up_ref[:, cols])
        d_up[f] = nn(low_t[...], gp[...]).astype(BF16).reshape(d_up.shape[1:])
        piece = tn(act[...], g_low[...]).astype(BF16)
        if z.fast:
            rows_of = z.hidden // (z.seq * z.dp)
            per = width // (rows_of * z.dp)
            for jj in range(per):
                for p in range(z.dp):
                    at = (jj * z.dp + p) * rows_of
                    d_down[p, f * per + jj] = piece[at : at + rows_of]
        else:
            d_down[cols, :] = piece
        return carry

    lax.fori_loop(0, z.hidden // width, chunk, 0)

    def last(t, carry):
        rows = pl.ds(pl.multiple_of(t * part, part), part)
        out_ref[t] = acc[rows, :].astype(BF16)
        unit, inverse = norm_parts(gm_ref[rows, :])
        grad = acc_n[rows, :]
        scaled = grad * gain_ref[...]
        inner = (
            scaled
            - jnp.mean(scaled, axis=-1, keepdims=True)
            - unit * jnp.mean(scaled * unit, axis=-1, keepdims=True)
        )
        grad_middle = g_low[rows, :].astype(F32) + inner * inverse
        gm_ref[rows, :] = grad_middle
        low[rows, :] = grad_middle.astype(BF16)
        return (
            carry[0] + jnp.sum(grad * unit, axis=0, keepdims=True),
            carry[1] + jnp.sum(grad, axis=0, keepdims=True),
        )

    zero = jnp.zeros((1, width), F32)
    grad_gain, grad_bias = lax.fori_loop(0, z.rows, last, (zero, zero))
    vec_ref[...] = jnp.concatenate([grad_gain, grad_bias], axis=0)
    d_out[...] = nn(att_t[...], low[...]).astype(BF16).reshape(d_out.shape)
    ga_t[...] = nt(wo_ref[...], low[...]).astype(BF16)


def backward_kernel(
    z,
    len_ref, xrow, gm_ref, n_t, k_t, v_t, wts, cent_t, cnts, res_t, rfac, clus, ga_t,
    gain_ref, wq_ref, wk_ref, wv_ref, d_out, d_up, d_down, vec_in, out_rows,
    out_ref, gx_ref, w_qkvo, w_up_ref, w_down_ref, vec_ref,
    body, g_s, g_send, g_recv, c_s, c_recv, gq_t, gk_t, gv_t, acc, x_part,
    dq, crecv, yrecv, xrecv, zrecv, gat, vec_buf, vec_got,
    o_send, o_recv, x_send, x_recv, ga_ss, ga_rs, gc_ss, gc_rs,
    core_s, core_r, y_s, y_r, x_s, x_r, z_s, z_r, dp_s, dp_r, v_s, v_r,
):
    j = lax.axis_index("seq")
    me = lax.axis_index("dp")
    r, h = z.place(j)
    barrier = greet_row(z, j)
    greeted = z.seq - 1
    if z.fast:
        for d in range(1, z.dp):
            pl.semaphore_signal(
                barrier, 1, device_id={"dp": lax.rem(me + d, z.dp)}, device_id_type=MESH
            )
        greeted += z.dp - 1
    seg, spans, mine = doc_masks(z, r, h, len_ref)
    body_value, tail = stacked_masks(z, seg)
    body[...] = body_value
    pl.semaphore_wait(barrier, greeted)

    core, y = lax.rem(me, 2), me // 2
    xx, zz = lax.rem(j, 2), j // 2
    sibling, across = me + 1 - 2 * core, me + 2 - 4 * y
    lanes_of_z = z.seq // 2
    grads = (d_down, d_up, dq)

    def core_copy(g, t):
        yy = (1 - y) if t == 0 else y
        return remote(
            grads[g].at[yy * 2 + 1 - core], crecv.at[g, t], core_s.at[g, t], core_r.at[g, t], {"dp": sibling}
        )

    def y_copy(g, b):
        return remote(
            crecv.at[g, 0, b], yrecv.at[g, b], y_s.at[g, b], y_r.at[g, b], {"dp": across}
        )

    def x_copy(g, k):
        return remote(
            crecv.at[g, 1, 2 * k + 1 - xx], xrecv.at[g, k], x_s.at[g, k], x_r.at[g, k],
            {"seq": j + 1 - 2 * xx},
        )

    def z_copy(g, k):
        to = lax.rem(zz + k, lanes_of_z) * 2 + xx
        return remote(
            crecv.at[g, 1, to], zrecv.at[g, k - 1], z_s.at[g, k - 1], z_r.at[g, k - 1], {"seq": to}
        )

    def dp_copy(g, k):
        return remote(
            gat.at[g, me], gat.at[g, me], dp_s.at[g, k - 1], dp_r.at[g, k - 1],
            {"dp": lax.rem(me + k, z.dp)},
        )

    def dp_wait(g, k):
        source = lax.rem(me + z.dp - k, z.dp)
        remote(
            gat.at[g, source], gat.at[g, source], dp_s.at[g, k - 1], dp_r.at[g, k - 1],
            {"dp": lax.rem(me + k, z.dp)},
        ).wait_recv()

    def add(ref, value):
        ref[...] = (ref[...].astype(F32) + value.astype(F32)).astype(BF16)

    def core_start(g):
        for t in range(2):
            core_copy(g, t).start()

    def block_order(i):
        return lax.rem(i, lanes_of_z) * 2 + jnp.where(i < lanes_of_z, 1 - xx, xx)

    def core_finish(g):
        core_copy(g, 0).wait_recv()

        def forward(i, carry):
            b = block_order(i)
            add(crecv.at[g, 0, b], grads[g][across, b])
            y_copy(g, b).start()
            return carry

        lax.fori_loop(0, z.seq, forward, 0)
        core_copy(g, 1).wait_recv()

        def keep(b, carry):
            add(crecv.at[g, 1, b], grads[g][me, b])
            return carry

        lax.fori_loop(0, z.seq, keep, 0)

    def y_finish(g):
        def away(k, carry):
            b = 2 * k + 1 - xx
            y_copy(g, b).wait_recv()
            add(crecv.at[g, 1, b], yrecv[g, b])
            x_copy(g, k).start()
            return carry

        def keep(k, carry):
            b = 2 * k + xx
            y_copy(g, b).wait_recv()
            add(crecv.at[g, 1, b], yrecv[g, b])
            return carry

        lax.fori_loop(0, lanes_of_z, away, 0)
        lax.fori_loop(0, lanes_of_z, keep, 0)

    def x_finish(g):
        for k in list(range(1, lanes_of_z)) + [0]:
            to = lax.rem(zz + k, lanes_of_z)
            x_copy(g, to).wait_recv()
            add(crecv.at[g, 1, 2 * to + xx], xrecv[g, to])
            if k:
                z_copy(g, k).start()

    def z_finish(g):
        total = crecv[g, 1, j].astype(F32)
        for k in range(1, lanes_of_z):
            z_copy(g, k).wait_recv()
            total = total + zrecv[g, k - 1].astype(F32)
        gat[g, me] = total.astype(BF16)
        for k in range(1, z.dp):
            dp_copy(g, k).start()

    def dp_finish(g):
        for k in range(1, z.dp):
            dp_wait(g, k)
        for p in range(z.dp):
            block = gat[g, p].astype(F32)
            if g == 0:
                w_down_ref[p * z.block : (p + 1) * z.block, :] = block
            elif g == 1:
                w_up_ref[:, p * z.width : (p + 1) * z.width] = block
            else:
                w_qkvo[p] = block

    def sent(g):
        for t in range(2):
            core_copy(g, t).wait_send()

        def y_sent(b, carry):
            y_copy(g, b).wait_send()
            return carry

        lax.fori_loop(0, z.seq, y_sent, 0)

        def x_sent(k, carry):
            x_copy(g, k).wait_send()
            return carry

        lax.fori_loop(0, lanes_of_z, x_sent, 0)
        for k in range(1, lanes_of_z):
            z_copy(g, k).wait_send()
        for k in range(1, z.dp):
            dp_copy(g, k).wait_send()

    if z.fast:
        core_start(0)
        core_start(1)

    def back(slot):
        return h * z.rows + slot

    def rows_back(src, dst, send, recv, wait=False):
        for slot in range(z.rows):
            to = back(slot)

            @pl.when(to != j)
            def _():
                copy = remote(src.at[slot], dst.at[r], send.at[slot], recv.at[r], {"seq": to})
                if wait:
                    copy.wait_send()
                else:
                    copy.start()

            if not wait:

                @pl.when(to == j)
                def _():
                    pltpu.make_async_copy(src.at[slot], dst.at[r], recv.at[r]).start()

    def rows_landed(src, dst, send, recv):
        for row in range(z.rows):
            source = z.owner(row, j // z.rows)

            @pl.when(source == j)
            def _():
                pltpu.make_async_copy(src.at[0], dst.at[row], recv.at[row]).wait()

            @pl.when(source != j)
            def _():
                remote(
                    src.at[0], dst.at[row], send.at[0], recv.at[row], {"seq": lax.rem(j + 1, z.seq)}
                ).wait_recv()

    rows_back(out_rows, out_ref, o_send, o_recv)

    def head_rows(i):
        return pl.ds(pl.multiple_of(i * z.head, z.head), z.head)

    def grad_copy(i, step):
        return remote(
            g_send.at[i], g_recv.at[step - 1, i], ga_ss.at[step - 1, i], ga_rs.at[step - 1, i],
            mate_id(z, r, h, step),
        )

    def cent_copy(i, step):
        return remote(
            c_s.at[i], c_recv.at[step - 1, i], gc_ss.at[step - 1, i], gc_rs.at[step - 1, i],
            mate_id(z, r, h, step),
        )

    def gather_grads(i, carry):
        member = one_hot(clus[pl.ds(i, 1), :])
        masked = jnp.concatenate([ga_t[head_rows(i), :]] * z.docs, axis=0) * body[...]
        both = nt(masked, member)
        g_s[i] = both
        if z.mates == 2:
            parts = [both[s * z.head : (s + 1) * z.head] for s in range(z.docs)]
            g_send[i] = pick_doc(z, parts, mine).astype(BF16)
        else:
            g_send[i] = both.astype(BF16)
        for step in range(1, z.mates):
            grad_copy(i, step).start()
        return carry

    lax.fori_loop(0, z.heads, gather_grads, 0)
    if z.fast:
        core_finish(0)
        core_finish(1)

    def attend_back(i, carry):
        for step in range(1, z.mates):
            grad_copy(i, step).wait()
        result, factor = res_t[i], rfac[i]
        lows, deltas = [], []
        for s in range(z.docs):
            grad = g_s[i, s * z.head : (s + 1) * z.head]
            joined = grad
            for step in range(1, z.mates):
                lo = 0 if z.mates == 2 else s * z.head
                joined = joined + g_recv[step - 1, i][lo : lo + z.head].astype(F32)
            if z.mates == 2:
                joined = jnp.where(jnp.logical_and(spans, mine == s), joined, grad)
            scaled = joined * factor[s : s + 1]
            lows.append(scaled.astype(BF16))
            part = result[s * z.head : (s + 1) * z.head].astype(F32)
            deltas.append(-jnp.sum(scaled * part, axis=0, keepdims=True))
        delta = jnp.concatenate(deltas, axis=0)
        high = delta.astype(BF16)
        rest = (delta - high.astype(F32)).astype(BF16)
        small = jnp.concatenate(
            [high.astype(F32), rest.astype(F32), jnp.zeros((16 - 2 * z.docs, PAD), F32)], axis=0
        ).astype(BF16)
        low = jnp.concatenate(lows, axis=0)
        value = v_t[head_rows(i), :]
        masked = jnp.concatenate([value] * z.docs, axis=0) * body[...]
        diff = tn(
            jnp.concatenate([low, small], axis=0), jnp.concatenate([masked, tail], axis=0)
        )
        weights = wts[i]
        raw = (0.125 * (weights.astype(F32) * diff)).astype(BF16)
        gk_t[head_rows(i), :] = nn(cent_t[i], raw).astype(BF16)
        spread = nn(low, weights)
        out = spread[: z.head]
        for s in range(1, z.docs):
            out = jnp.where(seg == s, spread[s * z.head : (s + 1) * z.head], out)
        gv_t[head_rows(i), :] = out.astype(BF16)
        c_s[i] = nt(k_t[head_rows(i), :], raw)
        for step in range(1, z.mates):
            cent_copy(i, step).start()
        return carry

    lax.fori_loop(0, z.heads, attend_back, 0)

    def query_back(i, carry):
        total = c_s[i]
        for step in range(1, z.mates):
            cent_copy(i, step).wait()
            total = total + c_recv[step - 1, i]
        member = one_hot(clus[pl.ds(i, 1), :])
        gq_t[head_rows(i), :] = nn((total / cnts[i, 0:1]).astype(BF16), member).astype(BF16)
        return carry

    lax.fori_loop(0, z.heads, query_back, 0)

    for p, g_ref in enumerate((gq_t, gk_t, gv_t)):
        dq[p] = nt(n_t[...], g_ref[...]).astype(BF16).reshape(dq.shape[1:])
    dq[3] = d_out[...]
    if z.fast:
        core_start(2)
    total = nn(wq_ref[...], gq_t[...]) + nn(wk_ref[...], gk_t[...]) + nn(wv_ref[...], gv_t[...])
    acc[...] = total.T

    def last(t, carry):
        rows = pl.ds(pl.multiple_of(t * z.part, z.part), z.part)
        unit, inverse = norm_parts(xrow[t].astype(F32))
        grad = acc[rows, :]
        scaled = grad * gain_ref[...]
        inner = (
            scaled
            - jnp.mean(scaled, axis=-1, keepdims=True)
            - unit * jnp.mean(scaled * unit, axis=-1, keepdims=True)
        )
        x_part[t] = (gm_ref[rows, :] + inner * inverse).astype(BF16)
        return (
            carry[0] + jnp.sum(grad * unit, axis=0, keepdims=True),
            carry[1] + jnp.sum(grad, axis=0, keepdims=True),
        )

    zero = jnp.zeros((1, z.width), F32)
    grad_gain, grad_bias = lax.fori_loop(0, z.rows, last, (zero, zero))
    vectors = jnp.concatenate([grad_gain, grad_bias, vec_in[...], jnp.zeros((4, z.width), F32)], axis=0)
    rows_back(x_part, gx_ref, x_send, x_recv)

    if z.fast:
        core_finish(2)
        y_finish(0)
        y_finish(1)
        x_finish(0)
        x_finish(1)
        y_finish(2)
        z_finish(0)
        z_finish(1)
        x_finish(2)
        z_finish(2)

        def vec_copy(t, to):
            return remote(vec_buf.at[min(t, 2)], vec_got.at[t], v_s.at[t], v_r.at[t], to)

        vec_buf[0] = vectors
        copy = vec_copy(0, {"dp": sibling})
        copy.start()
        copy.wait()
        vec_buf[1] = vec_buf[0] + vec_got[0]
        copy = vec_copy(1, {"dp": across})
        copy.start()
        copy.wait()
        vec_buf[2] = vec_buf[1] + vec_got[1]
        copies = [vec_copy(1 + d, {"seq": lax.rem(j + d, z.seq)}) for d in range(1, z.seq)]
        for copy in copies:
            copy.start()
        total = vec_buf[2]
        for d, copy in enumerate(copies):
            copy.wait()
            total = total + vec_got[2 + d]
        vec_ref[...] = total
        for g in range(3):
            dp_finish(g)
        for g in range(3):
            sent(g)
    else:
        vec_ref[...] = vectors
        for p in range(4):
            w_qkvo[p] = dq[p].astype(F32)

    rows_landed(out_rows, out_ref, o_send, o_recv)
    rows_landed(x_part, gx_ref, x_send, x_recv)
    rows_back(out_rows, out_ref, o_send, o_recv, wait=True)
    rows_back(x_part, gx_ref, x_send, x_recv, wait=True)


def local(
    mesh_shape,
    inputs, cotangent, lengths, clusters, gain_attn, bias_attn, w_query, w_key, w_value, w_out,
    gain_ffn, bias_ffn, w_up, w_down,
):
    z = Plan(mesh_shape, inputs, clusters, lengths, w_up)
    width, tokens, heads, mates, docs = z.width, z.tokens, z.heads, z.mates, z.docs
    any_space = pl.BlockSpec(memory_space=pl.ANY)
    vmem = pl.BlockSpec(memory_space=pltpu.VMEM)
    smem = pl.BlockSpec(memory_space=pltpu.SMEM)
    dma = pltpu.SemaphoreType.DMA
    shape = jax.ShapeDtypeStruct
    high_heads = -(-heads // 8) * 8
    turned = jnp.pad(jnp.transpose(clusters, (0, 2, 1)), ((0, 0), (0, high_heads - heads), (0, 0)))
    flat = lambda v: v.reshape(1, -1)
    row_like = shape((z.rows, z.part, width), BF16)
    long = shape((width, tokens), BF16)
    others = mates - 1
    xrow, crow, n_t, k_t, v_t, att_t, wts, cent_t, cnts, res_t, rfac, clus = pl.pallas_call(
        functools.partial(forward_kernel, z),
        out_shape=(
            row_like, row_like, long, long, long, long,
            shape((heads, PAD, tokens), BF16),
            shape((heads, z.head, PAD), BF16),
            shape((heads, 8, PAD), F32),
            shape((heads, docs * z.head, PAD), BF16),
            shape((heads, 8, PAD), F32),
            shape((high_heads, tokens), jnp.int32),
        ),
        in_specs=[any_space, any_space, any_space, smem] + [vmem] * 5,
        out_specs=[vmem] * 12,
        scratch_shapes=[
            pltpu.VMEM((z.rows, high_heads, z.part), jnp.int32),
            pltpu.VMEM((width, tokens), BF16),
            pltpu.VMEM((docs * z.head, tokens), BF16),
            pltpu.VMEM((heads, z.head + 8, PAD), F32),
            pltpu.VMEM((others, heads, z.head + 8, PAD), F32),
            pltpu.VMEM((heads, docs * z.head, PAD), F32),
            pltpu.VMEM((heads, z.sent_docs * z.head, PAD), BF16),
            pltpu.VMEM((others, heads, z.sent_docs * z.head, PAD), BF16),
            pltpu.VMEM((heads, 8, PAD), F32),
            pltpu.VMEM((others, heads, 8, PAD), F32),
        ]
        + [dma((z.rows,))] * 6
        + [dma((others, heads))] * 6,
        compiler_params=pltpu.CompilerParams(
            collective_id=0, has_side_effects=True, vmem_limit_bytes=VMEM_LIMIT
        ),
    )(
        inputs, cotangent, turned, lengths, flat(gain_attn), flat(bias_attn), w_query, w_key, w_value
    )

    if z.fast:
        square = shape((z.seq, z.block, width), BF16)
        up_shape = shape((4, z.seq, z.block, width), BF16)
        down_shape = shape((z.dp, z.seq, z.hidden // (z.seq * z.dp), width), BF16)
    else:
        square = shape((width, width), BF16)
        up_shape = shape((z.hidden // width, width, width), BF16)
        down_shape = shape((z.hidden, width), BF16)
    out_rows, gm, ga_t, d_out, d_up, d_down, vec_ffn = pl.pallas_call(
        functools.partial(middle_kernel, z),
        out_shape=(
            row_like, shape((tokens, width), F32), long, square, up_shape, down_shape,
            shape((2, width), F32),
        ),
        in_specs=[vmem] * 8,
        out_specs=[vmem] * 7,
        scratch_shapes=[
            pltpu.VMEM((tokens, width), BF16),
            pltpu.VMEM((width, tokens), BF16),
            pltpu.VMEM((tokens, width), BF16),
            pltpu.VMEM((tokens, width), BF16),
            pltpu.VMEM((tokens, width), BF16),
            pltpu.VMEM((tokens, width), F32),
            pltpu.VMEM((tokens, width), F32),
        ],
        compiler_params=pltpu.CompilerParams(vmem_limit_bytes=VMEM_LIMIT),
    )(xrow, crow, att_t, w_out, flat(gain_ffn), flat(bias_ffn), w_up, w_down)

    if z.fast:
        outs = (
            shape((4, z.block, width), F32),
            shape((z.block, z.hidden), F32),
            shape((z.hidden // z.seq, width), F32),
        )
        rs = [
            pltpu.VMEM((4, z.seq, z.block, width), BF16),
            pltpu.VMEM((3, 2, z.seq, z.block, width), BF16),
            pltpu.VMEM((3, z.seq, z.block, width), BF16),
            pltpu.VMEM((3, z.seq // 2, z.block, width), BF16),
            pltpu.VMEM((3, z.seq // 2 - 1, z.block, width), BF16),
            pltpu.VMEM((3, z.dp, z.block, width), BF16),
        ]
        wide = vmem
    else:
        outs = (shape((4, width, width), F32), shape((8, PAD), F32), shape((8, PAD), F32))
        rs = [pltpu.VMEM((4, width, width), BF16)] + [pltpu.VMEM((8, PAD), BF16)] * 5
        wide = any_space
    out_back, grad_back, g_qkvo, g_up, g_down, vectors = pl.pallas_call(
        functools.partial(backward_kernel, z),
        out_shape=(row_like, row_like) + outs + (shape((8, width), F32),),
        in_specs=[smem] + [vmem] * 17 + [wide, wide] + [vmem] * 2,
        out_specs=[vmem] * 6,
        scratch_shapes=[
            pltpu.VMEM((docs * z.head, tokens), BF16),
            pltpu.VMEM((heads, docs * z.head, PAD), F32),
            pltpu.VMEM((heads, z.sent_docs * z.head, PAD), BF16),
            pltpu.VMEM((others, heads, z.sent_docs * z.head, PAD), BF16),
            pltpu.VMEM((heads, z.head, PAD), F32),
            pltpu.VMEM((others, heads, z.head, PAD), F32),
            pltpu.VMEM((width, tokens), BF16),
            pltpu.VMEM((width, tokens), BF16),
            pltpu.VMEM((width, tokens), BF16),
            pltpu.VMEM((tokens, width), F32),
            pltpu.VMEM((z.rows, z.part, width), BF16),
        ]
        + rs
        + [pltpu.VMEM((3, 8, width), F32), pltpu.VMEM((z.seq + 1, 8, width), F32)]
        + [dma((z.rows,))] * 4
        + [dma((others, heads))] * 4
        + [dma((3, 2))] * 2
        + [dma((3, z.seq))] * 2
        + [dma((3, z.seq // 2))] * 4
        + [dma((3, z.dp))] * 2
        + [dma((z.seq + 1,))] * 2,
        compiler_params=pltpu.CompilerParams(
            collective_id=1, has_side_effects=True, vmem_limit_bytes=VMEM_LIMIT
        ),
    )(
        lengths, xrow, gm, n_t, k_t, v_t, wts, cent_t, cnts, res_t, rfac, clus, ga_t,
        flat(gain_attn), w_query, w_key, w_value, d_out, d_up, d_down, vec_ffn, out_rows,
    )

    if z.fast:
        own = lax.dynamic_slice_in_dim(vectors, lax.axis_index("seq") * z.block, z.block, 1)
    else:
        wide_up = jnp.transpose(d_up, (1, 0, 2)).reshape(width, z.hidden)

        def share(v, dim):
            v = lax.psum_scatter(v.astype(F32), "seq", scatter_dimension=dim, tiled=True)
            return lax.psum(v, "dp")

        g_qkvo, g_up, g_down, own = (
            share(g_qkvo, 1), share(wide_up, 0), share(d_down, 0), share(vectors, 1),
        )
    return (
        out_back.astype(F32), grad_back.astype(F32), own[0], own[1],
        g_qkvo[0], g_qkvo[1], g_qkvo[2], g_qkvo[3], own[2], own[3], g_up, g_down,
    )


def solution(mesh):
    spread = P("dp", "seq", None)
    return jax.shard_map(
        functools.partial(local, dict(mesh.shape)),
        mesh=mesh,
        in_specs=(spread, spread, P("dp", None), spread) + (P(),) * 10,
        out_specs=(spread, spread, P("seq"), P("seq")) + (P("seq", None),) * 4
        + (P("seq"), P("seq"), P("seq", None), P("seq", None)),
        check_vma=False,
    )
```

```python
import functools

import jax
import jax.numpy as jnp
from jax import lax
from jax.experimental import pallas as pl
from jax.experimental.pallas import tpu as pltpu
from jax.sharding import PartitionSpec as P

CLUSTERS = 100
PAD = 128
EPSILON = 1e-05
GELU_A = 0.7978845608028654
GELU_B = 0.044715
MESH = pl.DeviceIdType.MESH
F32 = jnp.float32
BF16 = jnp.bfloat16
VMEM_LIMIT = 63 * 2**20


def schedule():
    def both(g, *ks):
        return [("one", g, k, o) for k in ks for o in range(2)]

    def side(g, o, *ks):
        return [("one", g, k, o) for k in ks]

    def two(g):
        return [("two", g, k) for k in range(4)]

    return (
        ((),) * 6,
        (both(0, 0), both(0, 1), side(1, 0, 0, 1), side(1, 0, 2, 3), both(0, 2), ()),
        (both(0, 3), side(1, 1, 0, 1), side(1, 1, 2, 3)),
        [("part", 2), ("part", 0)],
        two(0) + two(1) + [("vec", 1)] + both(2, 0, 1, 2, 3) + [("vec", 2)] + two(2)
        + [("three", 0), ("three", 1), ("gather", 0), ("gather", 1), ("vec", 3), ("three", 2), ("gather", 2)],
    )


class Plan:
    def __init__(self, mesh_shape, inputs, clusters, lengths, w_up):
        self.seq, self.dp = mesh_shape["seq"], mesh_shape["dp"]
        self.rows, self.part, self.width = inputs.shape
        self.heads, self.docs, self.hidden = clusters.shape[2], lengths.shape[1], w_up.shape[1]
        self.head = self.width // self.heads
        self.tokens = self.rows * self.part
        self.mates = self.seq // self.rows
        self.sent_docs = 1 if self.mates == 2 else self.docs
        self.block = self.width // self.seq
        self.fast = (
            self.dp == 4 and self.seq == 8 and self.block % 16 == 0 and self.hidden == 4 * self.width
        )
        self.reduce = self.fast
        self.sent_rows = -(-CLUSTERS // 16) * 16
        self.small_rows = 8 if self.mates == 2 else 16
        self.count_rows = -(-self.heads // 8) * 8
        self.tasks = schedule()
        self.square = (self.seq, self.block, self.width) if self.fast else (self.width, self.width)
        self.y_first = ((True,) * 4, (False,) * 4, (True, False, True, False))

    def place(self, j):
        return lax.rem(j, self.rows), j // self.rows

    def owner(self, r, h):
        return h * self.rows + r


def nn(a, b):
    return lax.dot_general(a, b, (((1,), (0,)), ((), ())), preferred_element_type=F32)


def nt(a, b):
    return lax.dot_general(a, b, (((1,), (1,)), ((), ())), preferred_element_type=F32)


def tn(a, b):
    return lax.dot_general(a, b, (((0,), (0,)), ((), ())), preferred_element_type=F32)


def remote(src, dst, send, recv, to):
    return pltpu.make_async_remote_copy(
        src_ref=src, dst_ref=dst, send_sem=send, recv_sem=recv, device_id=to, device_id_type=MESH
    )


def one_hot(row):
    ids = lax.broadcasted_iota(jnp.int32, (PAD, row.shape[1]), 0)
    return jnp.where(ids == row, 1.0, 0.0).astype(BF16)


def doc_masks(z, r, h, len_ref):
    pos = h * z.tokens + lax.broadcasted_iota(jnp.int32, (1, z.tokens), 1)
    seg = jnp.zeros((1, z.tokens), jnp.int32)
    end, ends = jnp.int32(0), []
    for s in range(z.docs):
        end = end + len_ref[r, s]
        ends.append(end)
        seg = seg + (pos >= end).astype(jnp.int32)
    last = sum((z.tokens - 1 >= e).astype(jnp.int32) for e in ends)
    first = sum((z.tokens >= e).astype(jnp.int32) for e in ends)
    spans = last == first
    mine = jnp.where(h == 0, last, first)
    return seg, spans, mine


def stacked_masks(z, seg):
    ids = lax.broadcasted_iota(jnp.int32, (z.docs * z.head, z.tokens), 0)
    body = jnp.where(ids // z.head == seg, 1.0, 0.0).astype(BF16)
    low = lax.broadcasted_iota(jnp.int32, (16, z.tokens), 0)
    tail = jnp.where((low % z.docs == seg) & (low < 2 * z.docs), 1.0, 0.0).astype(BF16)
    return body, tail


def pick_doc(z, blocks, mine):
    out = blocks[0]
    for s in range(1, z.docs):
        out = jnp.where(mine == s, blocks[s], out)
    return out


def mate_id(z, r, h, step):
    return {"seq": z.owner(r, lax.rem(h + step, z.mates))}


def rows_out(z, j, r, h, src, dst, send, recv):
    for row in range(z.rows):
        to = z.owner(row, h)

        @pl.when(to != j)
        def _():
            remote(src.at[row], dst.at[r], send.at[row], recv.at[r], {"seq": to}).start()

        @pl.when(to == j)
        def _():
            pltpu.make_async_copy(src.at[row], dst.at[r], recv.at[r]).start()


def rows_landed(z, j, h, src, dst, send, recv, slot):
    source = z.owner(slot, h)

    @pl.when(source == j)
    def _():
        pltpu.make_async_copy(src.at[0], dst.at[slot], recv.at[slot]).wait()

    @pl.when(source != j)
    def _():
        remote(src.at[0], dst.at[slot], send.at[0], recv.at[slot], {"seq": source}).wait_recv()


def rows_sent(z, j, h, src, dst, send, recv):
    for row in range(z.rows):
        to = z.owner(row, h)

        @pl.when(to != j)
        def _():
            remote(src.at[row], dst.at[0], send.at[row], recv.at[0], {"seq": to}).wait_send()


def norm_parts(values):
    average = jnp.mean(values, axis=-1, keepdims=True)
    centered = values - average
    inverse = lax.rsqrt(jnp.mean(centered * centered, axis=-1, keepdims=True) + EPSILON)
    return centered * inverse, inverse


def norm_back(grad, unit, inverse, gain):
    scaled = grad * gain
    inner = (
        scaled
        - jnp.mean(scaled, axis=-1, keepdims=True)
        - unit * jnp.mean(scaled * unit, axis=-1, keepdims=True)
    )
    return inner * inverse


def joined_masks(z, blocks, seg):
    out = blocks[: z.head]
    for s in range(1, z.docs):
        out = jnp.where(seg == s, blocks[s * z.head : (s + 1) * z.head], out)
    return out


class Refs:
    def __init__(self, names, values):
        self.__dict__.update(zip(names, values, strict=True))


def block_kernel(z, names, *values):
    f = Refs(names, values)
    j = lax.axis_index("seq")
    me = lax.axis_index("dp")
    r, h = z.place(j)
    width, part = z.width, z.part

    barrier = pltpu.get_barrier_semaphore()
    for d in range(1, z.seq):
        pl.semaphore_signal(
            barrier, 1, device_id={"seq": lax.rem(j + d, z.seq)}, device_id_type=MESH
        )
    greeted = z.seq - 1
    if z.reduce:
        for d in range(1, z.dp):
            pl.semaphore_signal(
                barrier, 1, device_id={"dp": lax.rem(me + d, z.dp)}, device_id_type=MESH
            )
        greeted += z.dp - 1

    loads = [
        pltpu.make_async_copy(ref, f.w_qkv.at[p], f.load.at[p])
        for p, ref in enumerate((f.wq_in, f.wk_in, f.wv_in))
    ]
    loads.append(pltpu.make_async_copy(f.wo_in, f.w_o, f.load.at[3]))
    chunks = z.hidden // width
    for c in range(chunks):
        loads.append(
            pltpu.make_async_copy(
                f.up_in.at[(slice(None),) * (len(z.square) - 1) + (pl.ds(c * width, width),)],
                f.w_up.at[c],
                f.load.at[4 + c],
            )
        )
        loads.append(
            pltpu.make_async_copy(f.down_in.at[c], f.w_down.at[c], f.load.at[4 + chunks + c])
        )
    for copy in loads[:3]:
        copy.start()

    seg, spans, mine = doc_masks(z, r, h, f.lengths)
    body_value, tail = stacked_masks(z, seg)
    f.body[...] = body_value
    gain_attn, bias_attn = f.gain_attn[...].reshape(1, width), f.bias_attn[...].reshape(1, width)
    gain_ffn, bias_ffn = f.gain_ffn[...].reshape(1, width), f.bias_ffn[...].reshape(1, width)
    pl.semaphore_wait(barrier, greeted)

    def clu_copy(step):
        to = {"seq": z.owner(lax.rem(r + step, z.rows), h)}
        return remote(f.clu_in, f.clu_got.at[step], f.i_send.at[step], f.i_recv.at[step], to)

    own_clu = pltpu.make_async_copy(f.clu_in, f.clu_got.at[0], f.i_recv.at[0])
    own_clu.start()
    for step in range(1, z.rows):
        clu_copy(step).start()
    rows_out(z, j, r, h, f.x_in, f.xrow, f.x_send, f.x_recv)
    for copy in loads[3:]:
        copy.start()

    def part_rows(t):
        return pl.ds(pl.multiple_of(t * part, part), part)

    def head_rows(i):
        return pl.ds(pl.multiple_of(i * z.head, z.head), z.head)

    own_clu.wait()
    for step in range(z.rows):
        if step:
            clu_copy(step).wait()
        slot = lax.rem(r + z.rows - step, z.rows)
        numbers = f.clu_got[step, :, pl.ds(r, 1), :].reshape(z.heads, part)
        f.clus[:, part_rows(slot)] = numbers

    def mate_copy(src, dst, send, recv, i, step):
        to = {"seq": z.owner(r, lax.rem(h + step, z.mates))}
        return remote(src.at[i], dst.at[step - 1, i], send.at[step - 1, i], recv.at[step - 1, i], to)

    def sum_copy(i, step):
        return mate_copy(f.sums, f.sums_in, f.a_ss, f.a_rs, i, step)

    def result_copies(i, step):
        return (
            mate_copy(f.big, f.big_in, f.b_ss, f.b_rs, i, step),
            mate_copy(f.small, f.small_in, f.s_ss, f.s_rs, i, step),
        )

    def grad_copy(i, step):
        return mate_copy(f.g_send, f.g_recv, f.g_ss, f.g_rs, i, step)

    def cent_copy(i, step):
        return mate_copy(f.c_s, f.c_got, f.q_ss, f.q_rs, i, step)

    others = range(1, z.mates)
    stack = z.docs * z.head
    pairs = z.heads // 2
    low_lanes = z.sent_rows

    def pack(pair):
        return pair.astype(BF16).T[:low_lanes]

    def unpack(packed):
        rest = jnp.zeros((PAD - low_lanes, PAD), BF16)
        return jnp.concatenate([packed, rest], axis=0).T.astype(F32)

    def member_of(i):
        return one_hot(f.clus[pl.ds(i, 1), :])

    ones = jnp.ones((8, z.tokens), BF16)
    f.cnt_out[...] = jnp.zeros_like(f.cnt_out)
    for i in range(z.heads):
        f.cnt_out[i : i + 1] = nt(ones, one_hot(f.clus[i : i + 1, :]))[:1]

    def count_copy(step):
        to = {"seq": z.owner(r, lax.rem(h + step, z.mates))}
        return remote(f.cnt_out, f.cnt_in.at[step - 1], f.k_ss.at[step - 1], f.k_rs.at[step - 1], to)

    for step in others:
        count_copy(step).start()
    for copy in loads[:3]:
        copy.wait()

    def project(slot, carry):
        rows_landed(z, j, h, f.x_in, f.xrow, f.x_send, f.x_recv, slot)
        unit, _ = norm_parts(f.xrow[slot].astype(F32))
        normed = (unit * gain_attn + bias_attn).astype(BF16)
        f.low[part_rows(slot), :] = normed
        f.n_t[:, part_rows(slot)] = normed.T
        f.q_t[:, part_rows(slot)] = nn(normed, f.w_qkv[0]).astype(BF16).T
        return carry

    lax.fori_loop(0, z.rows, project, 0)

    def cluster_sums(i, carry):
        pair = jnp.concatenate(
            [nt(f.q_t[head_rows(2 * i + a), :], member_of(2 * i + a)) for a in range(2)], axis=0
        )
        f.sums_f[i] = pair
        f.sums[i] = pack(pair)
        for step in others:
            sum_copy(i, step).start()
        return carry

    lax.fori_loop(0, pairs, cluster_sums, 0)
    rows_sent(z, j, h, f.x_in, f.xrow, f.x_send, f.x_recv)
    rows_out(z, j, r, h, f.c_in, f.crow, f.c_send, f.c_recv)
    counts = f.cnt_out[...]
    for step in others:
        count_copy(step).wait()
        counts = counts + f.cnt_in[step - 1]
    f.cnts[...] = jnp.maximum(counts, 1.0)

    def project_more(t, carry):
        normed = f.low[part_rows(t), :]
        f.k_t[:, part_rows(t)] = nn(normed, f.w_qkv[1]).astype(BF16).T
        f.v_t[:, part_rows(t)] = nn(normed, f.w_qkv[2]).astype(BF16).T
        return carry

    lax.fori_loop(0, z.rows, project_more, 0)

    def masked_values(i):
        return jnp.concatenate([f.v_t[head_rows(i), :]] * z.docs, axis=0) * f.body[...]

    def doc_rows(blocks, s):
        return blocks[s * z.head : (s + 1) * z.head]

    def border(blocks):
        if z.mates == 2:
            parts = [[doc_rows(b, s) for s in range(z.docs)] for b in blocks]
            return [pack(jnp.concatenate([pick_doc(z, p, mine) for p in parts], axis=0))]
        return [
            pack(jnp.concatenate([doc_rows(b, s) for b in blocks], axis=0)) for s in range(z.docs)
        ]

    def attend(i, carry):
        total = f.sums_f[i]
        for step in others:
            sum_copy(i, step).wait()
            total = total + unpack(f.sums_in[step - 1, i])
        blocks, small = [], []
        for a in range(2):
            n = 2 * i + a
            count = f.cnts[pl.ds(n, 1), :]
            cent = (total[a * z.head : (a + 1) * z.head] / count).astype(BF16)
            f.cent_t[n] = cent
            scores = tn(cent, f.k_t[head_rows(n), :]) * 0.125
            top = jnp.max(scores, axis=1, keepdims=True)
            weights = jnp.exp(scores - top).astype(BF16)
            f.wts[n] = weights
            both = nt(jnp.concatenate([masked_values(n), tail], axis=0), weights)
            f.u_s[n] = both[:stack]
            top_row = jnp.broadcast_to(top, (PAD, PAD)).T
            denoms = both[stack : stack + 4]
            f.dens[n] = jnp.concatenate([denoms, top_row[:4]], axis=0)
            blocks.append(both[:stack])
            if z.mates == 2:
                own = pick_doc(z, [denoms[s : s + 1] for s in range(z.docs)], mine)
                small += [jnp.broadcast_to(own, (2, PAD)), top_row[:2]]
            else:
                small += [denoms, top_row[:4]]
        f.small[i] = jnp.concatenate(small, axis=0)
        for d, packed in enumerate(border(blocks)):
            f.big[i, d] = packed
        for step in others:
            for copy in result_copies(i, step):
                copy.start()
        return carry

    lax.fori_loop(0, pairs, attend, 0)
    empty = [jnp.where(jnp.sum((seg == s).astype(F32)) > 0.5, 0.0, 1.0) for s in range(z.docs)]
    half_small = z.small_rows // 2

    def finish(i, carry):
        got = []
        for step in others:
            for copy in result_copies(i, step):
                copy.wait()
            got.append([unpack(f.big_in[step - 1, i, d]) for d in range(z.sent_docs)])
        for a in range(2):
            n = 2 * i + a
            own = f.dens[n]
            top, highest = own[4:5], own[4:5]
            sides = []
            for step in others:
                side = f.small_in[step - 1, i, a * half_small : (a + 1) * half_small]
                sides.append((side, side[half_small // 2 : half_small // 2 + 1]))
                highest = jnp.maximum(highest, sides[-1][1])
            scale = jnp.exp(top - highest)
            scaled, factors = [], []
            for s in range(z.docs):
                piece = f.u_s[n, s * z.head : (s + 1) * z.head]
                denom = own[s : s + 1]
                joined, joined_denom = piece * scale, denom * scale
                d = 0 if z.mates == 2 else s
                for other, (side, side_top) in zip(got, sides):
                    side_scale = jnp.exp(side_top - highest)
                    joined = joined + other[d][a * z.head : (a + 1) * z.head] * side_scale
                    joined_denom = joined_denom + side[d : d + 1] * side_scale
                here = jnp.logical_and(spans, mine == s) if z.mates == 2 else True
                joined = jnp.where(here, joined, piece)
                joined_denom = jnp.where(here, joined_denom, denom)
                factor = jnp.where(here, scale, jnp.ones_like(scale))
                joined_denom = joined_denom + jnp.where(joined_denom > 0.0, 0.0, empty[s])
                inverse = 1.0 / joined_denom
                scaled.append((joined * inverse).astype(BF16))
                factors.append(inverse * factor)
            result = jnp.concatenate(scaled, axis=0)
            f.res_t[n] = result
            f.rfac[n] = jnp.concatenate(factors + [jnp.zeros((8 - z.docs, PAD), F32)], axis=0)
            f.att_t[head_rows(n), :] = joined_masks(z, nn(result, member_of(n)), seg).astype(BF16)
        return carry

    lax.fori_loop(0, pairs, finish, 0)

    core, y = lax.rem(me, 2), me // 2
    xx, zz = lax.rem(j, 2), j // 2
    sibling, across = me + 1 - 2 * core, me + 2 - 4 * y
    beside = j + 1 - 2 * xx
    deep = z.seq // 2
    if z.reduce:
        grads = (f.d_down, f.d_up, f.w_up)
        core_in = (f.core_in.at[0], f.core_in.at[1], f.w_down.at[pl.ds(0, 2)])
        first_in = (f.first_in.at[0], f.first_in.at[1], f.w_down.at[2])

    def add(ref, value):
        ref[...] = (ref[...].astype(F32) + value.astype(F32)).astype(BF16)

    def block(g, yp, xb, k):
        return core_in[g].at[yp, 2 * k + xb]

    def grad_block(g, p, b):
        return grads[g][p, b]

    def down_core(yp, c):
        src = f.d_down.at[yp * 2 + 1 - core, pl.ds(2 * c, 2)]
        dst = core_in[0].at[yp, pl.ds(2 * c, 2)]
        return remote(src, dst, f.dn_ss.at[yp, c], f.dn_rs.at[yp, c], {"dp": sibling})

    def part_core(g, p):
        yp = p // 2
        if g == 1:
            src, dst = f.d_up.at[p], core_in[1].at[yp]
        else:
            src, dst = f.w_up.at[p], f.w_down.at[yp]
        return remote(src, dst, f.co_ss.at[g - 1, yp], f.co_rs.at[g - 1, yp], {"dp": sibling})

    def y_first(g, k):
        return z.y_first[g][k]

    def step_one(g, k, other):
        if y_first(g, k):
            src, to = block(g, 1 - y, other, k), {"dp": across}
        else:
            src, to = block(g, other, 1 - xx, k), {"seq": beside}
        dst = first_in[g].at[other * deep + k]
        return remote(src, dst, f.f_ss.at[g, other, k], f.f_rs.at[g, other, k], to)

    def step_two(g, k):
        if y_first(g, k):
            src, to = block(g, y, 1 - xx, k), {"seq": beside}
        else:
            src, to = block(g, 1 - y, xx, k), {"dp": across}
        return remote(src, f.second_in.at[g, k], f.n_ss.at[g, k], f.n_rs.at[g, k], to)

    def one_done(g, k, other):
        if y_first(g, k):
            own, far = block(g, y, other, k), xx != other
        else:
            own, far = block(g, other, xx, k), y != other
        step_one(g, k, other).wait_recv()
        add(own, first_in[g][other * deep + k])
        pl.when(far)(lambda: step_two(g, k).start())

    def step_three(g, k):
        return remote(
            block(g, y, xx, k), f.third_in.at[g, zz], f.t_ss.at[g, k], f.t_rs.at[g, zz],
            {"seq": 2 * k + xx},
        )

    def two_done(g, k):
        step_two(g, k).wait_recv()
        add(block(g, y, xx, k), f.second_in[g, k])

        @pl.when(zz != k)
        def _():
            step_three(g, k).start()

    def gather_copy(g, kind):
        src = across if kind == 2 else me
        to = {"dp": across if kind == 1 else sibling}
        ref = f.gat.at[g, src]
        return remote(ref, ref, f.w_ss.at[g, kind], f.w_rs.at[g, kind], to)

    def three_done(g):
        total = core_in[g][y, j].astype(F32)
        for k in range(1, deep):
            source = lax.rem(zz + k, deep)
            remote(
                block(g, y, xx, zz), f.third_in.at[g, source], f.t_ss.at[g, source],
                f.t_rs.at[g, source], {"seq": 2 * source + xx},
            ).wait_recv()
            total = total + f.third_in[g, source].astype(F32)
        f.gat[g, me] = total.astype(BF16)
        gather_copy(g, 1).start()
        gather_copy(g, 0).start()

    def gather_wait(g, kind):
        source = (sibling, across, across + sibling - me)[kind]
        ref = f.gat.at[g, source]
        to = {"dp": across if kind == 1 else sibling}
        remote(ref, ref, f.w_ss.at[g, kind], f.w_rs.at[g, kind], to).wait_recv()

    def gather_done(g):
        gather_wait(g, 1)
        gather_copy(g, 2).start()

    def part_done(g, p):
        yp = p // 2
        part_core(g, p).wait_recv()

        def body(b, carry):
            add(core_in[g].at[yp, b], grad_block(g, p, b))
            return carry

        lax.fori_loop(0, z.seq, body, 0)
        for k in range(deep):
            if y_first(g, k):

                @pl.when(yp != y)
                def _():
                    step_one(g, k, 1 - xx).start()
                    step_one(g, k, xx).start()
            else:
                step_one(g, k, yp).start()

    def down_done(c):
        for yp in range(2):
            down_core(yp, c).wait_recv()
            for xb in range(2):
                add(block(0, yp, xb, c), f.d_down[yp * 2 + core, 2 * c + xb])
            if y_first(0, c):

                @pl.when(yp != y)
                def _():
                    step_one(0, c, 1 - xx).start()
                    step_one(0, c, xx).start()
            else:
                step_one(0, c, yp).start()

    def core_done(c):
        down_done(c)
        pl.when(c % 2 == core)(lambda: part_done(1, c))

    def vec_copy(t, to):
        return remote(f.vec_buf.at[min(t, 2)], f.vec_got.at[t], f.v_ss.at[t], f.v_rs.at[t], to)

    def vec_step(t):
        if t == 1:
            vec_copy(0, {"dp": sibling}).wait()
            f.vec_buf[1] = f.vec_buf[0] + f.vec_got[0]
            vec_copy(1, {"dp": across}).start()
            return
        if t == 2:
            vec_copy(1, {"dp": across}).wait()
            f.vec_buf[2] = f.vec_buf[1] + f.vec_got[1]
        total = f.vec_buf[2]
        for d in range(1, z.seq):
            copy = vec_copy(1 + d, {"seq": lax.rem(j + d, z.seq)})
            if t == 2:
                copy.start()
            else:
                copy.wait()
                total = total + f.vec_got[1 + d]
        if t == 3:
            f.vec_ref[...] = total

    def part_step(which):
        for p in range(2):
            pl.when(core == p)(lambda p=p: part_done(2, p + which))

    steps = {
        "one": one_done, "two": two_done, "three": three_done, "gather": gather_done,
        "vec": vec_step, "part": part_step,
    }

    def run(tasks):
        for name, *numbers in tasks:
            steps[name](*numbers)

    def serve(i, table):
        if z.reduce:
            for at, tasks in enumerate(table):
                if tasks:
                    pl.when(i == at)(functools.partial(run, tasks))

    for copy in loads[3:]:
        copy.wait()

    def first(t, carry):
        rows = part_rows(t)
        middle = f.xrow[t].astype(F32) + tn(f.att_t[:, rows], f.w_o[...])
        f.acc[rows, :] = middle
        f.gm[rows, :] = middle
        unit, _ = norm_parts(middle)
        normed = (unit * gain_ffn + bias_ffn).astype(BF16)
        f.low[rows, :] = normed
        f.low_t[:, rows] = normed.T
        f.acc_n[rows, :] = jnp.zeros((part, width), F32)
        return carry

    lax.fori_loop(0, z.rows, first, 0)
    for slot in range(z.rows):
        rows_landed(z, j, h, f.c_in, f.crow, f.c_send, f.c_recv, slot)
    rows_sent(z, j, h, f.c_in, f.crow, f.c_send, f.c_recv)
    halves = z.rows // 2

    def chunk(c, carry):
        w_up, w_down = f.w_up[c].reshape(width, width), f.w_down[c].reshape(width, width)
        for t in range(2):
            rows = slice(t * halves * part, (t + 1) * halves * part)
            own = slice(t * halves, (t + 1) * halves)
            grad_out = f.crow[own].reshape(halves * part, width)
            u = nn(f.low[rows, :], w_up)
            tanh = jnp.tanh(GELU_A * (u + GELU_B * (u * u * u)))
            cdf = 0.5 * (1.0 + tanh)
            f.act[own] = (u * cdf).astype(BF16).reshape(halves, part, width)
            slope = cdf + (0.5 * GELU_A) * u * (1.0 - tanh * tanh) * (1.0 + (3.0 * GELU_B) * (u * u))
            grad = nt(grad_out, w_down)
            f.gp[own] = (grad * slope).astype(BF16).reshape(halves, part, width)
            f.acc[rows, :] += nn(f.act[own].reshape(halves * part, width), w_down)
            f.acc_n[rows, :] += nt(f.gp[own].reshape(halves * part, width), w_up)
            if z.reduce and t == 0 and c:
                core_done(c - 1)
        down = tn(
            f.act[...].reshape(z.tokens, width), f.crow[...].reshape(z.tokens, width)
        ).astype(BF16)
        if z.fast:
            for b in range(2):
                for p in range(z.dp):
                    at = (b * z.dp + p) * z.block
                    f.d_down[p, 2 * c + b] = down[at : at + z.block]
        else:
            f.d_down[pl.ds(pl.multiple_of(c * width, width), width), :] = down
        if z.reduce:
            for yp in range(2):
                down_core(yp, c).start()
        up = nn(f.low_t[...], f.gp[...].reshape(z.tokens, width)).astype(BF16)
        f.d_up[c] = up.reshape(f.d_up.shape[1:])
        if z.reduce:
            pl.when(c % 2 != core)(lambda: part_core(1, c).start())
        return carry

    if z.reduce:
        for c in range(chunks):
            chunk(c, 0)
    else:
        lax.fori_loop(0, chunks, chunk, 0)

    def ffn_back(t, carry):
        rows = part_rows(t)
        f.act[t] = f.acc[rows, :].astype(BF16)
        unit, inverse = norm_parts(f.gm[rows, :])
        grad = f.acc_n[rows, :]
        grad_middle = f.crow[t].astype(F32) + norm_back(grad, unit, inverse, gain_ffn)
        f.gm[rows, :] = grad_middle
        f.low[rows, :] = grad_middle.astype(BF16)
        return (
            carry[0] + jnp.sum(grad * unit, axis=0, keepdims=True),
            carry[1] + jnp.sum(grad, axis=0, keepdims=True),
        )

    zero = jnp.zeros((1, width), F32)
    sums_ffn = lax.fori_loop(0, z.rows, ffn_back, (zero, zero))
    rows_out(z, j, r, h, f.act, f.out_ref, f.o_send, f.o_recv)
    f.ga_t[...] = nt(f.w_o[...], f.low[...]).astype(BF16)

    if z.reduce:
        core_done(chunks - 1)

    def gather_grads(i, carry):
        blocks = []
        for a in range(2):
            n = 2 * i + a
            masked = jnp.concatenate([f.ga_t[head_rows(n), :]] * z.docs, axis=0) * f.body[...]
            blocks.append(nt(masked, member_of(n)))
            f.u_s[n] = blocks[-1]
        for d, packed in enumerate(border(blocks)):
            f.g_send[i, d] = packed
        for step in others:
            grad_copy(i, step).start()
        serve(i, z.tasks[0])
        return carry

    lax.fori_loop(0, pairs, gather_grads, 0)
    f.w_up[3] = nn(f.att_t[...], f.low[...]).astype(BF16).reshape(z.square)
    if z.reduce:
        pl.when(core == 0)(lambda: part_core(2, 3).start())

    def attend_back(i, carry):
        serve(i, z.tasks[1])
        got = []
        for step in others:
            grad_copy(i, step).wait()
            got.append([unpack(f.g_recv[step - 1, i, d]) for d in range(z.sent_docs)])
        cents = []
        for a in range(2):
            n = 2 * i + a
            result, factor = f.res_t[n], f.rfac[n]
            lows, deltas = [], []
            for s in range(z.docs):
                grad = f.u_s[n, s * z.head : (s + 1) * z.head]
                joined = grad
                for other in got:
                    piece = other[0 if z.mates == 2 else s]
                    joined = joined + piece[a * z.head : (a + 1) * z.head]
                if z.mates == 2:
                    joined = jnp.where(jnp.logical_and(spans, mine == s), joined, grad)
                scaled = joined * factor[s : s + 1]
                lows.append(scaled.astype(BF16))
                piece = doc_rows(result, s).astype(F32)
                deltas.append(-jnp.sum(scaled * piece, axis=0, keepdims=True))
            delta = jnp.concatenate(deltas, axis=0)
            high = delta.astype(BF16).astype(F32)
            small = jnp.concatenate(
                [high, delta - high, jnp.zeros((16 - 2 * z.docs, PAD), F32)], axis=0
            ).astype(BF16)
            low = jnp.concatenate(lows, axis=0)
            diff = tn(
                jnp.concatenate([low, small], axis=0),
                jnp.concatenate([masked_values(n), tail], axis=0),
            )
            weights = f.wts[n]
            raw = (0.125 * (weights.astype(F32) * diff)).astype(BF16)
            f.gk_t[head_rows(n), :] = nn(f.cent_t[n], raw).astype(BF16)
            f.gv_t[head_rows(n), :] = joined_masks(z, nn(low, weights), seg).astype(BF16)
            cents.append(nt(f.k_t[head_rows(n), :], raw))
        pair = jnp.concatenate(cents, axis=0)
        f.c_f[i] = pair
        f.c_s[i] = pack(pair)
        for step in others:
            cent_copy(i, step).start()
        return carry

    lax.fori_loop(0, pairs, attend_back, 0)

    def weight_grad(p, g_ref):
        f.w_up[p] = nt(f.n_t[...], g_ref[...]).astype(BF16).reshape(z.square)
        if z.reduce:
            pl.when(p % 2 != core)(lambda: part_core(2, p).start())

    weight_grad(1, f.gk_t)
    weight_grad(2, f.gv_t)

    def query_back(i, carry):
        total = f.c_f[i]
        for step in others:
            cent_copy(i, step).wait()
            total = total + unpack(f.c_got[step - 1, i])
        for a in range(2):
            n = 2 * i + a
            low = (total[a * z.head : (a + 1) * z.head] / f.cnts[pl.ds(n, 1), :]).astype(BF16)
            f.q_t[head_rows(n), :] = nn(low, member_of(n)).astype(BF16)
        serve(i, z.tasks[2])
        return carry

    lax.fori_loop(0, pairs, query_back, 0)
    weight_grad(0, f.q_t)

    if z.reduce:
        run(z.tasks[3])

    total = (
        nn(f.w_qkv[0], f.q_t[...]) + nn(f.w_qkv[1], f.gk_t[...]) + nn(f.w_qkv[2], f.gv_t[...])
    )
    f.acc[...] = total.T

    def attn_back(t, carry):
        rows = part_rows(t)
        unit, inverse = norm_parts(f.xrow[t].astype(F32))
        grad = f.acc[rows, :]
        f.gp[t] = (f.gm[rows, :] + norm_back(grad, unit, inverse, gain_attn)).astype(BF16)
        return (
            carry[0] + jnp.sum(grad * unit, axis=0, keepdims=True),
            carry[1] + jnp.sum(grad, axis=0, keepdims=True),
        )

    sums_attn = lax.fori_loop(0, z.rows, attn_back, (zero, zero))
    rows_out(z, j, r, h, f.gp, f.gx_ref, f.y_send, f.y_recv)
    vectors = jnp.concatenate([*sums_attn, *sums_ffn, jnp.zeros((4, width), F32)], axis=0)

    if z.reduce:
        f.vec_buf[0] = vectors
        vec_copy(0, {"dp": sibling}).start()
        run(z.tasks[4])
        for g in range(3):
            gather_wait(g, 0)
            gather_wait(g, 2)
            for kind in range(3):
                gather_copy(g, kind).wait_send()
            for k in range(deep):
                for other in range(2):
                    step_one(g, k, other).wait_send()
                step_two(g, k).wait_send()

                @pl.when(zz != k)
                def _():
                    step_three(g, k).wait_send()

        for yp in range(2):
            for c in range(chunks):
                down_core(yp, c).wait_send()
            for g in (1, 2):
                part_core(g, yp * 2 + 1 - core).wait_send()
    else:
        f.vec_ref[...] = vectors
        if not z.fast:
            copy = pltpu.make_async_copy(f.w_up, f.d_qkvo, f.load.at[0])
            copy.start()
            copy.wait()

    for slot in range(z.rows):
        rows_landed(z, j, h, f.act, f.out_ref, f.o_send, f.o_recv, slot)
        rows_landed(z, j, h, f.gp, f.gx_ref, f.y_send, f.y_recv, slot)
    rows_sent(z, j, h, f.act, f.out_ref, f.o_send, f.o_recv)
    rows_sent(z, j, h, f.gp, f.gx_ref, f.y_send, f.y_recv)


def local(
    mesh_shape,
    inputs, cotangent, lengths, clusters, gain_attn, bias_attn, w_query, w_key, w_value, w_out,
    gain_ffn, bias_ffn, w_up, w_down,
):
    z = Plan(mesh_shape, inputs, clusters, lengths, w_up)
    width, tokens, heads, docs = z.width, z.tokens, z.heads, z.docs
    others, stack, chunks = z.mates - 1, z.docs * z.head, z.hidden // z.width
    anywhere = pl.BlockSpec(memory_space=pl.ANY)
    vmem = pl.BlockSpec(memory_space=pltpu.VMEM)
    smem = pl.BlockSpec(memory_space=pltpu.SMEM)
    dma = pltpu.SemaphoreType.DMA
    shape = jax.ShapeDtypeStruct
    turned = jnp.transpose(clusters, (2, 0, 1))
    rows = (z.rows, z.part, width)

    ins = [
        ("x_in", inputs, anywhere), ("c_in", cotangent, anywhere), ("clu_in", turned, anywhere),
        ("lengths", lengths, smem), ("gain_attn", gain_attn, vmem), ("bias_attn", bias_attn, vmem),
        ("gain_ffn", gain_ffn, vmem), ("bias_ffn", bias_ffn, vmem),
        ("wq_in", w_query, anywhere), ("wk_in", w_key, anywhere), ("wv_in", w_value, anywhere),
        ("wo_in", w_out, anywhere), ("up_in", w_up.reshape(z.square[:-1] + (z.hidden,)), anywhere),
        ("down_in", w_down.reshape((chunks,) + z.square), anywhere),
    ]
    outs = [
        ("out_ref", shape(rows, BF16), anywhere), ("gx_ref", shape(rows, BF16), anywhere),
        ("vec_ref", shape((8, width), F32), vmem),
    ]
    pairs, packed = heads // 2, (z.sent_rows, PAD)
    scratch = [
        ("w_qkv", (3, width, width), BF16), ("w_o", (width, width), BF16),
        ("w_up", (chunks,) + z.square, BF16), ("w_down", (chunks,) + z.square, BF16),
        ("xrow", rows, BF16), ("crow", rows, BF16),
        ("clu_got", (z.rows, heads, z.rows, z.part), jnp.int32), ("clus", (heads, tokens), jnp.int32),
        ("n_t", (width, tokens), BF16), ("q_t", (width, tokens), BF16),
        ("k_t", (width, tokens), BF16), ("v_t", (width, tokens), BF16),
        ("att_t", (width, tokens), BF16), ("wts", (heads, PAD, tokens), BF16),
        ("cent_t", (heads, z.head, PAD), BF16), ("cnts", (z.count_rows, PAD), F32), ("cnt_out", (z.count_rows, PAD), F32),
        ("cnt_in", (others, z.count_rows, PAD), F32), ("dens", (heads, 8, PAD), F32),
        ("res_t", (heads, stack, PAD), BF16), ("rfac", (heads, 8, PAD), F32),
        ("u_s", (heads, stack, PAD), F32), ("body", (stack, tokens), BF16),
        ("sums_f", (pairs, PAD, PAD), F32),
        ("sums", (pairs,) + packed, BF16), ("sums_in", (others, pairs) + packed, BF16),
        ("big", (pairs, z.sent_docs) + packed, BF16),
        ("big_in", (others, pairs, z.sent_docs) + packed, BF16),
        ("small", (pairs, z.small_rows, PAD), F32), ("small_in", (others, pairs, z.small_rows, PAD), F32),
        ("g_send", (pairs, z.sent_docs) + packed, BF16),
        ("g_recv", (others, pairs, z.sent_docs) + packed, BF16),
        ("c_f", (pairs, PAD, PAD), F32), ("c_s", (pairs,) + packed, BF16),
        ("c_got", (others, pairs) + packed, BF16),
        ("low", (tokens, width), BF16), ("low_t", (width, tokens), BF16),
        ("act", rows, BF16), ("gp", rows, BF16),
        ("acc", (tokens, width), F32), ("acc_n", (tokens, width), F32), ("gm", (tokens, width), F32),
        ("ga_t", (width, tokens), BF16), ("gk_t", (width, tokens), BF16), ("gv_t", (width, tokens), BF16),
    ]
    sems = [("load", (4 + 2 * chunks,))]
    for n in ("i", "x", "c", "o", "y"):
        sems += [(n + "_send", (z.rows,)), (n + "_recv", (z.rows,))]
    for n in ("a", "b", "s", "g", "q"):
        sems += [(n + "_ss", (others, pairs)), (n + "_rs", (others, pairs))]
    sems += [("k_ss", (others,)), ("k_rs", (others,))]
    if z.fast:
        piece = (z.block, width)
        deep = z.seq // 2
        outs.append(("gat", shape((3, z.dp) + piece, BF16), vmem))
        scratch += [
            ("d_down", (z.dp, z.seq) + piece, BF16), ("d_up", (z.dp, z.seq) + piece, BF16),
            ("core_in", (2, 2, z.seq) + piece, BF16), ("first_in", (2, z.seq) + piece, BF16),
            ("second_in", (3, deep) + piece, BF16), ("third_in", (3, deep) + piece, BF16),
            ("vec_buf", (3, 8, width), F32), ("vec_got", (z.seq + 1, 8, width), F32),
        ]
        sems += [
            ("dn_ss", (2, chunks)), ("dn_rs", (2, chunks)), ("co_ss", (2, 2)), ("co_rs", (2, 2)),
            ("f_ss", (3, 2, deep)), ("f_rs", (3, 2, deep)), ("n_ss", (3, deep)), ("n_rs", (3, deep)),
            ("t_ss", (3, deep)), ("t_rs", (3, deep)), ("w_ss", (3, 3)), ("w_rs", (3, 3)),
            ("v_ss", (z.seq + 1,)), ("v_rs", (z.seq + 1,)),
        ]
    else:
        outs += [
            ("d_qkvo", shape((4, width, width), BF16), anywhere),
            ("d_up", shape((chunks, width, width), BF16), vmem),
            ("d_down", shape((z.hidden, width), BF16), vmem),
        ]
    names = [n for n, _, _ in ins + outs + scratch] + [n for n, _ in sems]
    results = pl.pallas_call(
        functools.partial(block_kernel, z, names),
        out_shape=[s for _, s, _ in outs],
        in_specs=[s for _, _, s in ins],
        out_specs=[s for _, _, s in outs],
        scratch_shapes=[pltpu.VMEM(s, t) for _, s, t in scratch] + [dma(s) for _, s in sems],
        compiler_params=pltpu.CompilerParams(
            collective_id=0, has_side_effects=True, vmem_limit_bytes=VMEM_LIMIT
        ),
    )(*[v for _, v, _ in ins])

    out_back, grad_back, vectors = results[:3]
    if z.fast:
        gat = results[3].astype(F32)
        g_down = gat[0].reshape(-1, width)
        g_up = jnp.transpose(gat[1], (1, 0, 2)).reshape(z.block, -1)
        g_qkvo = gat[2]
        own = lax.dynamic_slice_in_dim(vectors, lax.axis_index("seq") * z.block, z.block, 1)
    else:

        def share(v, dim):
            v = lax.psum_scatter(v.astype(F32), "seq", scatter_dimension=dim, tiled=True)
            return lax.psum(v, "dp")

        g_up = share(jnp.transpose(results[4], (1, 0, 2)).reshape(width, z.hidden), 0)
        g_qkvo, g_down, own = share(results[3], 1), share(results[5], 0), share(vectors, 1)
    return (
        out_back.astype(F32), grad_back.astype(F32), own[0], own[1],
        g_qkvo[0], g_qkvo[1], g_qkvo[2], g_qkvo[3], own[2], own[3], g_up, g_down,
    )


def solution(mesh):
    spread = P("dp", "seq", None)
    return jax.shard_map(
        functools.partial(local, dict(mesh.shape)),
        mesh=mesh,
        in_specs=(spread, spread, P("dp", None), spread) + (P(),) * 10,
        out_specs=(spread, spread, P("seq"), P("seq")) + (P("seq", None),) * 4
        + (P("seq"), P("seq"), P("seq", None), P("seq", None)),
        check_vma=False,
    )
```

```python
import functools

import jax
import jax.numpy as jnp
from jax import lax
from jax.experimental import pallas as pl
from jax.experimental.pallas import tpu as pltpu
from jax.sharding import PartitionSpec as P

CLUSTERS = 100
PAD = 128
EPSILON = 1e-05
GELU_A = 0.7978845608028654
GELU_B = 0.044715
MESH = pl.DeviceIdType.MESH
YF = ((True, False, True, True), (False, True, False, True), (True, True, True, False))
F32 = jnp.float32
BF16 = jnp.bfloat16
VMEM_LIMIT = 63 * 2**20


def schedule(order):
    def both(g, *ks):
        return [("one", g, k, o) for k in ks for o in range(2)]

    def two(g, *ks):
        return [("two", g, k) for k in ks]

    def side(g, o, *ks):
        return [("one", g, k, o) for k in ks]

    a, b, c, d = order
    forward = {a: [], b: [("down", a)], c: [("down", b)], d: [("down", c)]}
    mixed = [step for k in order for step in two(1, k) + both(2, k)]
    return (
        [forward[k] for k in range(4)],
        ([("down", d)], [], [("up", 0)] + both(0, a), [("up", 1)] + both(0, b)),
        [("up", 2)] + both(0, c),
        ((), (), (), (), (), [("up", 3)]),
        ((), (), (), (), (), both(0, d)),
        ((),) * 6,
        both(1, *order),
        [("part", 3), ("part", 1), ("part", 2), ("part", 0), ("vec", 1)] + two(0, *order) + mixed + [("vec", 2)] + two(2, *order)
        + [("three", 0), ("gather", 0), ("three", 1), ("gather", 1), ("vec", 3), ("store", 0), ("store", 1)]
        + [("three", 2), ("gather", 2), ("store", 2)],
        [],
        [],
    )


class Plan:
    def __init__(self, mesh_shape, inputs, clusters, lengths, w_up):
        self.seq, self.dp = mesh_shape["seq"], mesh_shape["dp"]
        self.rows, self.part, self.width = inputs.shape
        self.heads, self.docs, self.hidden = clusters.shape[2], lengths.shape[1], w_up.shape[1]
        self.head = self.width // self.heads
        self.tokens = self.rows * self.part
        self.mates = self.seq // self.rows
        self.sent_docs = 1 if self.mates == 2 else self.docs
        self.block = self.width // self.seq
        self.fast = (
            self.dp == 4 and self.seq == 8 and self.block % 16 == 0 and self.hidden == 4 * self.width
        )
        self.reduce = self.fast
        self.sent_rows = -(-CLUSTERS // 16) * 16
        self.small_rows = 8 if self.mates == 2 else 16
        self.count_rows = -(-self.heads // 8) * 8
        self.order = (0, 3, 1, 2)
        self.tasks = schedule(self.order)
        self.square = (self.seq, self.block, self.width) if self.fast else (self.width, self.width)
        self.y_first = [[w[self.order.index(k)] for k in range(4)] for w in YF]

    def place(self, j):
        return lax.rem(j, self.rows), j // self.rows

    def owner(self, r, h):
        return h * self.rows + r


def nn(a, b):
    return lax.dot_general(a, b, (((1,), (0,)), ((), ())), preferred_element_type=F32)


def nt(a, b):
    return lax.dot_general(a, b, (((1,), (1,)), ((), ())), preferred_element_type=F32)


def tn(a, b):
    return lax.dot_general(a, b, (((0,), (0,)), ((), ())), preferred_element_type=F32)


def remote(src, dst, send, recv, to):
    return pltpu.make_async_remote_copy(
        src_ref=src, dst_ref=dst, send_sem=send, recv_sem=recv, device_id=to, device_id_type=MESH
    )


def one_hot(row):
    ids = lax.broadcasted_iota(jnp.int32, (PAD, row.shape[1]), 0)
    return jnp.where(ids == row, 1.0, 0.0).astype(BF16)


def doc_masks(z, r, h, len_ref):
    pos = h * z.tokens + lax.broadcasted_iota(jnp.int32, (1, z.tokens), 1)
    seg = jnp.zeros((1, z.tokens), jnp.int32)
    end, ends = jnp.int32(0), []
    for s in range(z.docs):
        end = end + len_ref[r, s]
        ends.append(end)
        seg = seg + (pos >= end).astype(jnp.int32)
    last = sum((z.tokens - 1 >= e).astype(jnp.int32) for e in ends)
    first = sum((z.tokens >= e).astype(jnp.int32) for e in ends)
    spans = last == first
    mine = jnp.where(h == 0, last, first)
    return seg, spans, mine


def stacked_masks(z, seg):
    ids = lax.broadcasted_iota(jnp.int32, (z.docs * z.head, z.tokens), 0)
    body = jnp.where(ids // z.head == seg, 1.0, 0.0).astype(BF16)
    low = lax.broadcasted_iota(jnp.int32, (16, z.tokens), 0)
    tail = jnp.where((low % z.docs == seg) & (low < 2 * z.docs), 1.0, 0.0).astype(BF16)
    return body, tail


def pick_doc(z, blocks, mine):
    out = blocks[0]
    for s in range(1, z.docs):
        out = jnp.where(mine == s, blocks[s], out)
    return out


def mate_id(z, r, h, step):
    return {"seq": z.owner(r, lax.rem(h + step, z.mates))}


def rows_out(z, j, r, h, src, dst, send, recv):
    for row in range(z.rows):
        to = z.owner(row, h)

        @pl.when(to != j)
        def _():
            remote(src.at[row], dst.at[r], send.at[row], recv.at[r], {"seq": to}).start()

        @pl.when(to == j)
        def _():
            pltpu.make_async_copy(src.at[row], dst.at[r], recv.at[r]).start()


def rows_landed(z, j, h, src, dst, send, recv, slot):
    source = z.owner(slot, h)

    @pl.when(source == j)
    def _():
        pltpu.make_async_copy(src.at[0], dst.at[slot], recv.at[slot]).wait()

    @pl.when(source != j)
    def _():
        remote(src.at[0], dst.at[slot], send.at[0], recv.at[slot], {"seq": source}).wait_recv()


def rows_sent(z, j, h, src, dst, send, recv):
    for row in range(z.rows):
        to = z.owner(row, h)

        @pl.when(to != j)
        def _():
            remote(src.at[row], dst.at[0], send.at[row], recv.at[0], {"seq": to}).wait_send()


def norm_parts(values):
    average = jnp.mean(values, axis=-1, keepdims=True)
    centered = values - average
    inverse = lax.rsqrt(jnp.mean(centered * centered, axis=-1, keepdims=True) + EPSILON)
    return centered * inverse, inverse


def norm_back(grad, unit, inverse, gain):
    scaled = grad * gain
    inner = (
        scaled
        - jnp.mean(scaled, axis=-1, keepdims=True)
        - unit * jnp.mean(scaled * unit, axis=-1, keepdims=True)
    )
    return inner * inverse


def joined_masks(z, blocks, seg):
    out = blocks[: z.head]
    for s in range(1, z.docs):
        out = jnp.where(seg == s, blocks[s * z.head : (s + 1) * z.head], out)
    return out


class Refs:
    def __init__(self, names, values):
        self.__dict__.update(zip(names, values, strict=True))


def block_kernel(z, names, *values):
    f = Refs(names, values)
    j = lax.axis_index("seq")
    me = lax.axis_index("dp")
    r, h = z.place(j)
    width, part = z.width, z.part

    barrier = pltpu.get_barrier_semaphore()
    for d in range(1, z.seq):
        pl.semaphore_signal(
            barrier, 1, device_id={"seq": lax.rem(j + d, z.seq)}, device_id_type=MESH
        )
    greeted = z.seq - 1
    if z.reduce:
        for d in range(1, z.dp):
            pl.semaphore_signal(
                barrier, 1, device_id={"dp": lax.rem(me + d, z.dp)}, device_id_type=MESH
            )
        greeted += z.dp - 1

    loads = [
        pltpu.make_async_copy(ref, f.w_qkv.at[p], f.load.at[p])
        for p, ref in enumerate((f.wq_in, f.wk_in, f.wv_in))
    ]
    loads.append(pltpu.make_async_copy(f.wo_in, f.w_o, f.load.at[3]))
    chunks = z.hidden // width
    for c in range(chunks):
        loads.append(
            pltpu.make_async_copy(
                f.up_in.at[(slice(None),) * (len(z.square) - 1) + (pl.ds(c * width, width),)],
                f.w_up.at[c],
                f.load.at[4 + c],
            )
        )
        loads.append(
            pltpu.make_async_copy(f.down_in.at[c], f.w_down.at[c], f.load.at[4 + chunks + c])
        )
    for copy in loads[:3]:
        copy.start()

    seg, spans, mine = doc_masks(z, r, h, f.lengths)
    body_value, tail = stacked_masks(z, seg)
    f.body[...] = body_value
    gain_attn, bias_attn = f.gain_attn[...].reshape(1, width), f.bias_attn[...].reshape(1, width)
    gain_ffn, bias_ffn = f.gain_ffn[...].reshape(1, width), f.bias_ffn[...].reshape(1, width)
    pl.semaphore_wait(barrier, greeted)

    def clu_copy(step):
        to = {"seq": z.owner(lax.rem(r + step, z.rows), h)}
        return remote(f.clu_in, f.clu_got.at[step], f.i_send.at[step], f.i_recv.at[step], to)

    own_clu = pltpu.make_async_copy(f.clu_in, f.clu_got.at[0], f.i_recv.at[0])
    own_clu.start()
    for step in range(1, z.rows):
        clu_copy(step).start()
    rows_out(z, j, r, h, f.x_in, f.xrow, f.x_send, f.x_recv)
    for copy in loads[3:]:
        copy.start()

    def part_rows(t):
        return pl.ds(pl.multiple_of(t * part, part), part)

    def head_rows(i):
        return pl.ds(pl.multiple_of(i * z.head, z.head), z.head)

    own_clu.wait()
    for step in range(z.rows):
        if step:
            clu_copy(step).wait()
        slot = lax.rem(r + z.rows - step, z.rows)
        numbers = f.clu_got[step, :, pl.ds(r, 1), :].reshape(z.heads, part)
        f.clus[:, part_rows(slot)] = numbers

    def mate_copy(src, dst, send, recv, i, step):
        to = {"seq": z.owner(r, lax.rem(h + step, z.mates))}
        return remote(src.at[i], dst.at[step - 1, i], send.at[step - 1, i], recv.at[step - 1, i], to)

    def sum_copy(i, step):
        return mate_copy(f.sums, f.sums_in, f.a_ss, f.a_rs, i, step)

    def result_copies(i, step):
        return (
            mate_copy(f.big, f.big_in, f.b_ss, f.b_rs, i, step),
            mate_copy(f.small, f.small_in, f.s_ss, f.s_rs, i, step),
        )

    def grad_copy(i, step):
        return mate_copy(f.g_send, f.g_recv, f.g_ss, f.g_rs, i, step)

    def cent_copy(i, step):
        return mate_copy(f.c_s, f.c_got, f.q_ss, f.q_rs, i, step)

    others = range(1, z.mates)
    stack = z.docs * z.head
    pairs = z.heads // 2
    low_lanes = z.sent_rows

    def pack(pair):
        return pair.astype(BF16).T[:low_lanes]

    def unpack(packed):
        rest = jnp.zeros((PAD - low_lanes, PAD), BF16)
        return jnp.concatenate([packed, rest], axis=0).T.astype(F32)

    def member_of(i):
        return one_hot(f.clus[pl.ds(i, 1), :])

    ones = jnp.ones((8, z.tokens), BF16)
    f.cnt_out[...] = jnp.zeros_like(f.cnt_out)
    for i in range(z.heads):
        f.cnt_out[i : i + 1] = nt(ones, one_hot(f.clus[i : i + 1, :]))[:1]

    def count_copy(step):
        to = {"seq": z.owner(r, lax.rem(h + step, z.mates))}
        return remote(f.cnt_out, f.cnt_in.at[step - 1], f.k_ss.at[step - 1], f.k_rs.at[step - 1], to)

    for step in others:
        count_copy(step).start()
    for copy in loads[:3]:
        copy.wait()

    def project(slot, carry):
        rows_landed(z, j, h, f.x_in, f.xrow, f.x_send, f.x_recv, slot)
        unit, _ = norm_parts(f.xrow[slot].astype(F32))
        normed = (unit * gain_attn + bias_attn).astype(BF16)
        f.low[part_rows(slot), :] = normed
        f.n_t[:, part_rows(slot)] = normed.T
        f.q_t[:, part_rows(slot)] = nn(normed, f.w_qkv[0]).astype(BF16).T
        return carry

    lax.fori_loop(0, z.rows, project, 0)

    def cluster_sums(i, carry):
        pair = jnp.concatenate(
            [nt(f.q_t[head_rows(2 * i + a), :], member_of(2 * i + a)) for a in range(2)], axis=0
        )
        f.sums_f[i] = pair
        f.sums[i] = pack(pair)
        for step in others:
            sum_copy(i, step).start()
        return carry

    lax.fori_loop(0, pairs, cluster_sums, 0)
    rows_sent(z, j, h, f.x_in, f.xrow, f.x_send, f.x_recv)
    rows_out(z, j, r, h, f.c_in, f.crow, f.c_send, f.c_recv)
    counts = f.cnt_out[...]
    for step in others:
        count_copy(step).wait()
        counts = counts + f.cnt_in[step - 1]
    f.cnts[...] = jnp.maximum(counts, 1.0)

    def project_more(t, carry):
        normed = f.low[part_rows(t), :]
        f.k_t[:, part_rows(t)] = nn(normed, f.w_qkv[1]).astype(BF16).T
        f.v_t[:, part_rows(t)] = nn(normed, f.w_qkv[2]).astype(BF16).T
        return carry

    lax.fori_loop(0, z.rows, project_more, 0)

    def masked_values(i):
        return jnp.concatenate([f.v_t[head_rows(i), :]] * z.docs, axis=0) * f.body[...]

    def doc_rows(blocks, s):
        return blocks[s * z.head : (s + 1) * z.head]

    def border(blocks):
        if z.mates == 2:
            parts = [[doc_rows(b, s) for s in range(z.docs)] for b in blocks]
            return [pack(jnp.concatenate([pick_doc(z, p, mine) for p in parts], axis=0))]
        return [
            pack(jnp.concatenate([doc_rows(b, s) for b in blocks], axis=0)) for s in range(z.docs)
        ]

    def attend(i, carry):
        total = f.sums_f[i]
        for step in others:
            sum_copy(i, step).wait()
            total = total + unpack(f.sums_in[step - 1, i])
        blocks, small = [], []
        for a in range(2):
            n = 2 * i + a
            count = f.cnts[pl.ds(n, 1), :]
            cent = (total[a * z.head : (a + 1) * z.head] / count).astype(BF16)
            f.cent_t[n] = cent
            scores = tn(cent, f.k_t[head_rows(n), :]) * 0.125
            top = jnp.max(scores, axis=1, keepdims=True)
            weights = jnp.exp(scores - top).astype(BF16)
            f.wts[n] = weights
            both = nt(jnp.concatenate([masked_values(n), tail], axis=0), weights)
            f.u_s[n] = both[:stack]
            top_row = jnp.broadcast_to(top, (PAD, PAD)).T
            denoms = both[stack : stack + 4]
            f.dens[n] = jnp.concatenate([denoms, top_row[:4]], axis=0)
            blocks.append(both[:stack])
            if z.mates == 2:
                own = pick_doc(z, [denoms[s : s + 1] for s in range(z.docs)], mine)
                small += [jnp.broadcast_to(own, (2, PAD)), top_row[:2]]
            else:
                small += [denoms, top_row[:4]]
        f.small[i] = jnp.concatenate(small, axis=0)
        for d, packed in enumerate(border(blocks)):
            f.big[i, d] = packed
        for step in others:
            for copy in result_copies(i, step):
                copy.start()
        return carry

    lax.fori_loop(0, pairs, attend, 0)
    empty = [jnp.where(jnp.sum((seg == s).astype(F32)) > 0.5, 0.0, 1.0) for s in range(z.docs)]
    half_small = z.small_rows // 2

    def finish(i, carry):
        got = []
        for step in others:
            for copy in result_copies(i, step):
                copy.wait()
            got.append([unpack(f.big_in[step - 1, i, d]) for d in range(z.sent_docs)])
        for a in range(2):
            n = 2 * i + a
            own = f.dens[n]
            top, highest = own[4:5], own[4:5]
            sides = []
            for step in others:
                side = f.small_in[step - 1, i, a * half_small : (a + 1) * half_small]
                sides.append((side, side[half_small // 2 : half_small // 2 + 1]))
                highest = jnp.maximum(highest, sides[-1][1])
            scale = jnp.exp(top - highest)
            scaled, factors = [], []
            for s in range(z.docs):
                piece = f.u_s[n, s * z.head : (s + 1) * z.head]
                denom = own[s : s + 1]
                joined, joined_denom = piece * scale, denom * scale
                d = 0 if z.mates == 2 else s
                for other, (side, side_top) in zip(got, sides):
                    side_scale = jnp.exp(side_top - highest)
                    joined = joined + other[d][a * z.head : (a + 1) * z.head] * side_scale
                    joined_denom = joined_denom + side[d : d + 1] * side_scale
                here = jnp.logical_and(spans, mine == s) if z.mates == 2 else True
                joined = jnp.where(here, joined, piece)
                joined_denom = jnp.where(here, joined_denom, denom)
                factor = jnp.where(here, scale, jnp.ones_like(scale))
                joined_denom = joined_denom + jnp.where(joined_denom > 0.0, 0.0, empty[s])
                inverse = 1.0 / joined_denom
                scaled.append((joined * inverse).astype(BF16))
                factors.append(inverse * factor)
            result = jnp.concatenate(scaled, axis=0)
            f.res_t[n] = result
            f.rfac[n] = jnp.concatenate(factors + [jnp.zeros((8 - z.docs, PAD), F32)], axis=0)
            f.att_t[head_rows(n), :] = joined_masks(z, nn(result, member_of(n)), seg).astype(BF16)
        return carry

    lax.fori_loop(0, pairs, finish, 0)

    core, y = lax.rem(me, 2), me // 2
    xx, zz = lax.rem(j, 2), j // 2
    sibling, across = me + 1 - 2 * core, me + 2 - 4 * y
    beside = j + 1 - 2 * xx
    deep = z.seq // 2
    if z.reduce:
        grads = (f.d_down, f.d_up, f.w_up)
        core_in = (f.core_in.at[0], f.core_in.at[1], f.w_down.at[pl.ds(0, 2)])
        first_in = (f.first_in.at[0], f.first_in.at[1], f.w_down.at[2])

    def add(ref, value):
        ref[...] = ref[...] + value

    def block(g, yp, xb, k):
        return core_in[g].at[yp, 2 * k + xb]

    def grad_block(g, p, b):
        return grads[g][p, b]

    def down_core(yp, c):
        src = f.d_down.at[yp * 2 + 1 - core, pl.ds(2 * c, 2)]
        dst = core_in[0].at[yp, pl.ds(2 * c, 2)]
        return remote(src, dst, f.dn_ss.at[yp, c], f.dn_rs.at[yp, c], {"dp": sibling})

    def part_core(g, p):
        yp = p // 2
        if g == 1:
            src, dst = f.d_up.at[p], core_in[1].at[yp]
        else:
            src, dst = f.w_up.at[p], f.w_down.at[yp]
        return remote(src, dst, f.co_ss.at[g - 1, yp], f.co_rs.at[g - 1, yp], {"dp": sibling})

    def y_first(g, k):
        return z.y_first[g][k]

    def step_one(g, k, other):
        if y_first(g, k):
            src, to = block(g, 1 - y, other, k), {"dp": across}
        else:
            src, to = block(g, other, 1 - xx, k), {"seq": beside}
        dst = first_in[g].at[other * deep + k]
        return remote(src, dst, f.f_ss.at[g, other, k], f.f_rs.at[g, other, k], to)

    def step_two(g, k):
        if y_first(g, k):
            src, to = block(g, y, 1 - xx, k), {"seq": beside}
        else:
            src, to = block(g, 1 - y, xx, k), {"dp": across}
        return remote(src, f.second_in.at[g, k], f.n_ss.at[g, k], f.n_rs.at[g, k], to)

    def one_done(g, k, other):
        if y_first(g, k):
            own, far = block(g, y, other, k), xx != other
        else:
            own, far = block(g, other, xx, k), y != other
        step_one(g, k, other).wait_recv()
        add(own, first_in[g][other * deep + k])
        pl.when(far)(lambda: step_two(g, k).start())


    def step_three(g, k):
        return remote(
            block(g, y, xx, k), f.third_in.at[g, zz], f.t_ss.at[g, k], f.t_rs.at[g, zz],
            {"seq": 2 * k + xx},
        )

    def two_done(g, k):
        step_two(g, k).wait_recv()
        add(block(g, y, xx, k), f.second_in[g, k])

        @pl.when(zz != k)
        def _():
            step_three(g, k).start()

    def gather_copy(g, kind):
        src = across if kind == 2 else me
        to = {"dp": across if kind == 1 else sibling}
        ref = f.gat.at[g, src]
        return remote(ref, ref, f.w_ss.at[g, kind], f.w_rs.at[g, kind], to)

    def three_done(g):
        total = core_in[g][y, j].astype(F32)
        for k in range(1, deep):
            source = lax.rem(zz + k, deep)
            remote(
                block(g, y, xx, zz), f.third_in.at[g, source], f.t_ss.at[g, source],
                f.t_rs.at[g, source], {"seq": 2 * source + xx},
            ).wait_recv()
            total = total + f.third_in[g, source].astype(F32)
        f.gat[g, me] = total.astype(BF16)
        gather_copy(g, 1).start()
        gather_copy(g, 0).start()

    def gather_wait(g, kind):
        source = (sibling, across, across + sibling - me)[kind]
        ref = f.gat.at[g, source]
        to = {"dp": across if kind == 1 else sibling}
        remote(ref, ref, f.w_ss.at[g, kind], f.w_rs.at[g, kind], to).wait_recv()

    def gather_done(g):
        gather_wait(g, 1)
        gather_copy(g, 2).start()

    def store_copy(g):
        return pltpu.make_async_copy(f.gat.at[g], f.sum_ref.at[g], f.load.at[g])

    def store(g):
        gather_wait(g, 0)
        gather_wait(g, 2)
        store_copy(g).start()

    def part_done(g, p):
        yp = p // 2
        part_core(g, p).wait_recv()

        def body(b, carry):
            add(core_in[g].at[yp, b], grad_block(g, p, b))
            return carry

        lax.fori_loop(0, z.seq, body, 0)
        for k in z.order:
            if y_first(g, k):

                @pl.when(yp != y)
                def _():
                    step_one(g, k, 1 - xx).start()
                    step_one(g, k, xx).start()
            else:
                step_one(g, k, yp).start()

    def down_done(c):
        for yp in range(2):
            down_core(yp, c).wait_recv()
            for xb in range(2):
                add(block(0, yp, xb, c), f.d_down[yp * 2 + core, 2 * c + xb])
            if y_first(0, c):

                @pl.when(yp != y)
                def _():
                    step_one(0, c, 1 - xx).start()
                    step_one(0, c, xx).start()
            else:
                step_one(0, c, yp).start()

    def vec_copy(t, to):
        return remote(f.vec_buf.at[min(t, 2)], f.vec_got.at[t], f.v_ss.at[t], f.v_rs.at[t], to)

    def vec_step(t):
        if t == 1:
            vec_copy(0, {"dp": sibling}).wait()
            f.vec_buf[1] = f.vec_buf[0] + f.vec_got[0]
            vec_copy(1, {"dp": across}).start()
            return
        if t == 2:
            vec_copy(1, {"dp": across}).wait()
            f.vec_buf[2] = f.vec_buf[1] + f.vec_got[1]
        total = f.vec_buf[2]
        for d in range(1, z.seq):
            copy = vec_copy(1 + d, {"seq": lax.rem(j + d, z.seq)})
            if t == 2:
                copy.start()
            else:
                copy.wait()
                total = total + f.vec_got[1 + d]
        if t == 3:
            f.vec_ref[...] = total

    def part_step(p):
        pl.when(core == p % 2)(lambda: part_done(2, p))

    def up_step(c):
        pl.when(c % 2 == core)(lambda: part_done(1, c))

    steps = {
        "down": down_done, "store": store,
        "one": one_done, "two": two_done, "three": three_done, "gather": gather_done,
        "vec": vec_step, "part": part_step, "up": up_step,
    }

    def run(tasks):
        for name, *numbers in tasks:
            steps[name](*numbers)

    def serve(i, table):
        if z.reduce:
            for at, tasks in enumerate(table):
                if tasks:
                    pl.when(i == at)(functools.partial(run, tasks))

    for copy in loads[3:]:
        copy.wait()

    def first(t, carry):
        rows = part_rows(t)
        middle = f.xrow[t].astype(F32) + tn(f.att_t[:, rows], f.w_o[...])
        f.acc[rows, :] = middle
        f.gm[rows, :] = middle
        unit, _ = norm_parts(middle)
        normed = (unit * gain_ffn + bias_ffn).astype(BF16)
        f.low[rows, :] = normed
        f.low_t[:, rows] = normed.T
        f.acc_n[rows, :] = jnp.zeros((part, width), F32)
        return carry

    lax.fori_loop(0, z.rows, first, 0)
    for slot in range(z.rows):
        rows_landed(z, j, h, f.c_in, f.crow, f.c_send, f.c_recv, slot)
    rows_sent(z, j, h, f.c_in, f.crow, f.c_send, f.c_recv)
    halves = z.rows // 2

    halves_of = [slice(t * halves, (t + 1) * halves) for t in range(2)]
    rows_of = [slice(t * halves * part, (t + 1) * halves * part) for t in range(2)]

    def ffn_chunk(c, carry):
        w_up, w_down = f.w_up[c].reshape(width, width), f.w_down[c].reshape(width, width)
        for t in range(2):
            rows, own = rows_of[t], halves_of[t]
            u = nn(f.low[rows, :], w_up)
            tanh = jnp.tanh(GELU_A * (u + GELU_B * (u * u * u)))
            cdf = 0.5 * (1.0 + tanh)
            f.act[own] = (u * cdf).astype(BF16).reshape(halves, part, width)
            slope = cdf + (0.5 * GELU_A) * u * (1.0 - tanh * tanh) * (1.0 + (3.0 * GELU_B) * (u * u))
            f.slope[c, rows, :] = slope.astype(BF16)
            f.acc[rows, :] += nn(f.act[own].reshape(halves * part, width), w_down)
        down = tn(
            f.act[...].reshape(z.tokens, width), f.crow[...].reshape(z.tokens, width)
        ).astype(BF16)
        if z.fast:
            for b in range(2):
                for p in range(z.dp):
                    at = (b * z.dp + p) * z.block
                    f.d_down[p, 2 * c + b] = down[at : at + z.block]
        else:
            f.d_down[pl.ds(pl.multiple_of(c * width, width), width), :] = down
        if z.reduce:
            run(z.tasks[0][c])
            for yp in range(2):
                down_core(yp, c).start()
        return carry

    def back_chunk(c, carry):
        w_up, w_down = f.w_up[c].reshape(width, width), f.w_down[c].reshape(width, width)
        for t in range(2):
            rows, own = rows_of[t], halves_of[t]
            grad = nt(f.crow[own].reshape(halves * part, width), w_down)
            f.gp[own] = (grad * f.slope[c, rows, :].astype(F32)).astype(BF16).reshape(halves, part, width)
            f.acc_n[rows, :] += nt(f.gp[own].reshape(halves * part, width), w_up)
        up = nn(f.low_t[...], f.gp[...].reshape(z.tokens, width)).astype(BF16)
        f.d_up[c] = up.reshape(f.d_up.shape[1:])
        if z.reduce:
            run(z.tasks[1][c])
            pl.when(c % 2 != core)(lambda: part_core(1, c).start())
        return carry

    def each_chunk(body, order):
        if z.reduce:
            for c in order:
                body(c, 0)
        else:
            lax.fori_loop(0, chunks, body, 0)

    each_chunk(ffn_chunk, z.order)

    def ffn_out(t, carry):
        f.act[t] = f.acc[part_rows(t), :].astype(BF16)
        return carry

    lax.fori_loop(0, z.rows, ffn_out, 0)
    rows_out(z, j, r, h, f.act, f.out_ref, f.o_send, f.o_recv)
    each_chunk(back_chunk, range(chunks))

    def ffn_back(t, carry):
        rows = part_rows(t)
        unit, inverse = norm_parts(f.gm[rows, :])
        grad = f.acc_n[rows, :]
        grad_middle = f.crow[t].astype(F32) + norm_back(grad, unit, inverse, gain_ffn)
        f.gm[rows, :] = grad_middle
        f.low[rows, :] = grad_middle.astype(BF16)
        return (
            carry[0] + jnp.sum(grad * unit, axis=0, keepdims=True),
            carry[1] + jnp.sum(grad, axis=0, keepdims=True),
        )

    zero = jnp.zeros((1, width), F32)
    sums_ffn = lax.fori_loop(0, z.rows, ffn_back, (zero, zero))
    f.ga_t[...] = nt(f.w_o[...], f.low[...]).astype(BF16)

    if z.reduce:
        run(z.tasks[2])

    def gather_grads(i, carry):
        blocks = []
        for a in range(2):
            n = 2 * i + a
            masked = jnp.concatenate([f.ga_t[head_rows(n), :]] * z.docs, axis=0) * f.body[...]
            blocks.append(nt(masked, member_of(n)))
            f.u_s[n] = blocks[-1]
        for d, packed in enumerate(border(blocks)):
            f.g_send[i, d] = packed
        for step in others:
            grad_copy(i, step).start()
        serve(i, z.tasks[3])
        return carry

    lax.fori_loop(0, pairs, gather_grads, 0)
    f.w_up[3] = nn(f.att_t[...], f.low[...]).astype(BF16).reshape(z.square)
    if z.reduce:
        pl.when(core == 0)(lambda: part_core(2, 3).start())

    def attend_back(i, carry):
        serve(i, z.tasks[4])
        got = []
        for step in others:
            grad_copy(i, step).wait()
            got.append([unpack(f.g_recv[step - 1, i, d]) for d in range(z.sent_docs)])
        cents = []
        for a in range(2):
            n = 2 * i + a
            result, factor = f.res_t[n], f.rfac[n]
            lows, deltas = [], []
            for s in range(z.docs):
                grad = f.u_s[n, s * z.head : (s + 1) * z.head]
                joined = grad
                for other in got:
                    piece = other[0 if z.mates == 2 else s]
                    joined = joined + piece[a * z.head : (a + 1) * z.head]
                if z.mates == 2:
                    joined = jnp.where(jnp.logical_and(spans, mine == s), joined, grad)
                scaled = joined * factor[s : s + 1]
                lows.append(scaled.astype(BF16))
                piece = doc_rows(result, s).astype(F32)
                deltas.append(-jnp.sum(scaled * piece, axis=0, keepdims=True))
            delta = jnp.concatenate(deltas, axis=0)
            high = delta.astype(BF16).astype(F32)
            small = jnp.concatenate(
                [high, delta - high, jnp.zeros((16 - 2 * z.docs, PAD), F32)], axis=0
            ).astype(BF16)
            low = jnp.concatenate(lows, axis=0)
            diff = tn(
                jnp.concatenate([low, small], axis=0),
                jnp.concatenate([masked_values(n), tail], axis=0),
            )
            weights = f.wts[n]
            raw = (0.125 * (weights.astype(F32) * diff)).astype(BF16)
            f.gk_t[head_rows(n), :] = nn(f.cent_t[n], raw).astype(BF16)
            f.gv_t[head_rows(n), :] = joined_masks(z, nn(low, weights), seg).astype(BF16)
            cents.append(nt(f.k_t[head_rows(n), :], raw))
        pair = jnp.concatenate(cents, axis=0)
        f.c_f[i] = pair
        f.c_s[i] = pack(pair)
        for step in others:
            cent_copy(i, step).start()
        return carry

    lax.fori_loop(0, pairs, attend_back, 0)
    if z.reduce:
        run(z.tasks[8])

    def weight_grad(p, g_ref):
        f.w_up[p] = nt(f.n_t[...], g_ref[...]).astype(BF16).reshape(z.square)
        if z.reduce:
            pl.when(p % 2 != core)(lambda: part_core(2, p).start())

    weight_grad(1, f.gk_t)
    weight_grad(2, f.gv_t)

    def query_back(i, carry):
        total = f.c_f[i]
        for step in others:
            cent_copy(i, step).wait()
            total = total + unpack(f.c_got[step - 1, i])
        for a in range(2):
            n = 2 * i + a
            low = (total[a * z.head : (a + 1) * z.head] / f.cnts[pl.ds(n, 1), :]).astype(BF16)
            f.q_t[head_rows(n), :] = nn(low, member_of(n)).astype(BF16)
        serve(i, z.tasks[5])
        return carry

    lax.fori_loop(0, pairs, query_back, 0)
    if z.reduce:
        run(z.tasks[9])
    weight_grad(0, f.q_t)

    if z.reduce:
        run(z.tasks[6])

    total = (
        nn(f.w_qkv[0], f.q_t[...]) + nn(f.w_qkv[1], f.gk_t[...]) + nn(f.w_qkv[2], f.gv_t[...])
    )
    f.acc[...] = total.T

    def attn_back(t, carry):
        rows = part_rows(t)
        unit, inverse = norm_parts(f.xrow[t].astype(F32))
        grad = f.acc[rows, :]
        f.gp[t] = (f.gm[rows, :] + norm_back(grad, unit, inverse, gain_attn)).astype(BF16)
        return (
            carry[0] + jnp.sum(grad * unit, axis=0, keepdims=True),
            carry[1] + jnp.sum(grad, axis=0, keepdims=True),
        )

    sums_attn = lax.fori_loop(0, z.rows, attn_back, (zero, zero))
    rows_out(z, j, r, h, f.gp, f.gx_ref, f.y_send, f.y_recv)
    vectors = jnp.concatenate([*sums_attn, *sums_ffn, jnp.zeros((4, width), F32)], axis=0)

    if z.reduce:
        f.vec_buf[0] = vectors
        vec_copy(0, {"dp": sibling}).start()
        run(z.tasks[7])
        for g in range(3):
            store_copy(g).wait()
            for kind in range(3):
                gather_copy(g, kind).wait_send()
            for k in range(deep):
                for other in range(2):
                    step_one(g, k, other).wait_send()
                step_two(g, k).wait_send()
                pl.when(zz != k)(lambda k=k, g=g: step_three(g, k).wait_send())

        for yp in range(2):
            for c in range(chunks):
                down_core(yp, c).wait_send()
            for g in (1, 2):
                part_core(g, yp * 2 + 1 - core).wait_send()
    else:
        f.vec_ref[...] = vectors
        if not z.fast:
            copy = pltpu.make_async_copy(f.w_up, f.d_qkvo, f.load.at[0])
            copy.start()
            copy.wait()

    for slot in range(z.rows):
        rows_landed(z, j, h, f.act, f.out_ref, f.o_send, f.o_recv, slot)
        rows_landed(z, j, h, f.gp, f.gx_ref, f.y_send, f.y_recv, slot)
    rows_sent(z, j, h, f.act, f.out_ref, f.o_send, f.o_recv)
    rows_sent(z, j, h, f.gp, f.gx_ref, f.y_send, f.y_recv)


def publish_kernel(
    z, rows_a, rows_b, sums, vectors, out_a, out_b, w_q, w_k, w_v, w_o, w_up, w_down, own,
    rows_in, sums_in, rows_wide, sums_wide, r_in, r_out, s_in, s_out,
):
    pieces = []
    for a, (src, dst) in enumerate(((rows_a, out_a), (rows_b, out_b))):
        for t in range(z.rows):
            pieces.append(
                (src.at[t], rows_in.at[a, t], rows_wide.at[a, t], dst.at[t], r_in.at[a, t], r_out.at[a, t])
            )
    for g in range(3):
        for p in range(z.dp):
            if g == 0:
                dst = w_down.at[pl.ds(p * z.block, z.block), :]
            elif g == 1:
                dst = w_up.at[:, pl.ds(p * z.width, z.width)]
            else:
                dst = (w_q, w_k, w_v, w_o)[p]
            pieces.append(
                (sums.at[g, p], sums_in.at[g, p], sums_wide.at[g, p], dst, s_in.at[g, p], s_out.at[g, p])
            )
    for src, low, _, _, sem, _ in pieces:
        pltpu.make_async_copy(src, low, sem).start()
    for src, low, wide, dst, sem, done in pieces:
        pltpu.make_async_copy(src, low, sem).wait()
        wide[...] = low[...].astype(F32)
        pltpu.make_async_copy(wide, dst, done).start()
    first = lax.axis_index("seq") * z.block
    rows = lax.broadcasted_iota(jnp.int32, (z.width, PAD), 0)
    lanes = lax.broadcasted_iota(jnp.int32, (z.width, PAD), 1)
    pick = jnp.where(rows == lanes + first, 1.0, 0.0)
    own[...] = jnp.dot(
        vectors[...], pick, precision=lax.Precision.HIGHEST, preferred_element_type=F32
    )
    for _, _, wide, dst, _, done in pieces:
        pltpu.make_async_copy(wide, dst, done).wait()


def local(
    mesh_shape,
    inputs, cotangent, lengths, clusters, gain_attn, bias_attn, w_query, w_key, w_value, w_out,
    gain_ffn, bias_ffn, w_up, w_down,
):
    z = Plan(mesh_shape, inputs, clusters, lengths, w_up)
    width, tokens, heads, docs = z.width, z.tokens, z.heads, z.docs
    others, stack, chunks = z.mates - 1, z.docs * z.head, z.hidden // z.width
    anywhere = pl.BlockSpec(memory_space=pl.ANY)
    vmem = pl.BlockSpec(memory_space=pltpu.VMEM)
    smem = pl.BlockSpec(memory_space=pltpu.SMEM)
    dma = pltpu.SemaphoreType.DMA
    shape = jax.ShapeDtypeStruct
    turned = jnp.transpose(clusters, (2, 0, 1))
    rows = (z.rows, z.part, width)

    ins = [
        ("x_in", inputs, anywhere), ("c_in", cotangent, anywhere), ("clu_in", turned, anywhere),
        ("lengths", lengths, smem), ("gain_attn", gain_attn, vmem), ("bias_attn", bias_attn, vmem),
        ("gain_ffn", gain_ffn, vmem), ("bias_ffn", bias_ffn, vmem),
        ("wq_in", w_query, anywhere), ("wk_in", w_key, anywhere), ("wv_in", w_value, anywhere),
        ("wo_in", w_out, anywhere), ("up_in", w_up.reshape(z.square[:-1] + (z.hidden,)), anywhere),
        ("down_in", w_down.reshape((chunks,) + z.square), anywhere),
    ]
    outs = [
        ("out_ref", shape(rows, BF16), anywhere), ("gx_ref", shape(rows, BF16), anywhere),
        ("vec_ref", shape((8, width), F32), vmem),
    ]
    pairs, packed = heads // 2, (z.sent_rows, PAD)
    scratch = [
        ("w_qkv", (3, width, width), BF16), ("w_o", (width, width), BF16),
        ("w_up", (chunks,) + z.square, BF16), ("w_down", (chunks,) + z.square, BF16),
        ("xrow", rows, BF16), ("crow", rows, BF16),
        ("clu_got", (z.rows, heads, z.rows, z.part), jnp.int32), ("clus", (heads, tokens), jnp.int32),
        ("n_t", (width, tokens), BF16), ("q_t", (width, tokens), BF16),
        ("k_t", (width, tokens), BF16), ("v_t", (width, tokens), BF16),
        ("att_t", (width, tokens), BF16), ("wts", (heads, PAD, tokens), BF16),
        ("cent_t", (heads, z.head, PAD), BF16), ("cnts", (z.count_rows, PAD), F32), ("cnt_out", (z.count_rows, PAD), F32),
        ("cnt_in", (others, z.count_rows, PAD), F32), ("dens", (heads, 8, PAD), F32),
        ("res_t", (heads, stack, PAD), BF16), ("rfac", (heads, 8, PAD), F32),
        ("u_s", (heads, stack, PAD), F32), ("body", (stack, tokens), BF16),
        ("sums_f", (pairs, PAD, PAD), F32),
        ("sums", (pairs,) + packed, BF16), ("sums_in", (others, pairs) + packed, BF16),
        ("big", (pairs, z.sent_docs) + packed, BF16),
        ("big_in", (others, pairs, z.sent_docs) + packed, BF16),
        ("small", (pairs, z.small_rows, PAD), F32), ("small_in", (others, pairs, z.small_rows, PAD), F32),
        ("g_send", (pairs, z.sent_docs) + packed, BF16),
        ("g_recv", (others, pairs, z.sent_docs) + packed, BF16),
        ("c_f", (pairs, PAD, PAD), F32), ("c_s", (pairs,) + packed, BF16),
        ("c_got", (others, pairs) + packed, BF16),
        ("low", (tokens, width), BF16), ("low_t", (width, tokens), BF16),
        ("act", rows, BF16), ("gp", rows, BF16),
        ("slope", (chunks, tokens, width), BF16),
        ("acc", (tokens, width), F32), ("acc_n", (tokens, width), F32), ("gm", (tokens, width), F32),
        ("ga_t", (width, tokens), BF16), ("gk_t", (width, tokens), BF16), ("gv_t", (width, tokens), BF16),
    ]
    sems = [("load", (4 + 2 * chunks,))]
    for n in ("i", "x", "c", "o", "y"):
        sems += [(n + "_send", (z.rows,)), (n + "_recv", (z.rows,))]
    for n in ("a", "b", "s", "g", "q"):
        sems += [(n + "_ss", (others, pairs)), (n + "_rs", (others, pairs))]
    sems += [("k_ss", (others,)), ("k_rs", (others,))]
    if z.fast:
        piece = (z.block, width)
        deep = z.seq // 2
        outs.append(("sum_ref", shape((3, z.dp) + piece, BF16), anywhere))
        scratch += [
            ("gat", (3, z.dp) + piece, BF16),
            ("d_down", (z.dp, z.seq) + piece, BF16), ("d_up", (z.dp, z.seq) + piece, BF16),
            ("core_in", (2, 2, z.seq) + piece, BF16), ("first_in", (2, z.seq) + piece, BF16),
            ("second_in", (3, deep) + piece, BF16), ("third_in", (3, deep) + piece, BF16),
            ("vec_buf", (3, 8, width), F32), ("vec_got", (z.seq + 1, 8, width), F32),
        ]
        sems += [
            ("dn_ss", (2, chunks)), ("dn_rs", (2, chunks)), ("co_ss", (2, 2)), ("co_rs", (2, 2)),
            ("f_ss", (3, 2, deep)), ("f_rs", (3, 2, deep)), ("n_ss", (3, deep)), ("n_rs", (3, deep)),
            ("t_ss", (3, deep)), ("t_rs", (3, deep)), ("w_ss", (3, 3)), ("w_rs", (3, 3)),
            ("v_ss", (z.seq + 1,)), ("v_rs", (z.seq + 1,)),
        ]
    else:
        outs += [
            ("d_qkvo", shape((4, width, width), BF16), anywhere),
            ("d_up", shape((chunks, width, width), BF16), vmem),
            ("d_down", shape((z.hidden, width), BF16), vmem),
        ]
    names = [n for n, _, _ in ins + outs + scratch] + [n for n, _ in sems]
    results = pl.pallas_call(
        functools.partial(block_kernel, z, names),
        out_shape=[s for _, s, _ in outs],
        in_specs=[s for _, _, s in ins],
        out_specs=[s for _, _, s in outs],
        scratch_shapes=[pltpu.VMEM(s, t) for _, s, t in scratch] + [dma(s) for _, s in sems],
        compiler_params=pltpu.CompilerParams(
            collective_id=0, has_side_effects=True, vmem_limit_bytes=VMEM_LIMIT
        ),
    )(*[v for _, v, _ in ins])

    out_back, grad_back, vectors = results[:3]
    if z.fast:
        flat = shape((z.block, width), F32)
        grid_rows = (z.rows, z.part, width)
        published = pl.pallas_call(
            functools.partial(publish_kernel, z),
            out_shape=[
                shape(grid_rows, F32), shape(grid_rows, F32), flat, flat, flat, flat,
                shape((z.block, z.hidden), F32), shape((z.hidden // z.seq, width), F32),
                shape((8, PAD), F32),
            ],
            in_specs=[anywhere] * 3 + [vmem],
            out_specs=[anywhere] * 8 + [vmem],
            scratch_shapes=[
                pltpu.VMEM((2,) + grid_rows, BF16), pltpu.VMEM((3, z.dp) + piece, BF16),
                pltpu.VMEM((2,) + grid_rows, F32), pltpu.VMEM((3, z.dp) + piece, F32),
                dma((2, z.rows)), dma((2, z.rows)), dma((3, z.dp)), dma((3, z.dp)),
            ],
            compiler_params=pltpu.CompilerParams(vmem_limit_bytes=VMEM_LIMIT),
        )(out_back, grad_back, results[3], vectors)
        out_full, grad_full, g_q, g_k, g_v, g_o, g_up, g_down, own = published
        own = own[:, : z.block]
        return (
            out_full, grad_full, own[0], own[1], g_q, g_k, g_v, g_o, own[2], own[3], g_up, g_down,
        )

    def share(v, dim):
        v = lax.psum_scatter(v.astype(F32), "seq", scatter_dimension=dim, tiled=True)
        return lax.psum(v, "dp")

    g_up = share(jnp.transpose(results[4], (1, 0, 2)).reshape(width, z.hidden), 0)
    g_qkvo, g_down, own = share(results[3], 1), share(results[5], 0), share(vectors, 1)
    return (
        out_back.astype(F32), grad_back.astype(F32), own[0], own[1],
        g_qkvo[0], g_qkvo[1], g_qkvo[2], g_qkvo[3], own[2], own[3], g_up, g_down,
    )


def solution(mesh):
    spread = P("dp", "seq", None)
    return jax.shard_map(
        functools.partial(local, dict(mesh.shape)),
        mesh=mesh,
        in_specs=(spread, spread, P("dp", None), spread) + (P(),) * 10,
        out_specs=(spread, spread, P("seq"), P("seq")) + (P("seq", None),) * 4
        + (P("seq"), P("seq"), P("seq", None), P("seq", None)),
        check_vma=False,
    )
```

```python
import functools

import jax
import jax.numpy as jnp
from jax import lax
from jax.experimental import pallas as pl
from jax.experimental.pallas import tpu as pltpu
from jax.sharding import PartitionSpec as P

CLUSTERS = 100
PAD = 128
EPSILON = 1e-05
GELU_A = 0.7978845608028654
GELU_B = 0.044715
MESH = pl.DeviceIdType.MESH
YF = ((True, False, True, True), (False, True, False, True), (True, True, True, False))
F32 = jnp.float32
BF16 = jnp.bfloat16
VMEM_LIMIT = 63 * 2**20


def schedule(order):
    def both(g, *ks):
        return [("one", g, k, o) for k in ks for o in range(2)]

    def two(g, *ks):
        return [("two", g, k) for k in ks]

    def side(g, o, *ks):
        return [("one", g, k, o) for k in ks]

    a, b, c, d = order
    forward = {a: [], b: [("down", a)], c: [("down", b)], d: [("down", c)]}
    mixed = [step for k in order for step in two(1, k) + both(2, k)]
    return (
        [forward[k] for k in range(4)],
        ([("down", d)], [], [("up", 0)] + both(0, a), [("up", 1)] + both(0, b)),
        [("up", 2)] + both(0, c),
        ((), (), (), (), (), [("up", 3)]),
        ((), (), (), (), (), both(0, d)),
        ((),) * 6,
        both(1, *order),
        [("part", 3), ("part", 1), ("part", 2), ("part", 0), ("vec", 1)] + two(0, *order) + mixed + [("vec", 2)] + two(2, *order)
        + [("three", 0), ("gather", 0), ("three", 1), ("gather", 1), ("three", 2), ("vec", 3), ("store", 0)]
        + [("store", 1), ("gather", 2), ("store", 2)],
        [],
        [],
    )


class Plan:
    def __init__(self, mesh_shape, inputs, clusters, lengths, w_up):
        self.seq, self.dp = mesh_shape["seq"], mesh_shape["dp"]
        self.rows, self.part, self.width = inputs.shape
        self.heads, self.docs, self.hidden = clusters.shape[2], lengths.shape[1], w_up.shape[1]
        self.head = self.width // self.heads
        self.tokens = self.rows * self.part
        self.mates = self.seq // self.rows
        self.sent_docs = 1 if self.mates == 2 else self.docs
        self.block = self.width // self.seq
        self.fast = (
            self.dp == 4 and self.seq == 8 and self.block % 16 == 0 and self.hidden == 4 * self.width
        )
        self.reduce = self.fast
        self.sent_rows = -(-CLUSTERS // 16) * 16
        self.small_rows = 8 if self.mates == 2 else 16
        self.count_rows = -(-self.heads // 8) * 8
        self.order = (0, 3, 1, 2)
        self.tasks = schedule(self.order)
        self.square = (self.seq, self.block, self.width) if self.fast else (self.width, self.width)
        self.y_first = [[w[self.order.index(k)] for k in range(4)] for w in YF]

    def place(self, j):
        return lax.rem(j, self.rows), j // self.rows

    def owner(self, r, h):
        return h * self.rows + r


def nn(a, b):
    return lax.dot_general(a, b, (((1,), (0,)), ((), ())), preferred_element_type=F32)


def nt(a, b):
    return lax.dot_general(a, b, (((1,), (1,)), ((), ())), preferred_element_type=F32)


def tn(a, b):
    return lax.dot_general(a, b, (((0,), (0,)), ((), ())), preferred_element_type=F32)


def remote(src, dst, send, recv, to):
    return pltpu.make_async_remote_copy(
        src_ref=src, dst_ref=dst, send_sem=send, recv_sem=recv, device_id=to, device_id_type=MESH
    )


def one_hot(row):
    ids = lax.broadcasted_iota(jnp.int32, (PAD, row.shape[1]), 0)
    return jnp.where(ids == row, 1.0, 0.0).astype(BF16)


def doc_masks(z, r, h, len_ref):
    pos = h * z.tokens + lax.broadcasted_iota(jnp.int32, (1, z.tokens), 1)
    seg = jnp.zeros((1, z.tokens), jnp.int32)
    end, ends = jnp.int32(0), []
    for s in range(z.docs):
        end = end + len_ref[r, s]
        ends.append(end)
        seg = seg + (pos >= end).astype(jnp.int32)
    last = sum((z.tokens - 1 >= e).astype(jnp.int32) for e in ends)
    first = sum((z.tokens >= e).astype(jnp.int32) for e in ends)
    spans = last == first
    mine = jnp.where(h == 0, last, first)
    return seg, spans, mine


def stacked_masks(z, seg):
    ids = lax.broadcasted_iota(jnp.int32, (z.docs * z.head, z.tokens), 0)
    body = jnp.where(ids // z.head == seg, 1.0, 0.0).astype(BF16)
    low = lax.broadcasted_iota(jnp.int32, (16, z.tokens), 0)
    tail = jnp.where((low % z.docs == seg) & (low < 2 * z.docs), 1.0, 0.0).astype(BF16)
    return body, tail


def pick_doc(z, blocks, mine):
    out = blocks[0]
    for s in range(1, z.docs):
        out = jnp.where(mine == s, blocks[s], out)
    return out


def mate_id(z, r, h, step):
    return {"seq": z.owner(r, lax.rem(h + step, z.mates))}


def rows_out(z, j, r, h, src, dst, send, recv):
    for row in range(z.rows):
        to = z.owner(row, h)

        @pl.when(to != j)
        def _():
            remote(src.at[row], dst.at[r], send.at[row], recv.at[r], {"seq": to}).start()

        @pl.when(to == j)
        def _():
            pltpu.make_async_copy(src.at[row], dst.at[r], recv.at[r]).start()


def rows_landed(z, j, h, src, dst, send, recv, slot):
    source = z.owner(slot, h)

    @pl.when(source == j)
    def _():
        pltpu.make_async_copy(src.at[0], dst.at[slot], recv.at[slot]).wait()

    @pl.when(source != j)
    def _():
        remote(src.at[0], dst.at[slot], send.at[0], recv.at[slot], {"seq": source}).wait_recv()


def rows_sent(z, j, h, src, dst, send, recv):
    for row in range(z.rows):
        to = z.owner(row, h)

        @pl.when(to != j)
        def _():
            remote(src.at[row], dst.at[0], send.at[row], recv.at[0], {"seq": to}).wait_send()


def norm_parts(values):
    average = jnp.mean(values, axis=-1, keepdims=True)
    centered = values - average
    inverse = lax.rsqrt(jnp.mean(centered * centered, axis=-1, keepdims=True) + EPSILON)
    return centered * inverse, inverse


def norm_back(grad, unit, inverse, gain):
    scaled = grad * gain
    inner = (
        scaled
        - jnp.mean(scaled, axis=-1, keepdims=True)
        - unit * jnp.mean(scaled * unit, axis=-1, keepdims=True)
    )
    return inner * inverse


def joined_masks(z, blocks, seg):
    out = blocks[: z.head]
    for s in range(1, z.docs):
        out = jnp.where(seg == s, blocks[s * z.head : (s + 1) * z.head], out)
    return out


class Refs:
    def __init__(self, names, values):
        self.__dict__.update(zip(names, values, strict=True))


def block_kernel(z, names, *values):
    f = Refs(names, values)
    j = lax.axis_index("seq")
    me = lax.axis_index("dp")
    r, h = z.place(j)
    width, part = z.width, z.part

    barrier = pltpu.get_barrier_semaphore()
    for d in range(1, z.seq):
        pl.semaphore_signal(
            barrier, 1, device_id={"seq": lax.rem(j + d, z.seq)}, device_id_type=MESH
        )
    greeted = z.seq - 1
    if z.reduce:
        for d in range(1, z.dp):
            pl.semaphore_signal(
                barrier, 1, device_id={"dp": lax.rem(me + d, z.dp)}, device_id_type=MESH
            )
        greeted += z.dp - 1

    loads = [
        pltpu.make_async_copy(ref, f.w_qkv.at[p], f.load.at[p])
        for p, ref in enumerate((f.wq_in, f.wk_in, f.wv_in))
    ]
    loads.append(pltpu.make_async_copy(f.wo_in, f.w_o, f.load.at[3]))
    chunks = z.hidden // width
    for c in range(chunks):
        loads.append(
            pltpu.make_async_copy(
                f.up_in.at[(slice(None),) * (len(z.square) - 1) + (pl.ds(c * width, width),)],
                f.w_up.at[c],
                f.load.at[4 + c],
            )
        )
        loads.append(
            pltpu.make_async_copy(f.down_in.at[c], f.w_down.at[c], f.load.at[4 + chunks + c])
        )
    for copy in loads[:3]:
        copy.start()

    seg, spans, mine = doc_masks(z, r, h, f.lengths)
    body_value, tail = stacked_masks(z, seg)
    f.body[...] = body_value
    gain_attn, bias_attn = f.gain_attn[...].reshape(1, width), f.bias_attn[...].reshape(1, width)
    gain_ffn, bias_ffn = f.gain_ffn[...].reshape(1, width), f.bias_ffn[...].reshape(1, width)
    pl.semaphore_wait(barrier, greeted)

    def clu_copy(step):
        to = {"seq": z.owner(lax.rem(r + step, z.rows), h)}
        return remote(f.clu_in, f.clu_got.at[step], f.i_send.at[step], f.i_recv.at[step], to)

    own_clu = pltpu.make_async_copy(f.clu_in, f.clu_got.at[0], f.i_recv.at[0])
    own_clu.start()
    for step in range(1, z.rows):
        clu_copy(step).start()
    rows_out(z, j, r, h, f.x_in, f.xrow, f.x_send, f.x_recv)
    for copy in loads[3:]:
        copy.start()

    def part_rows(t):
        return pl.ds(pl.multiple_of(t * part, part), part)

    def head_rows(i):
        return pl.ds(pl.multiple_of(i * z.head, z.head), z.head)

    own_clu.wait()
    for step in range(z.rows):
        if step:
            clu_copy(step).wait()
        slot = lax.rem(r + z.rows - step, z.rows)
        numbers = f.clu_got[step, :, pl.ds(r, 1), :].reshape(z.heads, part)
        f.clus[:, part_rows(slot)] = numbers

    def mate_copy(src, dst, send, recv, i, step):
        to = {"seq": z.owner(r, lax.rem(h + step, z.mates))}
        return remote(src.at[i], dst.at[step - 1, i], send.at[step - 1, i], recv.at[step - 1, i], to)

    def sum_copy(i, step):
        return mate_copy(f.sums, f.sums_in, f.a_ss, f.a_rs, i, step)

    def result_copies(i, step):
        return (
            mate_copy(f.big, f.big_in, f.b_ss, f.b_rs, i, step),
            mate_copy(f.small, f.small_in, f.s_ss, f.s_rs, i, step),
        )

    def grad_copy(i, step):
        return mate_copy(f.g_send, f.g_recv, f.g_ss, f.g_rs, i, step)

    def cent_copy(i, step):
        return mate_copy(f.c_s, f.c_got, f.q_ss, f.q_rs, i, step)

    others = range(1, z.mates)
    stack = z.docs * z.head
    pairs = z.heads // 2
    low_lanes = z.sent_rows

    def pack(pair):
        return pair.astype(BF16).T[:low_lanes]

    def unpack(packed):
        rest = jnp.zeros((PAD - low_lanes, PAD), BF16)
        return jnp.concatenate([packed, rest], axis=0).T.astype(F32)

    def member_of(i):
        return one_hot(f.clus[pl.ds(i, 1), :])

    ones = jnp.ones((8, z.tokens), BF16)
    f.cnt_out[...] = jnp.zeros_like(f.cnt_out)
    for i in range(z.heads):
        f.cnt_out[i : i + 1] = nt(ones, one_hot(f.clus[i : i + 1, :]))[:1]

    def count_copy(step):
        to = {"seq": z.owner(r, lax.rem(h + step, z.mates))}
        return remote(f.cnt_out, f.cnt_in.at[step - 1], f.k_ss.at[step - 1], f.k_rs.at[step - 1], to)

    for step in others:
        count_copy(step).start()
    for copy in loads[:3]:
        copy.wait()

    def project(slot, carry):
        rows_landed(z, j, h, f.x_in, f.xrow, f.x_send, f.x_recv, slot)
        unit, _ = norm_parts(f.xrow[slot].astype(F32))
        normed = (unit * gain_attn + bias_attn).astype(BF16)
        f.low[part_rows(slot), :] = normed
        f.n_t[:, part_rows(slot)] = normed.T
        f.q_t[:, part_rows(slot)] = nn(normed, f.w_qkv[0]).astype(BF16).T
        return carry

    lax.fori_loop(0, z.rows, project, 0)

    def cluster_sums(i, carry):
        pair = jnp.concatenate(
            [nt(f.q_t[head_rows(2 * i + a), :], member_of(2 * i + a)) for a in range(2)], axis=0
        )
        f.sums_f[i] = pair
        f.sums[i] = pack(pair)
        for step in others:
            sum_copy(i, step).start()
        return carry

    lax.fori_loop(0, pairs, cluster_sums, 0)
    rows_sent(z, j, h, f.x_in, f.xrow, f.x_send, f.x_recv)
    rows_out(z, j, r, h, f.c_in, f.crow, f.c_send, f.c_recv)
    counts = f.cnt_out[...]
    for step in others:
        count_copy(step).wait()
        counts = counts + f.cnt_in[step - 1]
    f.cnts[...] = jnp.maximum(counts, 1.0)

    def project_more(t, carry):
        normed = f.low[part_rows(t), :]
        f.k_t[:, part_rows(t)] = nn(normed, f.w_qkv[1]).astype(BF16).T
        f.v_t[:, part_rows(t)] = nn(normed, f.w_qkv[2]).astype(BF16).T
        return carry

    lax.fori_loop(0, z.rows, project_more, 0)

    def masked_values(i):
        return jnp.concatenate([f.v_t[head_rows(i), :]] * z.docs, axis=0) * f.body[...]

    def doc_rows(blocks, s):
        return blocks[s * z.head : (s + 1) * z.head]

    def border(blocks):
        if z.mates == 2:
            parts = [[doc_rows(b, s) for s in range(z.docs)] for b in blocks]
            return [pack(jnp.concatenate([pick_doc(z, p, mine) for p in parts], axis=0))]
        return [
            pack(jnp.concatenate([doc_rows(b, s) for b in blocks], axis=0)) for s in range(z.docs)
        ]

    def attend(i, carry):
        total = f.sums_f[i]
        for step in others:
            sum_copy(i, step).wait()
            total = total + unpack(f.sums_in[step - 1, i])
        blocks, small = [], []
        for a in range(2):
            n = 2 * i + a
            count = f.cnts[pl.ds(n, 1), :]
            cent = (total[a * z.head : (a + 1) * z.head] / count).astype(BF16)
            f.cent_t[n] = cent
            scores = tn(cent, f.k_t[head_rows(n), :]) * 0.125
            top = jnp.max(scores, axis=1, keepdims=True)
            weights = jnp.exp(scores - top).astype(BF16)
            f.wts[n] = weights
            both = nt(jnp.concatenate([masked_values(n), tail], axis=0), weights)
            f.u_s[n] = both[:stack]
            top_row = jnp.broadcast_to(top, (PAD, PAD)).T
            denoms = both[stack : stack + 4]
            f.dens[n] = jnp.concatenate([denoms, top_row[:4]], axis=0)
            blocks.append(both[:stack])
            if z.mates == 2:
                own = pick_doc(z, [denoms[s : s + 1] for s in range(z.docs)], mine)
                small += [jnp.broadcast_to(own, (2, PAD)), top_row[:2]]
            else:
                small += [denoms, top_row[:4]]
        f.small[i] = jnp.concatenate(small, axis=0)
        for d, packed in enumerate(border(blocks)):
            f.big[i, d] = packed
        for step in others:
            for copy in result_copies(i, step):
                copy.start()
        return carry

    lax.fori_loop(0, pairs, attend, 0)
    empty = [jnp.where(jnp.sum((seg == s).astype(F32)) > 0.5, 0.0, 1.0) for s in range(z.docs)]
    half_small = z.small_rows // 2

    def finish(i, carry):
        got = []
        for step in others:
            for copy in result_copies(i, step):
                copy.wait()
            got.append([unpack(f.big_in[step - 1, i, d]) for d in range(z.sent_docs)])
        for a in range(2):
            n = 2 * i + a
            own = f.dens[n]
            top, highest = own[4:5], own[4:5]
            sides = []
            for step in others:
                side = f.small_in[step - 1, i, a * half_small : (a + 1) * half_small]
                sides.append((side, side[half_small // 2 : half_small // 2 + 1]))
                highest = jnp.maximum(highest, sides[-1][1])
            scale = jnp.exp(top - highest)
            scaled, factors = [], []
            for s in range(z.docs):
                piece = f.u_s[n, s * z.head : (s + 1) * z.head]
                denom = own[s : s + 1]
                joined, joined_denom = piece * scale, denom * scale
                d = 0 if z.mates == 2 else s
                for other, (side, side_top) in zip(got, sides):
                    side_scale = jnp.exp(side_top - highest)
                    joined = joined + other[d][a * z.head : (a + 1) * z.head] * side_scale
                    joined_denom = joined_denom + side[d : d + 1] * side_scale
                here = jnp.logical_and(spans, mine == s) if z.mates == 2 else True
                joined = jnp.where(here, joined, piece)
                joined_denom = jnp.where(here, joined_denom, denom)
                factor = jnp.where(here, scale, jnp.ones_like(scale))
                joined_denom = joined_denom + jnp.where(joined_denom > 0.0, 0.0, empty[s])
                inverse = 1.0 / joined_denom
                scaled.append((joined * inverse).astype(BF16))
                factors.append(inverse * factor)
            result = jnp.concatenate(scaled, axis=0)
            f.res_t[n] = result
            f.rfac[n] = jnp.concatenate(factors + [jnp.zeros((8 - z.docs, PAD), F32)], axis=0)
            f.att_t[head_rows(n), :] = joined_masks(z, nn(result, member_of(n)), seg).astype(BF16)
        return carry

    lax.fori_loop(0, pairs, finish, 0)

    core, y = lax.rem(me, 2), me // 2
    xx, zz = lax.rem(j, 2), j // 2
    sibling, across = me + 1 - 2 * core, me + 2 - 4 * y
    beside = j + 1 - 2 * xx
    deep = z.seq // 2
    if z.reduce:
        grads = (f.d_down, f.d_up, f.w_up)
        core_in = (f.core_in.at[0], f.core_in.at[1], f.w_down.at[pl.ds(0, 2)])
        first_in = (f.first_in.at[0], f.first_in.at[1], f.w_down.at[2])

    def add(ref, value):
        ref[...] = ref[...] + value

    def block(g, yp, xb, k):
        return core_in[g].at[yp, 2 * k + xb]

    def grad_block(g, p, b):
        return grads[g][p, b]

    def down_core(yp, c):
        src = f.d_down.at[yp * 2 + 1 - core, pl.ds(2 * c, 2)]
        dst = core_in[0].at[yp, pl.ds(2 * c, 2)]
        return remote(src, dst, f.dn_ss.at[yp, c], f.dn_rs.at[yp, c], {"dp": sibling})

    def part_core(g, p):
        yp = p // 2
        if g == 1:
            src, dst = f.d_up.at[p], core_in[1].at[yp]
        else:
            src, dst = f.w_up.at[p], f.w_down.at[yp]
        return remote(src, dst, f.co_ss.at[g - 1, yp], f.co_rs.at[g - 1, yp], {"dp": sibling})

    def y_first(g, k):
        return z.y_first[g][k]

    def step_one(g, k, other):
        if y_first(g, k):
            src, to = block(g, 1 - y, other, k), {"dp": across}
        else:
            src, to = block(g, other, 1 - xx, k), {"seq": beside}
        dst = first_in[g].at[other * deep + k]
        return remote(src, dst, f.f_ss.at[g, other, k], f.f_rs.at[g, other, k], to)

    def step_two(g, k):
        if y_first(g, k):
            src, to = block(g, y, 1 - xx, k), {"seq": beside}
        else:
            src, to = block(g, 1 - y, xx, k), {"dp": across}
        return remote(src, f.second_in.at[g, k], f.n_ss.at[g, k], f.n_rs.at[g, k], to)

    def one_done(g, k, other):
        if y_first(g, k):
            own, far = block(g, y, other, k), xx != other
        else:
            own, far = block(g, other, xx, k), y != other
        step_one(g, k, other).wait_recv()
        add(own, first_in[g][other * deep + k])
        pl.when(far)(lambda: step_two(g, k).start())


    def step_three(g, k):
        return remote(
            block(g, y, xx, k), f.third_in.at[g, zz], f.t_ss.at[g, k], f.t_rs.at[g, zz],
            {"seq": 2 * k + xx},
        )

    def two_done(g, k):
        step_two(g, k).wait_recv()
        add(block(g, y, xx, k), f.second_in[g, k])

        @pl.when(zz != k)
        def _():
            step_three(g, k).start()

    def gather_copy(g, kind):
        src = across if kind == 2 else me
        to = {"dp": across if kind == 1 else sibling}
        ref = f.gat.at[g, src]
        return remote(ref, ref, f.w_ss.at[g, kind], f.w_rs.at[g, kind], to)

    def three_done(g):
        total = core_in[g][y, j].astype(F32)
        for k in range(1, deep):
            source = lax.rem(zz + k, deep)
            remote(
                block(g, y, xx, zz), f.third_in.at[g, source], f.t_ss.at[g, source],
                f.t_rs.at[g, source], {"seq": 2 * source + xx},
            ).wait_recv()
            total = total + f.third_in[g, source].astype(F32)
        f.gat[g, me] = total.astype(BF16)
        gather_copy(g, 1).start()
        gather_copy(g, 0).start()

    def gather_wait(g, kind):
        source = (sibling, across, across + sibling - me)[kind]
        ref = f.gat.at[g, source]
        to = {"dp": across if kind == 1 else sibling}
        remote(ref, ref, f.w_ss.at[g, kind], f.w_rs.at[g, kind], to).wait_recv()

    def gather_done(g):
        gather_wait(g, 1)
        gather_copy(g, 2).start()

    def store_copy(g):
        return pltpu.make_async_copy(f.gat.at[g], f.sum_ref.at[g], f.load.at[g])

    def store(g):
        gather_wait(g, 0)
        gather_wait(g, 2)
        store_copy(g).start()

    def part_done(g, p):
        yp = p // 2
        part_core(g, p).wait_recv()

        def body(b, carry):
            add(core_in[g].at[yp, b], grad_block(g, p, b))
            return carry

        lax.fori_loop(0, z.seq, body, 0)
        for k in z.order:
            if y_first(g, k):

                @pl.when(yp != y)
                def _():
                    step_one(g, k, 1 - xx).start()
                    step_one(g, k, xx).start()
            else:
                step_one(g, k, yp).start()

    def down_done(c):
        for yp in range(2):
            down_core(yp, c).wait_recv()
            for xb in range(2):
                add(block(0, yp, xb, c), f.d_down[yp * 2 + core, 2 * c + xb])
            if y_first(0, c):

                @pl.when(yp != y)
                def _():
                    step_one(0, c, 1 - xx).start()
                    step_one(0, c, xx).start()
            else:
                step_one(0, c, yp).start()

    def vec_copy(t, to):
        return remote(f.vec_buf.at[min(t, 2)], f.vec_got.at[t], f.v_ss.at[t], f.v_rs.at[t], to)

    def vec_step(t):
        if t == 1:
            vec_copy(0, {"dp": sibling}).wait()
            f.vec_buf[1] = f.vec_buf[0] + f.vec_got[0]
            vec_copy(1, {"dp": across}).start()
            return
        if t == 2:
            vec_copy(1, {"dp": across}).wait()
            f.vec_buf[2] = f.vec_buf[1] + f.vec_got[1]
        total = f.vec_buf[2]
        for d in range(1, z.seq):
            copy = vec_copy(1 + d, {"seq": lax.rem(j + d, z.seq)})
            if t == 2:
                copy.start()
            else:
                copy.wait()
                total = total + f.vec_got[1 + d]
        if t == 3:
            f.vec_ref[...] = total

    def part_step(p):
        pl.when(core == p % 2)(lambda: part_done(2, p))

    def up_step(c):
        pl.when(c % 2 == core)(lambda: part_done(1, c))

    steps = {
        "down": down_done, "store": store,
        "one": one_done, "two": two_done, "three": three_done, "gather": gather_done,
        "vec": vec_step, "part": part_step, "up": up_step,
    }

    def run(tasks):
        for name, *numbers in tasks:
            steps[name](*numbers)

    def serve(i, table):
        if z.reduce:
            for at, tasks in enumerate(table):
                if tasks:
                    pl.when(i == at)(functools.partial(run, tasks))

    for copy in loads[3:]:
        copy.wait()

    def first(t, carry):
        size = 2 * part
        rows = pl.ds(pl.multiple_of(t * size, size), size)
        values = f.xrow[pl.ds(2 * t, 2)].reshape(size, width).astype(F32)
        middle = values + tn(f.att_t[:, rows], f.w_o[...])
        f.acc[rows, :] = middle
        f.gm[rows, :] = middle
        unit, _ = norm_parts(middle)
        normed = (unit * gain_ffn + bias_ffn).astype(BF16)
        f.low[rows, :] = normed
        f.low_t[:, rows] = normed.T
        f.acc_n[rows, :] = jnp.zeros((size, width), F32)
        return carry

    lax.fori_loop(0, z.rows // 2, first, 0)
    for slot in range(z.rows):
        rows_landed(z, j, h, f.c_in, f.crow, f.c_send, f.c_recv, slot)
    rows_sent(z, j, h, f.c_in, f.crow, f.c_send, f.c_recv)
    halves = z.rows // 2

    halves_of = [slice(t * halves, (t + 1) * halves) for t in range(2)]
    rows_of = [slice(t * halves * part, (t + 1) * halves * part) for t in range(2)]

    def ffn_chunk(c, carry):
        w_up, w_down = f.w_up[c].reshape(width, width), f.w_down[c].reshape(width, width)
        for t in range(2):
            rows, own = rows_of[t], halves_of[t]
            u = nn(f.low[rows, :], w_up)
            tanh = jnp.tanh(GELU_A * (u + GELU_B * (u * u * u)))
            cdf = 0.5 * (1.0 + tanh)
            f.act[own] = (u * cdf).astype(BF16).reshape(halves, part, width)
            slope = cdf + (0.5 * GELU_A) * u * (1.0 - tanh * tanh) * (1.0 + (3.0 * GELU_B) * (u * u))
            f.slope[c, rows, :] = slope.astype(BF16)
            f.acc[rows, :] += nn(f.act[own].reshape(halves * part, width), w_down)
        down = tn(
            f.act[...].reshape(z.tokens, width), f.crow[...].reshape(z.tokens, width)
        ).astype(BF16)
        if z.fast:
            for b in range(2):
                for p in range(z.dp):
                    at = (b * z.dp + p) * z.block
                    f.d_down[p, 2 * c + b] = down[at : at + z.block]
        else:
            f.d_down[pl.ds(pl.multiple_of(c * width, width), width), :] = down
        if z.reduce:
            run(z.tasks[0][c])
            for yp in range(2):
                down_core(yp, c).start()
        return carry

    def back_chunk(c, carry):
        w_up, w_down = f.w_up[c].reshape(width, width), f.w_down[c].reshape(width, width)
        for t in range(2):
            rows, own = rows_of[t], halves_of[t]
            grad = nt(f.crow[own].reshape(halves * part, width), w_down)
            f.gp[own] = (grad * f.slope[c, rows, :].astype(F32)).astype(BF16).reshape(halves, part, width)
            f.acc_n[rows, :] += nt(f.gp[own].reshape(halves * part, width), w_up)
        up = nn(f.low_t[...], f.gp[...].reshape(z.tokens, width)).astype(BF16)
        f.d_up[c] = up.reshape(f.d_up.shape[1:])
        if z.reduce:
            run(z.tasks[1][c])
            pl.when(c % 2 != core)(lambda: part_core(1, c).start())
        return carry

    def each_chunk(body, order):
        if z.reduce:
            for c in order:
                body(c, 0)
        else:
            lax.fori_loop(0, chunks, body, 0)

    each_chunk(ffn_chunk, z.order)

    def ffn_out(t, carry):
        f.act[t] = f.acc[part_rows(t), :].astype(BF16)
        return carry

    lax.fori_loop(0, z.rows, ffn_out, 0)
    rows_out(z, j, r, h, f.act, f.out_ref, f.o_send, f.o_recv)
    each_chunk(back_chunk, range(chunks))

    def ffn_back(t, carry):
        rows = part_rows(t)
        unit, inverse = norm_parts(f.gm[rows, :])
        grad = f.acc_n[rows, :]
        grad_middle = f.crow[t].astype(F32) + norm_back(grad, unit, inverse, gain_ffn)
        f.gm[rows, :] = grad_middle
        f.low[rows, :] = grad_middle.astype(BF16)
        return (
            carry[0] + jnp.sum(grad * unit, axis=0, keepdims=True),
            carry[1] + jnp.sum(grad, axis=0, keepdims=True),
        )

    zero = jnp.zeros((1, width), F32)
    sums_ffn = lax.fori_loop(0, z.rows, ffn_back, (zero, zero))
    f.ga_t[...] = nt(f.w_o[...], f.low[...]).astype(BF16)

    if z.reduce:
        run(z.tasks[2])

    def gather_grads(i, carry):
        blocks = []
        for a in range(2):
            n = 2 * i + a
            masked = jnp.concatenate([f.ga_t[head_rows(n), :]] * z.docs, axis=0) * f.body[...]
            blocks.append(nt(masked, member_of(n)))
            f.u_s[n] = blocks[-1]
        for d, packed in enumerate(border(blocks)):
            f.g_send[i, d] = packed
        for step in others:
            grad_copy(i, step).start()
        serve(i, z.tasks[3])
        return carry

    lax.fori_loop(0, pairs, gather_grads, 0)
    f.w_up[3] = nn(f.att_t[...], f.low[...]).astype(BF16).reshape(z.square)
    if z.reduce:
        pl.when(core == 0)(lambda: part_core(2, 3).start())

    def attend_back(i, carry):
        serve(i, z.tasks[4])
        got = []
        for step in others:
            grad_copy(i, step).wait()
            got.append([unpack(f.g_recv[step - 1, i, d]) for d in range(z.sent_docs)])
        cents = []
        for a in range(2):
            n = 2 * i + a
            result, factor = f.res_t[n], f.rfac[n]
            lows, deltas = [], []
            for s in range(z.docs):
                grad = f.u_s[n, s * z.head : (s + 1) * z.head]
                joined = grad
                for other in got:
                    piece = other[0 if z.mates == 2 else s]
                    joined = joined + piece[a * z.head : (a + 1) * z.head]
                if z.mates == 2:
                    joined = jnp.where(jnp.logical_and(spans, mine == s), joined, grad)
                scaled = joined * factor[s : s + 1]
                lows.append(scaled.astype(BF16))
                piece = doc_rows(result, s).astype(F32)
                deltas.append(-jnp.sum(scaled * piece, axis=0, keepdims=True))
            delta = jnp.concatenate(deltas, axis=0)
            high = delta.astype(BF16).astype(F32)
            small = jnp.concatenate(
                [high, delta - high, jnp.zeros((16 - 2 * z.docs, PAD), F32)], axis=0
            ).astype(BF16)
            low = jnp.concatenate(lows, axis=0)
            diff = tn(
                jnp.concatenate([low, small], axis=0),
                jnp.concatenate([masked_values(n), tail], axis=0),
            )
            weights = f.wts[n]
            raw = (0.125 * (weights.astype(F32) * diff)).astype(BF16)
            f.gk_t[head_rows(n), :] = nn(f.cent_t[n], raw).astype(BF16)
            f.gv_t[head_rows(n), :] = joined_masks(z, nn(low, weights), seg).astype(BF16)
            cents.append(nt(f.k_t[head_rows(n), :], raw))
        pair = jnp.concatenate(cents, axis=0)
        f.c_f[i] = pair
        f.c_s[i] = pack(pair)
        for step in others:
            cent_copy(i, step).start()
        return carry

    lax.fori_loop(0, pairs, attend_back, 0)
    if z.reduce:
        run(z.tasks[8])

    def weight_grad(p, g_ref):
        f.w_up[p] = nt(f.n_t[...], g_ref[...]).astype(BF16).reshape(z.square)
        if z.reduce:
            pl.when(p % 2 != core)(lambda: part_core(2, p).start())

    weight_grad(1, f.gk_t)
    weight_grad(2, f.gv_t)

    def query_back(i, carry):
        total = f.c_f[i]
        for step in others:
            cent_copy(i, step).wait()
            total = total + unpack(f.c_got[step - 1, i])
        for a in range(2):
            n = 2 * i + a
            low = (total[a * z.head : (a + 1) * z.head] / f.cnts[pl.ds(n, 1), :]).astype(BF16)
            f.q_t[head_rows(n), :] = nn(low, member_of(n)).astype(BF16)
        serve(i, z.tasks[5])
        return carry

    lax.fori_loop(0, pairs, query_back, 0)
    if z.reduce:
        run(z.tasks[9])
    weight_grad(0, f.q_t)

    if z.reduce:
        run(z.tasks[6])

    total = (
        nn(f.w_qkv[0], f.q_t[...]) + nn(f.w_qkv[1], f.gk_t[...]) + nn(f.w_qkv[2], f.gv_t[...])
    )
    f.acc[...] = total.T

    def attn_back(t, carry):
        rows = part_rows(t)
        unit, inverse = norm_parts(f.xrow[t].astype(F32))
        grad = f.acc[rows, :]
        f.gp[t] = (f.gm[rows, :] + norm_back(grad, unit, inverse, gain_attn)).astype(BF16)
        return (
            carry[0] + jnp.sum(grad * unit, axis=0, keepdims=True),
            carry[1] + jnp.sum(grad, axis=0, keepdims=True),
        )

    sums_attn = lax.fori_loop(0, z.rows, attn_back, (zero, zero))
    rows_out(z, j, r, h, f.gp, f.gx_ref, f.y_send, f.y_recv)
    vectors = jnp.concatenate([*sums_attn, *sums_ffn, jnp.zeros((4, width), F32)], axis=0)

    if z.reduce:
        f.vec_buf[0] = vectors
        vec_copy(0, {"dp": sibling}).start()
        run(z.tasks[7])
        for g in range(3):
            store_copy(g).wait()
            for kind in range(3):
                gather_copy(g, kind).wait_send()
            for k in range(deep):
                for other in range(2):
                    step_one(g, k, other).wait_send()
                step_two(g, k).wait_send()
                pl.when(zz != k)(lambda k=k, g=g: step_three(g, k).wait_send())

        for yp in range(2):
            for c in range(chunks):
                down_core(yp, c).wait_send()
            for g in (1, 2):
                part_core(g, yp * 2 + 1 - core).wait_send()
    else:
        f.vec_ref[...] = vectors
        if not z.fast:
            copy = pltpu.make_async_copy(f.w_up, f.d_qkvo, f.load.at[0])
            copy.start()
            copy.wait()

    for slot in range(z.rows):
        rows_landed(z, j, h, f.act, f.out_ref, f.o_send, f.o_recv, slot)
        rows_landed(z, j, h, f.gp, f.gx_ref, f.y_send, f.y_recv, slot)
    rows_sent(z, j, h, f.act, f.out_ref, f.o_send, f.o_recv)
    rows_sent(z, j, h, f.gp, f.gx_ref, f.y_send, f.y_recv)


def publish_kernel(
    z, rows_a, rows_b, sums, vectors, out_a, out_b, w_q, w_k, w_v, w_o, w_up, w_down, own,
    rows_in, sums_in, rows_wide, sums_wide, r_in, r_out, s_in, s_out,
):
    pieces = []
    for a, (src, dst) in enumerate(((rows_a, out_a), (rows_b, out_b))):
        for t in range(z.rows):
            pieces.append(
                (src.at[t], rows_in.at[a, t], rows_wide.at[a, t], dst.at[t], r_in.at[a, t], r_out.at[a, t])
            )
    for g in range(3):
        for p in range(z.dp):
            if g == 0:
                dst = w_down.at[pl.ds(p * z.block, z.block), :]
            elif g == 1:
                dst = w_up.at[:, pl.ds(p * z.width, z.width)]
            else:
                dst = (w_q, w_k, w_v, w_o)[p]
            pieces.append(
                (sums.at[g, p], sums_in.at[g, p], sums_wide.at[g, p], dst, s_in.at[g, p], s_out.at[g, p])
            )
    for src, low, _, _, sem, _ in pieces:
        pltpu.make_async_copy(src, low, sem).start()
    for src, low, wide, dst, sem, done in pieces:
        pltpu.make_async_copy(src, low, sem).wait()
        wide[...] = low[...].astype(F32)
        pltpu.make_async_copy(wide, dst, done).start()
    first = lax.axis_index("seq") * z.block
    rows = lax.broadcasted_iota(jnp.int32, (z.width, PAD), 0)
    lanes = lax.broadcasted_iota(jnp.int32, (z.width, PAD), 1)
    pick = jnp.where(rows == lanes + first, 1.0, 0.0)
    own[...] = jnp.dot(
        vectors[...], pick, precision=lax.Precision.HIGHEST, preferred_element_type=F32
    )
    for _, _, wide, dst, _, done in pieces:
        pltpu.make_async_copy(wide, dst, done).wait()


def local(
    mesh_shape,
    inputs, cotangent, lengths, clusters, gain_attn, bias_attn, w_query, w_key, w_value, w_out,
    gain_ffn, bias_ffn, w_up, w_down,
):
    z = Plan(mesh_shape, inputs, clusters, lengths, w_up)
    width, tokens, heads, docs = z.width, z.tokens, z.heads, z.docs
    others, stack, chunks = z.mates - 1, z.docs * z.head, z.hidden // z.width
    anywhere = pl.BlockSpec(memory_space=pl.ANY)
    vmem = pl.BlockSpec(memory_space=pltpu.VMEM)
    smem = pl.BlockSpec(memory_space=pltpu.SMEM)
    dma = pltpu.SemaphoreType.DMA
    shape = jax.ShapeDtypeStruct
    turned = jnp.transpose(clusters, (2, 0, 1))
    rows = (z.rows, z.part, width)

    ins = [
        ("x_in", inputs, anywhere), ("c_in", cotangent, anywhere), ("clu_in", turned, anywhere),
        ("lengths", lengths, smem), ("gain_attn", gain_attn, vmem), ("bias_attn", bias_attn, vmem),
        ("gain_ffn", gain_ffn, vmem), ("bias_ffn", bias_ffn, vmem),
        ("wq_in", w_query, anywhere), ("wk_in", w_key, anywhere), ("wv_in", w_value, anywhere),
        ("wo_in", w_out, anywhere), ("up_in", w_up.reshape(z.square[:-1] + (z.hidden,)), anywhere),
        ("down_in", w_down.reshape((chunks,) + z.square), anywhere),
    ]
    outs = [
        ("out_ref", shape(rows, BF16), anywhere), ("gx_ref", shape(rows, BF16), anywhere),
        ("vec_ref", shape((8, width), F32), vmem),
    ]
    pairs, packed = heads // 2, (z.sent_rows, PAD)
    scratch = [
        ("w_qkv", (3, width, width), BF16), ("w_o", (width, width), BF16),
        ("w_up", (chunks,) + z.square, BF16), ("w_down", (chunks,) + z.square, BF16),
        ("xrow", rows, BF16), ("crow", rows, BF16),
        ("clu_got", (z.rows, heads, z.rows, z.part), jnp.int32), ("clus", (heads, tokens), jnp.int32),
        ("n_t", (width, tokens), BF16), ("q_t", (width, tokens), BF16),
        ("k_t", (width, tokens), BF16), ("v_t", (width, tokens), BF16),
        ("att_t", (width, tokens), BF16), ("wts", (heads, PAD, tokens), BF16),
        ("cent_t", (heads, z.head, PAD), BF16), ("cnts", (z.count_rows, PAD), F32), ("cnt_out", (z.count_rows, PAD), F32),
        ("cnt_in", (others, z.count_rows, PAD), F32), ("dens", (heads, 8, PAD), F32),
        ("res_t", (heads, stack, PAD), BF16), ("rfac", (heads, 8, PAD), F32),
        ("u_s", (heads, stack, PAD), F32), ("body", (stack, tokens), BF16),
        ("sums_f", (pairs, PAD, PAD), F32),
        ("sums", (pairs,) + packed, BF16), ("sums_in", (others, pairs) + packed, BF16),
        ("big", (pairs, z.sent_docs) + packed, BF16),
        ("big_in", (others, pairs, z.sent_docs) + packed, BF16),
        ("small", (pairs, z.small_rows, PAD), F32), ("small_in", (others, pairs, z.small_rows, PAD), F32),
        ("g_send", (pairs, z.sent_docs) + packed, BF16),
        ("g_recv", (others, pairs, z.sent_docs) + packed, BF16),
        ("c_f", (pairs, PAD, PAD), F32), ("c_s", (pairs,) + packed, BF16),
        ("c_got", (others, pairs) + packed, BF16),
        ("low", (tokens, width), BF16), ("low_t", (width, tokens), BF16),
        ("act", rows, BF16), ("gp", rows, BF16),
        ("slope", (chunks, tokens, width), BF16),
        ("acc", (tokens, width), F32), ("acc_n", (tokens, width), F32), ("gm", (tokens, width), F32),
        ("ga_t", (width, tokens), BF16), ("gk_t", (width, tokens), BF16), ("gv_t", (width, tokens), BF16),
    ]
    sems = [("load", (4 + 2 * chunks,))]
    for n in ("i", "x", "c", "o", "y"):
        sems += [(n + "_send", (z.rows,)), (n + "_recv", (z.rows,))]
    for n in ("a", "b", "s", "g", "q"):
        sems += [(n + "_ss", (others, pairs)), (n + "_rs", (others, pairs))]
    sems += [("k_ss", (others,)), ("k_rs", (others,))]
    if z.fast:
        piece = (z.block, width)
        deep = z.seq // 2
        outs.append(("sum_ref", shape((3, z.dp) + piece, BF16), anywhere))
        scratch += [
            ("gat", (3, z.dp) + piece, BF16),
            ("d_down", (z.dp, z.seq) + piece, BF16), ("d_up", (z.dp, z.seq) + piece, BF16),
            ("core_in", (2, 2, z.seq) + piece, BF16), ("first_in", (2, z.seq) + piece, BF16),
            ("second_in", (3, deep) + piece, BF16), ("third_in", (3, deep) + piece, BF16),
            ("vec_buf", (3, 8, width), F32), ("vec_got", (z.seq + 1, 8, width), F32),
        ]
        sems += [
            ("dn_ss", (2, chunks)), ("dn_rs", (2, chunks)), ("co_ss", (2, 2)), ("co_rs", (2, 2)),
            ("f_ss", (3, 2, deep)), ("f_rs", (3, 2, deep)), ("n_ss", (3, deep)), ("n_rs", (3, deep)),
            ("t_ss", (3, deep)), ("t_rs", (3, deep)), ("w_ss", (3, 3)), ("w_rs", (3, 3)),
            ("v_ss", (z.seq + 1,)), ("v_rs", (z.seq + 1,)),
        ]
    else:
        outs += [
            ("d_qkvo", shape((4, width, width), BF16), anywhere),
            ("d_up", shape((chunks, width, width), BF16), vmem),
            ("d_down", shape((z.hidden, width), BF16), vmem),
        ]
    names = [n for n, _, _ in ins + outs + scratch] + [n for n, _ in sems]
    results = pl.pallas_call(
        functools.partial(block_kernel, z, names),
        out_shape=[s for _, s, _ in outs],
        in_specs=[s for _, _, s in ins],
        out_specs=[s for _, _, s in outs],
        scratch_shapes=[pltpu.VMEM(s, t) for _, s, t in scratch] + [dma(s) for _, s in sems],
        compiler_params=pltpu.CompilerParams(
            collective_id=0, has_side_effects=True, vmem_limit_bytes=VMEM_LIMIT
        ),
    )(*[v for _, v, _ in ins])

    out_back, grad_back, vectors = results[:3]
    if z.fast:
        flat = shape((z.block, width), F32)
        grid_rows = (z.rows, z.part, width)
        published = pl.pallas_call(
            functools.partial(publish_kernel, z),
            out_shape=[
                shape(grid_rows, F32), shape(grid_rows, F32), flat, flat, flat, flat,
                shape((z.block, z.hidden), F32), shape((z.hidden // z.seq, width), F32),
                shape((8, PAD), F32),
            ],
            in_specs=[anywhere] * 3 + [vmem],
            out_specs=[anywhere] * 8 + [vmem],
            scratch_shapes=[
                pltpu.VMEM((2,) + grid_rows, BF16), pltpu.VMEM((3, z.dp) + piece, BF16),
                pltpu.VMEM((2,) + grid_rows, F32), pltpu.VMEM((3, z.dp) + piece, F32),
                dma((2, z.rows)), dma((2, z.rows)), dma((3, z.dp)), dma((3, z.dp)),
            ],
            compiler_params=pltpu.CompilerParams(vmem_limit_bytes=VMEM_LIMIT),
        )(out_back, grad_back, results[3], vectors)
        out_full, grad_full, g_q, g_k, g_v, g_o, g_up, g_down, own = published
        own = own[:, : z.block]
        return (
            out_full, grad_full, own[0], own[1], g_q, g_k, g_v, g_o, own[2], own[3], g_up, g_down,
        )

    def share(v, dim):
        v = lax.psum_scatter(v.astype(F32), "seq", scatter_dimension=dim, tiled=True)
        return lax.psum(v, "dp")

    g_up = share(jnp.transpose(results[4], (1, 0, 2)).reshape(width, z.hidden), 0)
    g_qkvo, g_down, own = share(results[3], 1), share(results[5], 0), share(vectors, 1)
    return (
        out_back.astype(F32), grad_back.astype(F32), own[0], own[1],
        g_qkvo[0], g_qkvo[1], g_qkvo[2], g_qkvo[3], own[2], own[3], g_up, g_down,
    )


def solution(mesh):
    spread = P("dp", "seq", None)
    return jax.shard_map(
        functools.partial(local, dict(mesh.shape)),
        mesh=mesh,
        in_specs=(spread, spread, P("dp", None), spread) + (P(),) * 10,
        out_specs=(spread, spread, P("seq"), P("seq")) + (P("seq", None),) * 4
        + (P("seq"), P("seq"), P("seq", None), P("seq", None)),
        check_vma=False,
    )
```

```python
import functools

import jax
import jax.numpy as jnp
from jax import lax
from jax.experimental import pallas as pl
from jax.experimental.pallas import tpu as pltpu
from jax.sharding import PartitionSpec as P

CLUSTERS = 100
PAD = 128
EPSILON = 1e-05
GELU_A = 0.7978845608028654
GELU_B = 0.044715
MESH = pl.DeviceIdType.MESH
YF = ((True, False, True, True), (False, True, False, True), (True, True, True, False))
F32 = jnp.float32
BF16 = jnp.bfloat16
VMEM_LIMIT = 63 * 2**20


def schedule(order):
    def both(g, *ks):
        return [("one", g, k, o) for k in ks for o in range(2)]

    def two(g, *ks):
        return [("two", g, k) for k in ks]

    def side(g, o, *ks):
        return [("one", g, k, o) for k in ks]

    a, b, c, d = order
    forward = {a: [], b: [("down", a)], c: [("down", b)], d: [("down", c)]}
    mixed = [step for k in order for step in two(1, k) + both(2, k)]
    return (
        [forward[k] for k in range(4)],
        ([("down", d)], [], [("up", 0)] + both(0, a), [("up", 1)] + both(0, b)),
        [("up", 2)] + both(0, c),
        ((), (), (), (), (), [("up", 3)]),
        ((), (), (), (), (), both(0, d)),
        ((),) * 6,
        both(1, *order),
        [("part", 3), ("part", 1), ("part", 2), ("part", 0), ("vec", 1)] + two(0, *order) + mixed + [("vec", 2)] + two(2, *order)
        + [("three", 0), ("gather", 0), ("three", 1), ("gather", 1), ("three", 2), ("vec", 3), ("store", 0)]
        + [("store", 1), ("gather", 2), ("store", 2)],
        [],
        [],
    )


class Plan:
    def __init__(self, mesh_shape, inputs, clusters, lengths, w_up):
        self.seq, self.dp = mesh_shape["seq"], mesh_shape["dp"]
        self.rows, self.part, self.width = inputs.shape
        self.heads, self.docs, self.hidden = clusters.shape[2], lengths.shape[1], w_up.shape[1]
        self.head = self.width // self.heads
        self.tokens = self.rows * self.part
        self.mates = self.seq // self.rows
        self.sent_docs = 1 if self.mates == 2 else self.docs
        self.block = self.width // self.seq
        self.fast = (
            self.dp == 4 and self.seq == 8 and self.block % 16 == 0 and self.hidden == 4 * self.width
        )
        self.reduce = self.fast
        self.sent_rows = -(-CLUSTERS // 16) * 16
        self.small_rows = 8 if self.mates == 2 else 16
        self.count_rows = -(-self.heads // 8) * 8
        self.order = (0, 3, 1, 2)
        self.tasks = schedule(self.order)
        self.square = (self.seq, self.block, self.width) if self.fast else (self.width, self.width)
        self.y_first = [[w[self.order.index(k)] for k in range(4)] for w in YF]

    def place(self, j):
        return lax.rem(j, self.rows), j // self.rows

    def owner(self, r, h):
        return h * self.rows + r


def nn(a, b):
    return lax.dot_general(a, b, (((1,), (0,)), ((), ())), preferred_element_type=F32)


def nt(a, b):
    return lax.dot_general(a, b, (((1,), (1,)), ((), ())), preferred_element_type=F32)


def tn(a, b):
    return lax.dot_general(a, b, (((0,), (0,)), ((), ())), preferred_element_type=F32)


def remote(src, dst, send, recv, to):
    return pltpu.make_async_remote_copy(
        src_ref=src, dst_ref=dst, send_sem=send, recv_sem=recv, device_id=to, device_id_type=MESH
    )


def one_hot(row):
    ids = lax.broadcasted_iota(jnp.int32, (PAD, row.shape[1]), 0)
    return jnp.where(ids == row, 1.0, 0.0).astype(BF16)


def doc_masks(z, r, h, len_ref):
    pos = h * z.tokens + lax.broadcasted_iota(jnp.int32, (1, z.tokens), 1)
    seg = jnp.zeros((1, z.tokens), jnp.int32)
    end, ends = jnp.int32(0), []
    for s in range(z.docs):
        end = end + len_ref[r, s]
        ends.append(end)
        seg = seg + (pos >= end).astype(jnp.int32)
    last = sum((z.tokens - 1 >= e).astype(jnp.int32) for e in ends)
    first = sum((z.tokens >= e).astype(jnp.int32) for e in ends)
    spans = last == first
    mine = jnp.where(h == 0, last, first)
    return seg, spans, mine


def stacked_masks(z, seg):
    ids = lax.broadcasted_iota(jnp.int32, (z.docs * z.head, z.tokens), 0)
    body = jnp.where(ids // z.head == seg, 1.0, 0.0).astype(BF16)
    low = lax.broadcasted_iota(jnp.int32, (16, z.tokens), 0)
    tail = jnp.where((low % z.docs == seg) & (low < 2 * z.docs), 1.0, 0.0).astype(BF16)
    return body, tail


def pick_doc(z, blocks, mine):
    out = blocks[0]
    for s in range(1, z.docs):
        out = jnp.where(mine == s, blocks[s], out)
    return out


def mate_id(z, r, h, step):
    return {"seq": z.owner(r, lax.rem(h + step, z.mates))}


def rows_out(z, j, r, h, src, dst, send, recv):
    for row in range(z.rows):
        to = z.owner(row, h)

        @pl.when(to != j)
        def _():
            remote(src.at[row], dst.at[r], send.at[row], recv.at[r], {"seq": to}).start()

        @pl.when(to == j)
        def _():
            pltpu.make_async_copy(src.at[row], dst.at[r], recv.at[r]).start()


def rows_landed(z, j, h, src, dst, send, recv, slot):
    source = z.owner(slot, h)

    @pl.when(source == j)
    def _():
        pltpu.make_async_copy(src.at[0], dst.at[slot], recv.at[slot]).wait()

    @pl.when(source != j)
    def _():
        remote(src.at[0], dst.at[slot], send.at[0], recv.at[slot], {"seq": source}).wait_recv()


def rows_sent(z, j, h, src, dst, send, recv):
    for row in range(z.rows):
        to = z.owner(row, h)

        @pl.when(to != j)
        def _():
            remote(src.at[row], dst.at[0], send.at[row], recv.at[0], {"seq": to}).wait_send()


def norm_parts(values):
    average = jnp.mean(values, axis=-1, keepdims=True)
    centered = values - average
    inverse = lax.rsqrt(jnp.mean(centered * centered, axis=-1, keepdims=True) + EPSILON)
    return centered * inverse, inverse


def norm_back(grad, unit, inverse, gain):
    scaled = grad * gain
    inner = (
        scaled
        - jnp.mean(scaled, axis=-1, keepdims=True)
        - unit * jnp.mean(scaled * unit, axis=-1, keepdims=True)
    )
    return inner * inverse


def joined_masks(z, blocks, seg):
    out = blocks[: z.head]
    for s in range(1, z.docs):
        out = jnp.where(seg == s, blocks[s * z.head : (s + 1) * z.head], out)
    return out


class Refs:
    def __init__(self, names, values):
        self.__dict__.update(zip(names, values, strict=True))


def block_kernel(z, names, *values):
    f = Refs(names, values)
    j = lax.axis_index("seq")
    me = lax.axis_index("dp")
    r, h = z.place(j)
    width, part = z.width, z.part

    barrier = pltpu.get_barrier_semaphore()
    for d in range(1, z.seq):
        pl.semaphore_signal(
            barrier, 1, device_id={"seq": lax.rem(j + d, z.seq)}, device_id_type=MESH
        )
    greeted = z.seq - 1
    if z.reduce:
        for d in range(1, z.dp):
            pl.semaphore_signal(
                barrier, 1, device_id={"dp": lax.rem(me + d, z.dp)}, device_id_type=MESH
            )
        greeted += z.dp - 1

    loads = [
        pltpu.make_async_copy(ref, f.w_qkv.at[p], f.load.at[p])
        for p, ref in enumerate((f.wq_in, f.wk_in, f.wv_in))
    ]
    loads.append(pltpu.make_async_copy(f.wo_in, f.w_o, f.load.at[3]))
    chunks = z.hidden // width
    for c in range(chunks):
        loads.append(
            pltpu.make_async_copy(
                f.up_in.at[(slice(None),) * (len(z.square) - 1) + (pl.ds(c * width, width),)],
                f.w_up.at[c],
                f.load.at[4 + c],
            )
        )
        loads.append(
            pltpu.make_async_copy(f.down_in.at[c], f.w_down.at[c], f.load.at[4 + chunks + c])
        )
    for copy in loads[:3]:
        copy.start()

    seg, spans, mine = doc_masks(z, r, h, f.lengths)
    body_value, tail = stacked_masks(z, seg)
    f.body[...] = body_value
    gain_attn, bias_attn = f.gain_attn[...].reshape(1, width), f.bias_attn[...].reshape(1, width)
    gain_ffn, bias_ffn = f.gain_ffn[...].reshape(1, width), f.bias_ffn[...].reshape(1, width)
    pl.semaphore_wait(barrier, greeted)

    def clu_copy(step):
        to = {"seq": z.owner(lax.rem(r + step, z.rows), h)}
        return remote(f.clu_in, f.clu_got.at[step], f.i_send.at[step], f.i_recv.at[step], to)

    own_clu = pltpu.make_async_copy(f.clu_in, f.clu_got.at[0], f.i_recv.at[0])
    own_clu.start()
    for step in range(1, z.rows):
        clu_copy(step).start()
    rows_out(z, j, r, h, f.x_in, f.xrow, f.x_send, f.x_recv)
    for copy in loads[3:]:
        copy.start()

    def part_rows(t):
        return pl.ds(pl.multiple_of(t * part, part), part)

    def head_rows(i):
        return pl.ds(pl.multiple_of(i * z.head, z.head), z.head)

    own_clu.wait()
    for step in range(z.rows):
        if step:
            clu_copy(step).wait()
        slot = lax.rem(r + z.rows - step, z.rows)
        numbers = f.clu_got[step, :, pl.ds(r, 1), :].reshape(z.heads, part)
        f.clus[:, part_rows(slot)] = numbers

    def mate_copy(src, dst, send, recv, i, step):
        to = {"seq": z.owner(r, lax.rem(h + step, z.mates))}
        return remote(src.at[i], dst.at[step - 1, i], send.at[step - 1, i], recv.at[step - 1, i], to)

    def sum_copy(i, step):
        return mate_copy(f.sums, f.sums_in, f.a_ss, f.a_rs, i, step)

    def result_copies(i, step):
        return (
            mate_copy(f.big, f.big_in, f.b_ss, f.b_rs, i, step),
            mate_copy(f.small, f.small_in, f.s_ss, f.s_rs, i, step),
        )

    def grad_copy(i, step):
        return mate_copy(f.g_send, f.g_recv, f.g_ss, f.g_rs, i, step)

    def cent_copy(i, step):
        return mate_copy(f.c_s, f.c_got, f.q_ss, f.q_rs, i, step)

    others = range(1, z.mates)
    stack = z.docs * z.head
    pairs = z.heads // 2
    low_lanes = z.sent_rows

    def pack(pair):
        return pair.astype(BF16).T[:low_lanes]

    def unpack(packed):
        rest = jnp.zeros((PAD - low_lanes, PAD), BF16)
        return jnp.concatenate([packed, rest], axis=0).T.astype(F32)

    def member_of(i):
        return one_hot(f.clus[pl.ds(i, 1), :])

    ones = jnp.ones((8, z.tokens), BF16)
    f.cnt_out[...] = jnp.zeros_like(f.cnt_out)
    for i in range(z.heads):
        f.cnt_out[i : i + 1] = nt(ones, one_hot(f.clus[i : i + 1, :]))[:1]

    def count_copy(step):
        to = {"seq": z.owner(r, lax.rem(h + step, z.mates))}
        return remote(f.cnt_out, f.cnt_in.at[step - 1], f.k_ss.at[step - 1], f.k_rs.at[step - 1], to)

    for step in others:
        count_copy(step).start()
    for copy in loads[:3]:
        copy.wait()

    def project(slot, carry):
        rows_landed(z, j, h, f.x_in, f.xrow, f.x_send, f.x_recv, slot)
        unit, _ = norm_parts(f.xrow[slot].astype(F32))
        normed = (unit * gain_attn + bias_attn).astype(BF16)
        f.low[part_rows(slot), :] = normed
        f.n_t[:, part_rows(slot)] = normed.T
        f.q_t[:, part_rows(slot)] = nn(normed, f.w_qkv[0]).astype(BF16).T
        return carry

    lax.fori_loop(0, z.rows, project, 0)

    def cluster_sums(i, carry):
        pair = jnp.concatenate(
            [nt(f.q_t[head_rows(2 * i + a), :], member_of(2 * i + a)) for a in range(2)], axis=0
        )
        f.sums_f[i] = pair
        f.sums[i] = pack(pair)
        for step in others:
            sum_copy(i, step).start()
        return carry

    lax.fori_loop(0, pairs, cluster_sums, 0)
    rows_sent(z, j, h, f.x_in, f.xrow, f.x_send, f.x_recv)
    rows_out(z, j, r, h, f.c_in, f.crow, f.c_send, f.c_recv)
    counts = f.cnt_out[...]
    for step in others:
        count_copy(step).wait()
        counts = counts + f.cnt_in[step - 1]
    f.cnts[...] = jnp.maximum(counts, 1.0)

    def project_more(t, carry):
        rows = pl.ds(pl.multiple_of(t * 2 * part, 2 * part), 2 * part)
        normed = f.low[rows, :]
        f.k_t[:, rows] = nn(normed, f.w_qkv[1]).astype(BF16).T
        f.v_t[:, rows] = nn(normed, f.w_qkv[2]).astype(BF16).T
        return carry

    lax.fori_loop(0, z.rows // 2, project_more, 0)

    def masked_values(i):
        return jnp.concatenate([f.v_t[head_rows(i), :]] * z.docs, axis=0) * f.body[...]

    def doc_rows(blocks, s):
        return blocks[s * z.head : (s + 1) * z.head]

    def border(blocks):
        if z.mates == 2:
            parts = [[doc_rows(b, s) for s in range(z.docs)] for b in blocks]
            return [pack(jnp.concatenate([pick_doc(z, p, mine) for p in parts], axis=0))]
        return [
            pack(jnp.concatenate([doc_rows(b, s) for b in blocks], axis=0)) for s in range(z.docs)
        ]

    def attend(i, carry):
        total = f.sums_f[i]
        for step in others:
            sum_copy(i, step).wait()
            total = total + unpack(f.sums_in[step - 1, i])
        blocks, small = [], []
        for a in range(2):
            n = 2 * i + a
            count = f.cnts[pl.ds(n, 1), :]
            cent = (total[a * z.head : (a + 1) * z.head] / count).astype(BF16)
            f.cent_t[n] = cent
            scores = tn(cent, f.k_t[head_rows(n), :]) * 0.125
            top = jnp.max(scores, axis=1, keepdims=True)
            weights = jnp.exp(scores - top).astype(BF16)
            f.wts[n] = weights
            both = nt(jnp.concatenate([masked_values(n), tail], axis=0), weights)
            f.u_s[n] = both[:stack]
            top_row = jnp.broadcast_to(top, (PAD, PAD)).T
            denoms = both[stack : stack + 4]
            f.dens[n] = jnp.concatenate([denoms, top_row[:4]], axis=0)
            blocks.append(both[:stack])
            if z.mates == 2:
                own = pick_doc(z, [denoms[s : s + 1] for s in range(z.docs)], mine)
                small += [jnp.broadcast_to(own, (2, PAD)), top_row[:2]]
            else:
                small += [denoms, top_row[:4]]
        f.small[i] = jnp.concatenate(small, axis=0)
        for d, packed in enumerate(border(blocks)):
            f.big[i, d] = packed
        for step in others:
            for copy in result_copies(i, step):
                copy.start()
        return carry

    lax.fori_loop(0, pairs, attend, 0)
    empty = [jnp.where(jnp.sum((seg == s).astype(F32)) > 0.5, 0.0, 1.0) for s in range(z.docs)]
    half_small = z.small_rows // 2

    def finish(i, carry):
        got = []
        for step in others:
            for copy in result_copies(i, step):
                copy.wait()
            got.append([unpack(f.big_in[step - 1, i, d]) for d in range(z.sent_docs)])
        for a in range(2):
            n = 2 * i + a
            own = f.dens[n]
            top, highest = own[4:5], own[4:5]
            sides = []
            for step in others:
                side = f.small_in[step - 1, i, a * half_small : (a + 1) * half_small]
                sides.append((side, side[half_small // 2 : half_small // 2 + 1]))
                highest = jnp.maximum(highest, sides[-1][1])
            scale = jnp.exp(top - highest)
            scaled, factors = [], []
            for s in range(z.docs):
                piece = f.u_s[n, s * z.head : (s + 1) * z.head]
                denom = own[s : s + 1]
                joined, joined_denom = piece * scale, denom * scale
                d = 0 if z.mates == 2 else s
                for other, (side, side_top) in zip(got, sides):
                    side_scale = jnp.exp(side_top - highest)
                    joined = joined + other[d][a * z.head : (a + 1) * z.head] * side_scale
                    joined_denom = joined_denom + side[d : d + 1] * side_scale
                here = jnp.logical_and(spans, mine == s) if z.mates == 2 else True
                joined = jnp.where(here, joined, piece)
                joined_denom = jnp.where(here, joined_denom, denom)
                factor = jnp.where(here, scale, jnp.ones_like(scale))
                joined_denom = joined_denom + jnp.where(joined_denom > 0.0, 0.0, empty[s])
                inverse = 1.0 / joined_denom
                scaled.append((joined * inverse).astype(BF16))
                factors.append(inverse * factor)
            result = jnp.concatenate(scaled, axis=0)
            f.res_t[n] = result
            f.rfac[n] = jnp.concatenate(factors + [jnp.zeros((8 - z.docs, PAD), F32)], axis=0)
            f.att_t[head_rows(n), :] = joined_masks(z, nn(result, member_of(n)), seg).astype(BF16)
        return carry

    lax.fori_loop(0, pairs, finish, 0)

    core, y = lax.rem(me, 2), me // 2
    xx, zz = lax.rem(j, 2), j // 2
    sibling, across = me + 1 - 2 * core, me + 2 - 4 * y
    beside = j + 1 - 2 * xx
    deep = z.seq // 2
    if z.reduce:
        grads = (f.d_down, f.d_up, f.w_up)
        core_in = (f.core_in.at[0], f.core_in.at[1], f.w_down.at[pl.ds(0, 2)])
        first_in = (f.first_in.at[0], f.first_in.at[1], f.w_down.at[2])

    def add(ref, value):
        ref[...] = ref[...] + value

    def block(g, yp, xb, k):
        return core_in[g].at[yp, 2 * k + xb]

    def grad_block(g, p, b):
        return grads[g][p, b]

    def down_core(yp, c):
        src = f.d_down.at[yp * 2 + 1 - core, pl.ds(2 * c, 2)]
        dst = core_in[0].at[yp, pl.ds(2 * c, 2)]
        return remote(src, dst, f.dn_ss.at[yp, c], f.dn_rs.at[yp, c], {"dp": sibling})

    def part_core(g, p):
        yp = p // 2
        if g == 1:
            src, dst = f.d_up.at[p], core_in[1].at[yp]
        else:
            src, dst = f.w_up.at[p], f.w_down.at[yp]
        return remote(src, dst, f.co_ss.at[g - 1, yp], f.co_rs.at[g - 1, yp], {"dp": sibling})

    def y_first(g, k):
        return z.y_first[g][k]

    def step_one(g, k, other):
        if y_first(g, k):
            src, to = block(g, 1 - y, other, k), {"dp": across}
        else:
            src, to = block(g, other, 1 - xx, k), {"seq": beside}
        dst = first_in[g].at[other * deep + k]
        return remote(src, dst, f.f_ss.at[g, other, k], f.f_rs.at[g, other, k], to)

    def step_two(g, k):
        if y_first(g, k):
            src, to = block(g, y, 1 - xx, k), {"seq": beside}
        else:
            src, to = block(g, 1 - y, xx, k), {"dp": across}
        return remote(src, f.second_in.at[g, k], f.n_ss.at[g, k], f.n_rs.at[g, k], to)

    def one_done(g, k, other):
        if y_first(g, k):
            own, far = block(g, y, other, k), xx != other
        else:
            own, far = block(g, other, xx, k), y != other
        step_one(g, k, other).wait_recv()
        add(own, first_in[g][other * deep + k])
        pl.when(far)(lambda: step_two(g, k).start())


    def step_three(g, k):
        return remote(
            block(g, y, xx, k), f.third_in.at[g, zz], f.t_ss.at[g, k], f.t_rs.at[g, zz],
            {"seq": 2 * k + xx},
        )

    def two_done(g, k):
        step_two(g, k).wait_recv()
        add(block(g, y, xx, k), f.second_in[g, k])

        @pl.when(zz != k)
        def _():
            step_three(g, k).start()

    def gather_copy(g, kind):
        src = across if kind == 2 else me
        to = {"dp": across if kind == 1 else sibling}
        ref = f.gat.at[g, src]
        return remote(ref, ref, f.w_ss.at[g, kind], f.w_rs.at[g, kind], to)

    def three_done(g):
        total = core_in[g][y, j].astype(F32)
        for k in range(1, deep):
            source = lax.rem(zz + k, deep)
            remote(
                block(g, y, xx, zz), f.third_in.at[g, source], f.t_ss.at[g, source],
                f.t_rs.at[g, source], {"seq": 2 * source + xx},
            ).wait_recv()
            total = total + f.third_in[g, source].astype(F32)
        f.gat[g, me] = total.astype(BF16)
        gather_copy(g, 1).start()
        gather_copy(g, 0).start()

    def gather_wait(g, kind):
        source = (sibling, across, across + sibling - me)[kind]
        ref = f.gat.at[g, source]
        to = {"dp": across if kind == 1 else sibling}
        remote(ref, ref, f.w_ss.at[g, kind], f.w_rs.at[g, kind], to).wait_recv()

    def gather_done(g):
        gather_wait(g, 1)
        gather_copy(g, 2).start()

    def store_copy(g):
        return pltpu.make_async_copy(f.gat.at[g], f.sum_ref.at[g], f.load.at[g])

    def store(g):
        gather_wait(g, 0)
        gather_wait(g, 2)
        store_copy(g).start()

    def part_done(g, p):
        yp = p // 2
        part_core(g, p).wait_recv()

        def body(b, carry):
            add(core_in[g].at[yp, b], grad_block(g, p, b))
            return carry

        lax.fori_loop(0, z.seq, body, 0)
        for k in z.order:
            if y_first(g, k):

                @pl.when(yp != y)
                def _():
                    step_one(g, k, 1 - xx).start()
                    step_one(g, k, xx).start()
            else:
                step_one(g, k, yp).start()

    def down_done(c):
        for yp in range(2):
            down_core(yp, c).wait_recv()
            for xb in range(2):
                add(block(0, yp, xb, c), f.d_down[yp * 2 + core, 2 * c + xb])
            if y_first(0, c):

                @pl.when(yp != y)
                def _():
                    step_one(0, c, 1 - xx).start()
                    step_one(0, c, xx).start()
            else:
                step_one(0, c, yp).start()

    def vec_copy(t, to):
        return remote(f.vec_buf.at[min(t, 2)], f.vec_got.at[t], f.v_ss.at[t], f.v_rs.at[t], to)

    def vec_step(t):
        if t == 1:
            vec_copy(0, {"dp": sibling}).wait()
            f.vec_buf[1] = f.vec_buf[0] + f.vec_got[0]
            vec_copy(1, {"dp": across}).start()
            return
        if t == 2:
            vec_copy(1, {"dp": across}).wait()
            f.vec_buf[2] = f.vec_buf[1] + f.vec_got[1]
        total = f.vec_buf[2]
        for d in range(1, z.seq):
            copy = vec_copy(1 + d, {"seq": lax.rem(j + d, z.seq)})
            if t == 2:
                copy.start()
            else:
                copy.wait()
                total = total + f.vec_got[1 + d]
        if t == 3:
            f.vec_ref[...] = total

    def part_step(p):
        pl.when(core == p % 2)(lambda: part_done(2, p))

    def up_step(c):
        pl.when(c % 2 == core)(lambda: part_done(1, c))

    steps = {
        "down": down_done, "store": store,
        "one": one_done, "two": two_done, "three": three_done, "gather": gather_done,
        "vec": vec_step, "part": part_step, "up": up_step,
    }

    def run(tasks):
        for name, *numbers in tasks:
            steps[name](*numbers)

    def serve(i, table):
        if z.reduce:
            for at, tasks in enumerate(table):
                if tasks:
                    pl.when(i == at)(functools.partial(run, tasks))

    for copy in loads[3:]:
        copy.wait()

    def first(t, carry):
        size = 2 * part
        rows = pl.ds(pl.multiple_of(t * size, size), size)
        values = f.xrow[pl.ds(2 * t, 2)].reshape(size, width).astype(F32)
        middle = values + tn(f.att_t[:, rows], f.w_o[...])
        f.acc[rows, :] = middle
        f.gm[rows, :] = middle
        unit, _ = norm_parts(middle)
        normed = (unit * gain_ffn + bias_ffn).astype(BF16)
        f.low[rows, :] = normed
        f.low_t[:, rows] = normed.T
        f.acc_n[rows, :] = jnp.zeros((size, width), F32)
        return carry

    lax.fori_loop(0, z.rows // 2, first, 0)
    for slot in range(z.rows):
        rows_landed(z, j, h, f.c_in, f.crow, f.c_send, f.c_recv, slot)
    rows_sent(z, j, h, f.c_in, f.crow, f.c_send, f.c_recv)
    halves = z.rows // 2

    halves_of = [slice(t * halves, (t + 1) * halves) for t in range(2)]
    rows_of = [slice(t * halves * part, (t + 1) * halves * part) for t in range(2)]

    def ffn_chunk(c, carry):
        w_up, w_down = f.w_up[c].reshape(width, width), f.w_down[c].reshape(width, width)
        for t in range(2):
            rows, own = rows_of[t], halves_of[t]
            u = nn(f.low[rows, :], w_up)
            tanh = jnp.tanh(GELU_A * (u + GELU_B * (u * u * u)))
            cdf = 0.5 * (1.0 + tanh)
            f.act[own] = (u * cdf).astype(BF16).reshape(halves, part, width)
            slope = cdf + (0.5 * GELU_A) * u * (1.0 - tanh * tanh) * (1.0 + (3.0 * GELU_B) * (u * u))
            f.slope[c, rows, :] = slope.astype(BF16)
            f.acc[rows, :] += nn(f.act[own].reshape(halves * part, width), w_down)
        down = tn(
            f.act[...].reshape(z.tokens, width), f.crow[...].reshape(z.tokens, width)
        ).astype(BF16)
        if z.fast:
            for b in range(2):
                for p in range(z.dp):
                    at = (b * z.dp + p) * z.block
                    f.d_down[p, 2 * c + b] = down[at : at + z.block]
        else:
            f.d_down[pl.ds(pl.multiple_of(c * width, width), width), :] = down
        if z.reduce:
            run(z.tasks[0][c])
            for yp in range(2):
                down_core(yp, c).start()
        return carry

    def back_chunk(c, carry):
        w_up, w_down = f.w_up[c].reshape(width, width), f.w_down[c].reshape(width, width)
        for t in range(2):
            rows, own = rows_of[t], halves_of[t]
            grad = nt(f.crow[own].reshape(halves * part, width), w_down)
            f.gp[own] = (grad * f.slope[c, rows, :].astype(F32)).astype(BF16).reshape(halves, part, width)
            f.acc_n[rows, :] += nt(f.gp[own].reshape(halves * part, width), w_up)
        up = nn(f.low_t[...], f.gp[...].reshape(z.tokens, width)).astype(BF16)
        f.d_up[c] = up.reshape(f.d_up.shape[1:])
        if z.reduce:
            run(z.tasks[1][c])
            pl.when(c % 2 != core)(lambda: part_core(1, c).start())
        return carry

    def each_chunk(body, order):
        if z.reduce:
            for c in order:
                body(c, 0)
        else:
            lax.fori_loop(0, chunks, body, 0)

    each_chunk(ffn_chunk, z.order)

    def ffn_out(t, carry):
        f.act[t] = f.acc[part_rows(t), :].astype(BF16)
        return carry

    lax.fori_loop(0, z.rows, ffn_out, 0)
    rows_out(z, j, r, h, f.act, f.out_ref, f.o_send, f.o_recv)
    each_chunk(back_chunk, range(chunks))

    def ffn_back(t, carry):
        rows = part_rows(t)
        unit, inverse = norm_parts(f.gm[rows, :])
        grad = f.acc_n[rows, :]
        grad_middle = f.crow[t].astype(F32) + norm_back(grad, unit, inverse, gain_ffn)
        f.gm[rows, :] = grad_middle
        f.low[rows, :] = grad_middle.astype(BF16)
        return (
            carry[0] + jnp.sum(grad * unit, axis=0, keepdims=True),
            carry[1] + jnp.sum(grad, axis=0, keepdims=True),
        )

    zero = jnp.zeros((1, width), F32)
    sums_ffn = lax.fori_loop(0, z.rows, ffn_back, (zero, zero))
    f.ga_t[...] = nt(f.w_o[...], f.low[...]).astype(BF16)

    if z.reduce:
        run(z.tasks[2])

    def gather_grads(i, carry):
        blocks = []
        for a in range(2):
            n = 2 * i + a
            masked = jnp.concatenate([f.ga_t[head_rows(n), :]] * z.docs, axis=0) * f.body[...]
            blocks.append(nt(masked, member_of(n)))
            f.u_s[n] = blocks[-1]
        for d, packed in enumerate(border(blocks)):
            f.g_send[i, d] = packed
        for step in others:
            grad_copy(i, step).start()
        serve(i, z.tasks[3])
        return carry

    lax.fori_loop(0, pairs, gather_grads, 0)
    f.w_up[3] = nn(f.att_t[...], f.low[...]).astype(BF16).reshape(z.square)
    if z.reduce:
        pl.when(core == 0)(lambda: part_core(2, 3).start())

    def attend_back(i, carry):
        serve(i, z.tasks[4])
        got = []
        for step in others:
            grad_copy(i, step).wait()
            got.append([unpack(f.g_recv[step - 1, i, d]) for d in range(z.sent_docs)])
        cents = []
        for a in range(2):
            n = 2 * i + a
            result, factor = f.res_t[n], f.rfac[n]
            lows, deltas = [], []
            for s in range(z.docs):
                grad = f.u_s[n, s * z.head : (s + 1) * z.head]
                joined = grad
                for other in got:
                    piece = other[0 if z.mates == 2 else s]
                    joined = joined + piece[a * z.head : (a + 1) * z.head]
                if z.mates == 2:
                    joined = jnp.where(jnp.logical_and(spans, mine == s), joined, grad)
                scaled = joined * factor[s : s + 1]
                lows.append(scaled.astype(BF16))
                piece = doc_rows(result, s).astype(F32)
                deltas.append(-jnp.sum(scaled * piece, axis=0, keepdims=True))
            delta = jnp.concatenate(deltas, axis=0)
            high = delta.astype(BF16).astype(F32)
            small = jnp.concatenate(
                [high, delta - high, jnp.zeros((16 - 2 * z.docs, PAD), F32)], axis=0
            ).astype(BF16)
            low = jnp.concatenate(lows, axis=0)
            diff = tn(
                jnp.concatenate([low, small], axis=0),
                jnp.concatenate([masked_values(n), tail], axis=0),
            )
            weights = f.wts[n]
            raw = (0.125 * (weights.astype(F32) * diff)).astype(BF16)
            f.gk_t[head_rows(n), :] = nn(f.cent_t[n], raw).astype(BF16)
            f.gv_t[head_rows(n), :] = joined_masks(z, nn(low, weights), seg).astype(BF16)
            cents.append(nt(f.k_t[head_rows(n), :], raw))
        pair = jnp.concatenate(cents, axis=0)
        f.c_f[i] = pair
        f.c_s[i] = pack(pair)
        for step in others:
            cent_copy(i, step).start()
        return carry

    lax.fori_loop(0, pairs, attend_back, 0)
    if z.reduce:
        run(z.tasks[8])

    def weight_grad(p, g_ref):
        f.w_up[p] = nt(f.n_t[...], g_ref[...]).astype(BF16).reshape(z.square)
        if z.reduce:
            pl.when(p % 2 != core)(lambda: part_core(2, p).start())

    weight_grad(1, f.gk_t)
    weight_grad(2, f.gv_t)

    def query_back(i, carry):
        total = f.c_f[i]
        for step in others:
            cent_copy(i, step).wait()
            total = total + unpack(f.c_got[step - 1, i])
        for a in range(2):
            n = 2 * i + a
            low = (total[a * z.head : (a + 1) * z.head] / f.cnts[pl.ds(n, 1), :]).astype(BF16)
            f.q_t[head_rows(n), :] = nn(low, member_of(n)).astype(BF16)
        serve(i, z.tasks[5])
        return carry

    lax.fori_loop(0, pairs, query_back, 0)
    if z.reduce:
        run(z.tasks[9])
    weight_grad(0, f.q_t)

    if z.reduce:
        run(z.tasks[6])

    total = (
        nn(f.w_qkv[0], f.q_t[...]) + nn(f.w_qkv[1], f.gk_t[...]) + nn(f.w_qkv[2], f.gv_t[...])
    )
    f.acc[...] = total.T

    def attn_back(t, carry):
        rows = part_rows(t)
        unit, inverse = norm_parts(f.xrow[t].astype(F32))
        grad = f.acc[rows, :]
        f.gp[t] = (f.gm[rows, :] + norm_back(grad, unit, inverse, gain_attn)).astype(BF16)
        return (
            carry[0] + jnp.sum(grad * unit, axis=0, keepdims=True),
            carry[1] + jnp.sum(grad, axis=0, keepdims=True),
        )

    sums_attn = lax.fori_loop(0, z.rows, attn_back, (zero, zero))
    rows_out(z, j, r, h, f.gp, f.gx_ref, f.y_send, f.y_recv)
    vectors = jnp.concatenate([*sums_attn, *sums_ffn, jnp.zeros((4, width), F32)], axis=0)

    if z.reduce:
        f.vec_buf[0] = vectors
        vec_copy(0, {"dp": sibling}).start()
        run(z.tasks[7])
        for g in range(3):
            store_copy(g).wait()
            for kind in range(3):
                gather_copy(g, kind).wait_send()
            for k in range(deep):
                for other in range(2):
                    step_one(g, k, other).wait_send()
                step_two(g, k).wait_send()
                pl.when(zz != k)(lambda k=k, g=g: step_three(g, k).wait_send())

        for yp in range(2):
            for c in range(chunks):
                down_core(yp, c).wait_send()
            for g in (1, 2):
                part_core(g, yp * 2 + 1 - core).wait_send()
    else:
        f.vec_ref[...] = vectors
        if not z.fast:
            copy = pltpu.make_async_copy(f.w_up, f.d_qkvo, f.load.at[0])
            copy.start()
            copy.wait()

    for slot in range(z.rows):
        rows_landed(z, j, h, f.act, f.out_ref, f.o_send, f.o_recv, slot)
        rows_landed(z, j, h, f.gp, f.gx_ref, f.y_send, f.y_recv, slot)
    rows_sent(z, j, h, f.act, f.out_ref, f.o_send, f.o_recv)
    rows_sent(z, j, h, f.gp, f.gx_ref, f.y_send, f.y_recv)


def publish_kernel(
    z, rows_a, rows_b, sums, vectors, out_a, out_b, w_q, w_k, w_v, w_o, w_up, w_down, own,
    rows_in, sums_in, rows_wide, sums_wide, r_in, r_out, s_in, s_out,
):
    pieces = []
    for a, (src, dst) in enumerate(((rows_a, out_a), (rows_b, out_b))):
        for t in range(z.rows):
            pieces.append(
                (src.at[t], rows_in.at[a, t], rows_wide.at[a, t], dst.at[t], r_in.at[a, t], r_out.at[a, t])
            )
    for g in range(3):
        for p in range(z.dp):
            if g == 0:
                dst = w_down.at[pl.ds(p * z.block, z.block), :]
            elif g == 1:
                dst = w_up.at[:, pl.ds(p * z.width, z.width)]
            else:
                dst = (w_q, w_k, w_v, w_o)[p]
            pieces.append(
                (sums.at[g, p], sums_in.at[g, p], sums_wide.at[g, p], dst, s_in.at[g, p], s_out.at[g, p])
            )
    for src, low, _, _, sem, _ in pieces:
        pltpu.make_async_copy(src, low, sem).start()
    for src, low, wide, dst, sem, done in pieces:
        pltpu.make_async_copy(src, low, sem).wait()
        wide[...] = low[...].astype(F32)
        pltpu.make_async_copy(wide, dst, done).start()
    first = lax.axis_index("seq") * z.block
    rows = lax.broadcasted_iota(jnp.int32, (z.width, PAD), 0)
    lanes = lax.broadcasted_iota(jnp.int32, (z.width, PAD), 1)
    pick = jnp.where(rows == lanes + first, 1.0, 0.0)
    own[...] = jnp.dot(
        vectors[...], pick, precision=lax.Precision.HIGHEST, preferred_element_type=F32
    )
    for _, _, wide, dst, _, done in pieces:
        pltpu.make_async_copy(wide, dst, done).wait()


def local(
    mesh_shape,
    inputs, cotangent, lengths, clusters, gain_attn, bias_attn, w_query, w_key, w_value, w_out,
    gain_ffn, bias_ffn, w_up, w_down,
):
    z = Plan(mesh_shape, inputs, clusters, lengths, w_up)
    width, tokens, heads, docs = z.width, z.tokens, z.heads, z.docs
    others, stack, chunks = z.mates - 1, z.docs * z.head, z.hidden // z.width
    anywhere = pl.BlockSpec(memory_space=pl.ANY)
    vmem = pl.BlockSpec(memory_space=pltpu.VMEM)
    smem = pl.BlockSpec(memory_space=pltpu.SMEM)
    dma = pltpu.SemaphoreType.DMA
    shape = jax.ShapeDtypeStruct
    turned = jnp.transpose(clusters, (2, 0, 1))
    rows = (z.rows, z.part, width)

    ins = [
        ("x_in", inputs, anywhere), ("c_in", cotangent, anywhere), ("clu_in", turned, anywhere),
        ("lengths", lengths, smem), ("gain_attn", gain_attn, vmem), ("bias_attn", bias_attn, vmem),
        ("gain_ffn", gain_ffn, vmem), ("bias_ffn", bias_ffn, vmem),
        ("wq_in", w_query, anywhere), ("wk_in", w_key, anywhere), ("wv_in", w_value, anywhere),
        ("wo_in", w_out, anywhere), ("up_in", w_up.reshape(z.square[:-1] + (z.hidden,)), anywhere),
        ("down_in", w_down.reshape((chunks,) + z.square), anywhere),
    ]
    outs = [
        ("out_ref", shape(rows, BF16), anywhere), ("gx_ref", shape(rows, BF16), anywhere),
        ("vec_ref", shape((8, width), F32), vmem),
    ]
    pairs, packed = heads // 2, (z.sent_rows, PAD)
    scratch = [
        ("w_qkv", (3, width, width), BF16), ("w_o", (width, width), BF16),
        ("w_up", (chunks,) + z.square, BF16), ("w_down", (chunks,) + z.square, BF16),
        ("xrow", rows, BF16), ("crow", rows, BF16),
        ("clu_got", (z.rows, heads, z.rows, z.part), jnp.int32), ("clus", (heads, tokens), jnp.int32),
        ("n_t", (width, tokens), BF16), ("q_t", (width, tokens), BF16),
        ("k_t", (width, tokens), BF16), ("v_t", (width, tokens), BF16),
        ("att_t", (width, tokens), BF16), ("wts", (heads, PAD, tokens), BF16),
        ("cent_t", (heads, z.head, PAD), BF16), ("cnts", (z.count_rows, PAD), F32), ("cnt_out", (z.count_rows, PAD), F32),
        ("cnt_in", (others, z.count_rows, PAD), F32), ("dens", (heads, 8, PAD), F32),
        ("res_t", (heads, stack, PAD), BF16), ("rfac", (heads, 8, PAD), F32),
        ("u_s", (heads, stack, PAD), F32), ("body", (stack, tokens), BF16),
        ("sums_f", (pairs, PAD, PAD), F32),
        ("sums", (pairs,) + packed, BF16), ("sums_in", (others, pairs) + packed, BF16),
        ("big", (pairs, z.sent_docs) + packed, BF16),
        ("big_in", (others, pairs, z.sent_docs) + packed, BF16),
        ("small", (pairs, z.small_rows, PAD), F32), ("small_in", (others, pairs, z.small_rows, PAD), F32),
        ("g_send", (pairs, z.sent_docs) + packed, BF16),
        ("g_recv", (others, pairs, z.sent_docs) + packed, BF16),
        ("c_f", (pairs, PAD, PAD), F32), ("c_s", (pairs,) + packed, BF16),
        ("c_got", (others, pairs) + packed, BF16),
        ("low", (tokens, width), BF16), ("low_t", (width, tokens), BF16),
        ("act", rows, BF16), ("gp", rows, BF16),
        ("slope", (chunks, tokens, width), BF16),
        ("acc", (tokens, width), F32), ("acc_n", (tokens, width), F32), ("gm", (tokens, width), F32),
        ("ga_t", (width, tokens), BF16), ("gk_t", (width, tokens), BF16), ("gv_t", (width, tokens), BF16),
    ]
    sems = [("load", (4 + 2 * chunks,))]
    for n in ("i", "x", "c", "o", "y"):
        sems += [(n + "_send", (z.rows,)), (n + "_recv", (z.rows,))]
    for n in ("a", "b", "s", "g", "q"):
        sems += [(n + "_ss", (others, pairs)), (n + "_rs", (others, pairs))]
    sems += [("k_ss", (others,)), ("k_rs", (others,))]
    if z.fast:
        piece = (z.block, width)
        deep = z.seq // 2
        outs.append(("sum_ref", shape((3, z.dp) + piece, BF16), anywhere))
        scratch += [
            ("gat", (3, z.dp) + piece, BF16),
            ("d_down", (z.dp, z.seq) + piece, BF16), ("d_up", (z.dp, z.seq) + piece, BF16),
            ("core_in", (2, 2, z.seq) + piece, BF16), ("first_in", (2, z.seq) + piece, BF16),
            ("second_in", (3, deep) + piece, BF16), ("third_in", (3, deep) + piece, BF16),
            ("vec_buf", (3, 8, width), F32), ("vec_got", (z.seq + 1, 8, width), F32),
        ]
        sems += [
            ("dn_ss", (2, chunks)), ("dn_rs", (2, chunks)), ("co_ss", (2, 2)), ("co_rs", (2, 2)),
            ("f_ss", (3, 2, deep)), ("f_rs", (3, 2, deep)), ("n_ss", (3, deep)), ("n_rs", (3, deep)),
            ("t_ss", (3, deep)), ("t_rs", (3, deep)), ("w_ss", (3, 3)), ("w_rs", (3, 3)),
            ("v_ss", (z.seq + 1,)), ("v_rs", (z.seq + 1,)),
        ]
    else:
        outs += [
            ("d_qkvo", shape((4, width, width), BF16), anywhere),
            ("d_up", shape((chunks, width, width), BF16), vmem),
            ("d_down", shape((z.hidden, width), BF16), vmem),
        ]
    names = [n for n, _, _ in ins + outs + scratch] + [n for n, _ in sems]
    results = pl.pallas_call(
        functools.partial(block_kernel, z, names),
        out_shape=[s for _, s, _ in outs],
        in_specs=[s for _, _, s in ins],
        out_specs=[s for _, _, s in outs],
        scratch_shapes=[pltpu.VMEM(s, t) for _, s, t in scratch] + [dma(s) for _, s in sems],
        compiler_params=pltpu.CompilerParams(
            collective_id=0, has_side_effects=True, vmem_limit_bytes=VMEM_LIMIT
        ),
    )(*[v for _, v, _ in ins])

    out_back, grad_back, vectors = results[:3]
    if z.fast:
        flat = shape((z.block, width), F32)
        grid_rows = (z.rows, z.part, width)
        published = pl.pallas_call(
            functools.partial(publish_kernel, z),
            out_shape=[
                shape(grid_rows, F32), shape(grid_rows, F32), flat, flat, flat, flat,
                shape((z.block, z.hidden), F32), shape((z.hidden // z.seq, width), F32),
                shape((8, PAD), F32),
            ],
            in_specs=[anywhere] * 3 + [vmem],
            out_specs=[anywhere] * 8 + [vmem],
            scratch_shapes=[
                pltpu.VMEM((2,) + grid_rows, BF16), pltpu.VMEM((3, z.dp) + piece, BF16),
                pltpu.VMEM((2,) + grid_rows, F32), pltpu.VMEM((3, z.dp) + piece, F32),
                dma((2, z.rows)), dma((2, z.rows)), dma((3, z.dp)), dma((3, z.dp)),
            ],
            compiler_params=pltpu.CompilerParams(vmem_limit_bytes=VMEM_LIMIT),
        )(out_back, grad_back, results[3], vectors)
        out_full, grad_full, g_q, g_k, g_v, g_o, g_up, g_down, own = published
        own = own[:, : z.block]
        return (
            out_full, grad_full, own[0], own[1], g_q, g_k, g_v, g_o, own[2], own[3], g_up, g_down,
        )

    def share(v, dim):
        v = lax.psum_scatter(v.astype(F32), "seq", scatter_dimension=dim, tiled=True)
        return lax.psum(v, "dp")

    g_up = share(jnp.transpose(results[4], (1, 0, 2)).reshape(width, z.hidden), 0)
    g_qkvo, g_down, own = share(results[3], 1), share(results[5], 0), share(vectors, 1)
    return (
        out_back.astype(F32), grad_back.astype(F32), own[0], own[1],
        g_qkvo[0], g_qkvo[1], g_qkvo[2], g_qkvo[3], own[2], own[3], g_up, g_down,
    )


def solution(mesh):
    spread = P("dp", "seq", None)
    return jax.shard_map(
        functools.partial(local, dict(mesh.shape)),
        mesh=mesh,
        in_specs=(spread, spread, P("dp", None), spread) + (P(),) * 10,
        out_specs=(spread, spread, P("seq"), P("seq")) + (P("seq", None),) * 4
        + (P("seq"), P("seq"), P("seq", None), P("seq", None)),
        check_vma=False,
    )
```
